32 devices in a mesh: dp: 8 (over z, y), mp: 4 (over x, core).
Axes of the slice: x: 2, y: 2, z: 4, core: 2. Of those that a mesh axis runs over, the one named last changes fastest.
Arguments:
- token_ids: int32 [1024, 16], P('dp'), may hold values from 0 to 31999
- lengths: int32 [1024], P('dp'), may hold values from 1 to 16
- images: bfloat16 [1024, 768], P(('dp', 'mp')), may hold values from -6 to 6
- table: bfloat16 [32000, 768], P('mp'), may hold values from -6 to 6
- pos_table: bfloat16 [16, 768], replicated, may hold values from -4 to 4
- ln1_gain: bfloat16 [768], replicated, may hold values from 0.5 to 1.5
- ln1_bias: bfloat16 [768], replicated, may hold values from -2 to 2
- w_qkv: bfloat16 [3, 768, 768], P(None, None, 'mp'), may hold values from -0.21875 to 0.21875
- w_out: bfloat16 [768, 768], P('mp'), may hold values from -0.625 to 0.625
- b_out: bfloat16 [768], replicated, may hold values from -2 to 2
- ln2_gain: bfloat16 [768], replicated, may hold values from 0.5 to 1.5
- ln2_bias: bfloat16 [768], replicated, may hold values from -2 to 2
- w_up: bfloat16 [768, 3072], P(None, 'mp'), may hold values from -0.21875 to 0.21875
- b_up: bfloat16 [3072], P('mp'), may hold values from -2 to 2
- w_down: bfloat16 [3072, 768], P('mp'), may hold values from -0.109375 to 0.109375
- b_down: bfloat16 [768], replicated, may hold values from -2 to 2
- w_head: bfloat16 [768, 768], replicated, may hold values from -0.21875 to 0.21875
Outputs:
- loss: float32 [], replicated
- table_grad: float32 [32000, 768], P(('mp', 'dp'))
- pos_table_grad: float32 [16, 768], P(None, 'dp')
- ln1_gain_grad: float32 [768], P('dp')
- ln1_bias_grad: float32 [768], P('dp')
- w_qkv_grad: float32 [3, 768, 768], P(None, 'dp', 'mp')
- w_out_grad: float32 [768, 768], P('mp', 'dp')
- b_out_grad: float32 [768], P('dp')
- ln2_gain_grad: float32 [768], P('dp')
- ln2_bias_grad: float32 [768], P('dp')
- w_up_grad: float32 [768, 3072], P('dp', 'mp')
- b_up_grad: float32 [3072], P(('mp', 'dp'))
- w_down_grad: float32 [3072, 768], P('mp', 'dp')
- b_down_grad: float32 [768], P('dp')
- w_head_grad: float32 [768, 768], P('dp')
The draws below stay inside these ranges and needn't reach their ends.
Inputs may be any that keep to these rules, and one draw needn't show every extreme that they name: Caption lengths; positions at or after a caption's length are padding.
All inputs are finite; a program needn't handle non-finite values.
Results may differ from the reference program's by a relative error of at most 0.014.
Values may be sent and summed in bfloat16 or wider, within the bound.
No kernel may reach another device: no remote copies, remote signals or barrier semaphores. Data moves between devices by JAX's collectives and lax.ppermute only.
A program may use at most 192 MiB of HBM per device.

```python
import math
import jax
import jax.numpy as jnp
import numpy as np
from jax import lax

D = 768
HEAD_DIM = 64
FF = 3072
VOCAB = 32000
EMBED = 768
LEN = 16
CAPTIONS = 1024


def with_ends(result, stream_key, least, top_value):
    index_at = [jax.random.randint(jax.random.fold_in(stream_key, axis), (), 0, length) for axis, length in enumerate(result.shape)]
    widest = result.shape.index(max(result.shape))
    beside = index_at[:widest] + [(index_at[widest] + 1) % result.shape[widest]] + index_at[widest + 1:]
    return result.at[tuple(index_at)].set(least).at[tuple(beside)].set(top_value)


def shard_levels(key, shape, pieces, low, largest):
    def one(dim, blocks):
        steps = jax.random.uniform(jax.random.fold_in(jax.random.fold_in(key, 6), dim), (blocks,), jnp.float32, low / len(pieces), largest / len(pieces))
        return jnp.repeat(jnp.exp(steps), shape[dim] // blocks).reshape((-1,) + (1,) * (len(shape) - dim - 1))

    loudness = one(*pieces[0])
    for cut in pieces[1:]:
        loudness = loudness * one(*cut)
    return loudness


def rank_table(number_of, lean):
    loads = [(1 << 20) // math.isqrt(grade ** lean) + 1 for grade in range(1, number_of + 1)]
    scale = 1 + sum(loads) // (1 << 30)
    return np.cumsum(np.array([max(1, weight // scale) for weight in loads]))


def ranked_ids(own_key, extent, count, lean):
    grid = rank_table(count, lean)
    ticket = jax.random.randint(jax.random.fold_in(own_key, 1), extent, 0, int(grid[count - 1]))
    rank = jnp.searchsorted(jnp.asarray(grid, jnp.int32), ticket, side="right")
    return jax.random.permutation(jax.random.fold_in(own_key, 2), count)[rank].astype(jnp.int32)


def scatter_about(rng, dims, width, most, shards=(), held_as=jnp.bfloat16):
    drawn = jax.random.normal(rng, dims, jnp.float32) * width
    if len(shards) > 0:
        drawn = shard_levels(rng, dims, shards, -0.22, 0.18) * drawn
    return jnp.clip(drawn, min=-most, max=most).astype(held_as)


def setup_inputs(seed: int = 0) -> dict:
    seeds = jax.random.split(jax.random.key(seed), 18)
    return {
        "token_ids": with_ends(ranked_ids(seeds[0], (CAPTIONS, LEN), VOCAB, 2), jax.random.fold_in(seeds[0], 3), 0, VOCAB - 1).astype(jnp.int32),
        "lengths": with_ends(jax.random.randint(seeds[1], (CAPTIONS,), 1, LEN + 1), jax.random.fold_in(seeds[1], 1), 1, LEN).astype(jnp.int32),
        "images": scatter_about(seeds[2], (CAPTIONS, EMBED), 1.0, 6.0, ((0, 32),)),
        "table": scatter_about(seeds[3], (VOCAB, D), 1.0, 6.0, ((0, 4),)),
        "pos_table": scatter_about(seeds[4], (LEN, D), 0.5, 4.0),
        "ln1_gain": jnp.clip(1.0 + 0.1 * jax.random.normal(seeds[5], (D,), jnp.float32), 0.5, 1.5).astype(jnp.bfloat16),
        "ln1_bias": scatter_about(seeds[6], (D,), 0.3, 2.0),
        "w_qkv": scatter_about(seeds[7], (3, D, D), D ** -0.5, 0.21875, ((2, 4),)),
        "w_out": scatter_about(seeds[8], (D, D), (D // 8) ** -0.5, 0.625, ((0, 4),)),
        "b_out": scatter_about(seeds[9], (D,), 0.3, 2.0),
        "ln2_gain": jnp.clip(1.0 + 0.1 * jax.random.normal(seeds[10], (D,), jnp.float32), 0.5, 1.5).astype(jnp.bfloat16),
        "ln2_bias": scatter_about(seeds[11], (D,), 0.3, 2.0),
        "w_up": scatter_about(seeds[12], (D, FF), D ** -0.5, 0.21875, ((1, 4),)),
        "b_up": scatter_about(seeds[13], (FF,), 0.3, 2.0, ((0, 4),)),
        "w_down": scatter_about(seeds[14], (FF, D), FF ** -0.5, 0.109375, ((0, 4),)),
        "b_down": scatter_about(seeds[15], (D,), 0.3, 2.0),
        "w_head": scatter_about(seeds[16], (D, EMBED), D ** -0.5, 0.21875),
    }


logit_scale = 50.0
norm_eps = 1e-06
mask_fill = -1000000000.0
highest = lax.Precision.HIGHEST

@jax.custom_vjp
def low(v):
    return lax.optimization_barrier(v.astype(jnp.bfloat16)).astype(jnp.float32)

@jax.custom_vjp
def low_back(v):
    return v

def low_keep(v):
    return (low(v), None)

def low_pass(kept, grad):
    return (grad,)

def back_keep(v):
    return (v, None)

def back_low(kept, grad):
    return (low(grad),)
low.defvjp(low_keep, low_pass)
low_back.defvjp(back_keep, back_low)

def layer_norm(values_in, gain_vec, bias_vec):
    row_mean = lax.optimization_barrier(jnp.mean(values_in, -1, keepdims=True))
    centred = values_in - row_mean
    inverse = lax.rsqrt(lax.optimization_barrier(jnp.mean(centred * centred, -1, keepdims=True)) + norm_eps)
    return centred * inverse * gain_vec + bias_vec

def caption_block(params, group_ids, group_lengths):
    table, pos_table, ln1_gain, ln1_bias, w_qkv, w_out, b_out, ln2_gain, ln2_bias, w_up, b_up, w_down, b_down = params
    captions_here, seq_len = group_ids.shape
    model_width = table.shape[1]
    heads_all = model_width // HEAD_DIM
    embedded = low_back(jnp.take(table, group_ids, axis=0) + pos_table[None])
    normed_one = low(layer_norm(embedded, ln1_gain, ln1_bias))

    def project(matrix):
        out_rows = jnp.einsum('cld,de->cle', normed_one, matrix, precision=highest)
        return low_back(low(out_rows)).reshape(captions_here, seq_len, heads_all, HEAD_DIM)
    queries = project(w_qkv[0])
    key_rows = project(w_qkv[1])
    value_rows = project(w_qkv[2])
    scale_factor = 1.0 / math.sqrt(HEAD_DIM)
    raw_scores = low_back(jnp.einsum('cqhd,ckhd->chqk', queries, key_rows, precision=highest) * scale_factor)
    key_valid = jnp.arange(seq_len)[None, :] < group_lengths[:, None]
    scores = jnp.where(key_valid[:, None, None, :], raw_scores, mask_fill)
    score_top = lax.optimization_barrier(jnp.max(scores, -1, keepdims=True))
    expd = jnp.exp(scores - score_top)
    attn_probs = low(expd / lax.optimization_barrier(jnp.sum(expd, -1, keepdims=True)))
    context = low_back(low(jnp.einsum('chqk,ckhd->cqhd', attn_probs, value_rows, precision=highest)))
    context = context.reshape(captions_here, seq_len, model_width)
    branch = low_back(jnp.einsum('cle,ed->cld', context, w_out, precision=highest) + b_out)
    after_attn = embedded + branch
    normed_two = low(layer_norm(after_attn, ln2_gain, ln2_bias))
    hidden_pre = low_back(jnp.einsum('cld,df->clf', normed_two, w_up, precision=highest) + b_up)
    hidden = low(jax.nn.gelu(hidden_pre, approximate=True))
    mlp_out = low_back(jnp.einsum('clf,fd->cld', hidden, w_down, precision=highest) + b_down)
    block_out = after_attn + mlp_out
    end_pick = (jnp.arange(seq_len)[None, :] == (group_lengths - 1)[:, None]).astype(jnp.float32)
    return lax.optimization_barrier(jnp.sum(block_out * end_pick[:, :, None], axis=1))

def reference(token_ids, lengths, images, table, pos_table, ln1_gain, ln1_bias, w_qkv, w_out, b_out, ln2_gain, ln2_bias, w_up, b_up, w_down, b_down, w_head):
    params = tuple((weight_in.astype(jnp.float32) for weight_in in (table, pos_table, ln1_gain, ln1_bias, w_qkv, w_out, b_out, ln2_gain, ln2_bias, w_up, b_up, w_down, b_down, w_head)))
    caption_total = token_ids.shape[0]
    group_size = math.gcd(caption_total, 256)
    image_f = images.astype(jnp.float32)
    image_unit = low(image_f * lax.rsqrt(lax.optimization_barrier(jnp.sum(image_f * image_f, -1, keepdims=True)) + norm_eps))
    grouped_ids = token_ids.reshape(caption_total // group_size, group_size, -1)
    grouped_lengths = lengths.reshape(caption_total // group_size, group_size)

    def forward(weights):
        block_params = weights[:-1]
        head_matrix = weights[-1]

        def one_group(group_pair):
            return caption_block(block_params, group_pair[0], group_pair[1])
        pooled = lax.map(jax.checkpoint(one_group), (grouped_ids, grouped_lengths))
        pooled = low(pooled.reshape(caption_total, -1))
        projected = low_back(jnp.dot(pooled, head_matrix, precision=highest))
        inverse = lax.rsqrt(lax.optimization_barrier(jnp.sum(projected * projected, -1, keepdims=True)) + norm_eps)
        text_unit = low(projected * inverse)
        logits = low_back(logit_scale * jnp.dot(text_unit, image_unit.T, precision=highest))
        diagonal = jnp.diagonal(logits)
        row_loss = jax.nn.logsumexp(logits, axis=1) - diagonal
        col_loss = jax.nn.logsumexp(logits, axis=0) - diagonal
        return (jnp.sum(row_loss) + jnp.sum(col_loss)) / (2.0 * caption_total)
    loss_value, pull_back = jax.vjp(forward, params)
    gradients = pull_back(jnp.ones((), jnp.float32))[0]
    return (loss_value, gradients[0], gradients[1], gradients[2], gradients[3], gradients[4], gradients[5], gradients[6], gradients[7], gradients[8], gradients[9], gradients[10], gradients[11], gradients[12], gradients[13])
```

```python
import functools
import math

import jax
import jax.numpy as jnp
from jax import lax
from jax.experimental import pallas as pl
from jax.experimental.pallas import tpu as pltpu
from jax.sharding import PartitionSpec as P

HEAD_DIM = 64
LOGIT_SCALE = 50.0
EPS = 1e-06
MASK_FILL = -1000000000.0
NO_KEY = -1e30
BF = jnp.bfloat16
F32 = jnp.float32
I32 = jnp.int32
GELU_C = math.sqrt(2.0 / math.pi)
CAP_BLOCK = 16
HEAD_GROUP = 4
VMEM_LIMIT = 56 * 1024 * 1024


def nn(a, b):
    return lax.dot_general(a, b, (((1,), (0,)), ((), ())), preferred_element_type=F32)


def nt(a, b):
    return lax.dot_general(a, b, (((1,), (1,)), ((), ())), preferred_element_type=F32)


def tn(a, b):
    return lax.dot_general(a, b, (((0,), (0,)), ((), ())), preferred_element_type=F32)


def normalize(rows):
    centred = rows - jnp.mean(rows, -1, keepdims=True)
    inverse = lax.rsqrt(jnp.mean(centred * centred, -1, keepdims=True) + EPS)
    return centred * inverse, inverse


def norm_back(upstream, unit, inverse, gain):
    scaled = upstream * gain
    mean_scaled = jnp.mean(scaled, -1, keepdims=True)
    mean_unit = jnp.mean(scaled * unit, -1, keepdims=True)
    return inverse * (scaled - mean_scaled - unit * mean_unit)


def iota2(shape, dim):
    return lax.broadcasted_iota(I32, shape, dim)


def vmem_call(body, outs, args, scratch=()):
    spec = pl.BlockSpec(memory_space=pltpu.VMEM)
    return pl.pallas_call(
        body,
        out_shape=[jax.ShapeDtypeStruct(s, t) for s, t in outs],
        in_specs=[spec] * len(args),
        out_specs=[spec] * len(outs),
        scratch_shapes=list(scratch),
        compiler_params=pltpu.CompilerParams(vmem_limit_bytes=VMEM_LIMIT),
    )(*args)


def head_mask(captions):
    shape = (HEAD_GROUP * captions, HEAD_GROUP * HEAD_DIM)
    return (iota2(shape, 0) // captions) == (iota2(shape, 1) // HEAD_DIM)


def spread_heads(rows, group, mask):
    width = HEAD_GROUP * HEAD_DIM
    part = rows[:, group * width : (group + 1) * width].astype(F32)
    tall = jnp.concatenate([part] * HEAD_GROUP, axis=0)
    return jnp.where(mask, tall, 0.0).astype(BF)


def fold_heads(tall, captions, mask):
    kept = jnp.where(mask, tall, 0.0)
    total = kept[:captions]
    for h in range(1, HEAD_GROUP):
        total = total + kept[h * captions : (h + 1) * captions]
    return total


def block_masks(code, heads, seq_len):
    shape = (heads * CAP_BLOCK, CAP_BLOCK * seq_len)
    same = (iota2(shape, 0) % CAP_BLOCK) == (iota2(shape, 1) // seq_len)
    own = jnp.logical_and(same, code > 0)
    return own, jnp.logical_and(same, code > 1)


def masked_block_scores(qk, rows, own, valid):
    raw = nt(qk, rows)
    return jnp.where(own, jnp.where(valid, raw, MASK_FILL), NO_KEY)


def input_rows(emb_ref, pos, block, rows_per_block):
    rows = emb_ref[pl.ds(block * rows_per_block, rows_per_block), :].astype(F32)
    return rows + jnp.concatenate([pos] * CAP_BLOCK, axis=0)


def attend_body(
    parts_ref, pos_pick_ref, pos_ref, vec_ref, emb_ref, code_ref, wq_ref, wk_ref, wv_ref,
    pay_ref, qk_ref, x0p_ref, q_ref, t_ref,
):
    captions, width = x0p_ref.shape
    heads = width // HEAD_DIM
    groups = heads // HEAD_GROUP
    seq_len = pos_ref.shape[0]
    rows_per_block = CAP_BLOCK * seq_len
    gain, bias = vec_ref[0:1], vec_ref[1:2]
    pos = pos_ref[...].astype(F32)
    pooled_in = nn(pos_pick_ref[...], pos_ref[...])
    for i in range(parts_ref.shape[0]):
        pooled_in = pooled_in + parts_ref[i].astype(F32)
    x0p_ref[...] = pooled_in
    unit, _ = normalize(pooled_in)
    q = nt((unit * gain + bias).astype(BF), wq_ref[...]).astype(BF)
    q_ref[...] = q
    mask = head_mask(captions)
    span = HEAD_GROUP * HEAD_DIM
    scale = 1.0 / math.sqrt(HEAD_DIM)
    for g in range(groups):
        tall = nn(spread_heads(q, g, mask), wk_ref[g * span : (g + 1) * span]) * scale
        qk_ref[g * HEAD_GROUP : (g + 1) * HEAD_GROUP] = tall.astype(BF).reshape(
            HEAD_GROUP, captions, width
        )
    lane = iota2((heads, CAP_BLOCK, 128), 2)
    head_of = iota2((heads, CAP_BLOCK, 128), 0)
    for block in range(captions // CAP_BLOCK):
        caps = pl.ds(block * CAP_BLOCK, CAP_BLOCK)
        unit, _ = normalize(input_rows(emb_ref, pos, block, rows_per_block))
        rows = (unit * gain + bias).astype(BF)
        own, valid = block_masks(code_ref[block : block + 1], heads, seq_len)
        qk = qk_ref[:, caps, :].reshape(heads * CAP_BLOCK, width)
        scores = masked_block_scores(qk, rows, own, valid)
        top = jnp.max(scores, -1, keepdims=True)
        weights = jnp.where(own, jnp.exp(scores - top), 0.0)
        total = jnp.sum(weights, -1, keepdims=True)
        some = total > 0.0
        total = jnp.where(some, total, 1.0)
        log_total = jnp.where(some, top + jnp.log(total), NO_KEY)
        mixed = nn((weights / total).astype(BF), rows)
        t_ref[:, caps, :] = mixed.astype(BF).reshape(heads, CAP_BLOCK, width)
        first = log_total.astype(BF).astype(F32)
        second = (log_total - first).astype(BF).astype(F32)
        third = log_total - first - second
        stat = jnp.zeros((heads, CAP_BLOCK, 128), F32)
        for k, piece in enumerate((first, second, third)):
            stat = stat + jnp.where(
                lane == head_of + 16 * k, piece.reshape(heads, CAP_BLOCK, 1), 0.0
            )
        pay_ref[caps, width:] = jnp.sum(stat, 0).astype(BF)
    for g in range(groups):
        tall = t_ref[g * HEAD_GROUP : (g + 1) * HEAD_GROUP].reshape(HEAD_GROUP * captions, width)
        piece = nt(tall, wv_ref[g * span : (g + 1) * span])
        pay_ref[:, g * span : (g + 1) * span] = fold_heads(piece, captions, mask).astype(BF)


def hidden_body(
    pay_ref, x0p_ref, vec_ref, wo_ref, wup_ref, wdown_ref,
    ctx_ref, lse_ref, x1_ref, u_ref, part_ref,
):
    captions, width = x0p_ref.shape
    shape = (128, width)
    stat_row, head = iota2(shape, 0), iota2(shape, 1) // HEAD_DIM
    picks = jnp.logical_and(stat_row % 16 == head, stat_row < 48)
    expand = jnp.where(picks, 1.0, 0.0).astype(BF)
    n = pay_ref.shape[0]
    logs = [nn(pay_ref[i, :, width:], expand) for i in range(n)]
    top = functools.reduce(jnp.maximum, logs)
    total = jnp.zeros_like(top)
    ctx = jnp.zeros_like(top)
    for i in range(n):
        weight = jnp.exp(logs[i] - top)
        total = total + weight
        ctx = ctx + weight * pay_ref[i, :, :width].astype(F32)
    ctx = ctx / total
    ctx_ref[...] = ctx
    lse_ref[...] = top + jnp.log(total)
    x1 = x0p_ref[...] + nn(ctx.astype(BF), wo_ref[...]) + vec_ref[2:3]
    x1_ref[...] = x1
    unit, _ = normalize(x1)
    h2 = (unit * vec_ref[3:4] + vec_ref[4:5]).astype(BF)
    u = nn(h2, wup_ref[...]) + vec_ref[6:7]
    u_ref[...] = u
    hidden = (0.5 * u * (1.0 + jnp.tanh(GELU_C * (u + 0.044715 * u * u * u)))).astype(BF)
    part_ref[...] = nn(hidden, wdown_ref[...]).astype(BF)


def logits_body(
    parts_ref, x1_ref, vec_ref, wh_ref, img_ref, diag_ref,
    pooled_ref, proj_ref, e_ref, sums_ref,
):
    x2 = x1_ref[...] + vec_ref[5:6]
    for i in range(parts_ref.shape[0]):
        x2 = x2 + parts_ref[i].astype(F32)
    pooled = x2.astype(BF)
    pooled_ref[...] = pooled
    proj = nn(pooled, wh_ref[...])
    proj_ref[...] = proj
    text = (proj * lax.rsqrt(jnp.sum(proj * proj, -1, keepdims=True) + EPS)).astype(BF)
    logits = LOGIT_SCALE * nt(text, img_ref[...])
    powers = jnp.exp(logits)
    e_ref[...] = powers
    n_all = img_ref.shape[0]
    is_diag = iota2(logits.shape, 1) == diag_ref[...]
    rows = jnp.log(jnp.sum(powers, -1, keepdims=True))
    rows = rows - 2.0 * jnp.sum(jnp.where(is_diag, logits, 0.0), -1, keepdims=True)
    sums_ref[:, :n_all] = jnp.sum(powers, 0, keepdims=True)
    sums_ref[:, n_all:] = jnp.broadcast_to(jnp.sum(rows, 0, keepdims=True), (1, 128))


def loss_body(
    sums_ref, e_ref, proj_ref, pooled_ref, img_ref, diag_ref, x1_ref, u_ref, vec_ref,
    wh_ref, wup_ref, wdown_ref, pick_ref,
    loss_ref, dpooled_ref, part_ref, grads_ref, small_ref,
):
    n_all = img_ref.shape[0]
    sums = jnp.sum(sums_ref[...], 0, keepdims=True)
    cols = sums[:, :n_all]
    loss = jnp.sum(jnp.log(cols), -1, keepdims=True) + sums[:, n_all : n_all + 1]
    loss_ref[...] = jnp.broadcast_to(loss * (0.5 / n_all), (1, 128))
    powers = e_ref[...]
    row_inv = 1.0 / jnp.sum(powers, -1, keepdims=True)
    is_diag = iota2(powers.shape, 1) == diag_ref[...]
    grad = powers * row_inv + powers * (1.0 / cols) - jnp.where(is_diag, 2.0, 0.0)
    grad = (grad * (0.5 / n_all)).astype(BF)
    dtext = LOGIT_SCALE * nn(grad, img_ref[...])
    proj = proj_ref[...]
    inv = lax.rsqrt(jnp.sum(proj * proj, -1, keepdims=True) + EPS)
    along = jnp.sum(proj * dtext, -1, keepdims=True)
    dproj = (inv * dtext - inv * inv * inv * proj * along).astype(BF)
    dpooled = nt(dproj, wh_ref[...])
    dpooled_ref[...] = dpooled
    dy = dpooled.astype(BF)
    u = u_ref[...]
    th = jnp.tanh(GELU_C * (u + 0.044715 * u * u * u))
    slope = 0.5 * (1.0 + th) + 0.5 * u * (1.0 - th * th) * (
        GELU_C * (1.0 + 3.0 * 0.044715 * u * u)
    )
    du = (nt(dy, wdown_ref[...]) * slope).astype(BF)
    part_ref[...] = nt(du, wup_ref[...]).astype(BF)
    hidden = (0.5 * u * (1.0 + th)).astype(BF)
    unit, _ = normalize(x1_ref[...])
    h2 = (unit * vec_ref[3:4] + vec_ref[4:5]).astype(BF)
    ff = u.shape[1]
    grads_ref[:, :ff] = tn(dy, hidden).astype(BF)
    grads_ref[:, ff : 2 * ff] = tn(h2, du).astype(BF)
    own_cols = nn(dproj, pick_ref[...]).astype(BF)
    grads_ref[:, 2 * ff :] = tn(pooled_ref[...], own_cols).astype(BF)
    small_ref[0:1] = jnp.sum(dy.astype(F32), 0, keepdims=True)
    small_ref[1:2] = jnp.sum(du.astype(F32), 0, keepdims=True)


def attend_back_body(
    parts_ref, dpooled_ref, x1_ref, ctx_ref, lse_ref, q_ref, qk_ref, emb_ref, code_ref,
    pos_ref, vec_ref, wo_ref, wk_ref, wv_ref, pick_ref,
    dx1_ref, dq_ref, wout_ref, wkv_ref, dx_ref, posg_ref, small_ref,
    a_ref, t_ref, s_ref,
):
    captions, width = dpooled_ref.shape
    heads = width // HEAD_DIM
    groups = heads // HEAD_GROUP
    seq_len = pos_ref.shape[0]
    rows_per_block = CAP_BLOCK * seq_len
    span = HEAD_GROUP * HEAD_DIM
    dh2 = parts_ref[0].astype(F32)
    for i in range(1, parts_ref.shape[0]):
        dh2 = dh2 + parts_ref[i].astype(F32)
    unit2, inv2 = normalize(x1_ref[...])
    small_ref[0:1] = jnp.sum(dh2 * unit2, 0, keepdims=True)
    small_ref[1:2] = jnp.sum(dh2, 0, keepdims=True)
    dx1 = dpooled_ref[...] + norm_back(dh2, unit2, inv2, vec_ref[3:4])
    dx1_ref[...] = dx1
    da = dx1.astype(BF)
    small_ref[2:3] = jnp.sum(da.astype(F32), 0, keepdims=True)
    ctx = ctx_ref[...]
    wout_ref[...] = tn(da, nn(ctx.astype(BF), pick_ref[...]).astype(BF))
    dctx = nt(da, wo_ref[...]).astype(BF)
    mask = head_mask(captions)
    for g in range(groups):
        tall = nn(spread_heads(dctx, g, mask), wv_ref[g * span : (g + 1) * span])
        a_ref[g * HEAD_GROUP : (g + 1) * HEAD_GROUP] = tall.astype(BF).reshape(
            HEAD_GROUP, captions, width
        )
    prod = dctx.astype(F32) * ctx
    lse = lse_ref[...]
    pos = pos_ref[...].astype(F32)
    gain, bias = vec_ref[0:1], vec_ref[1:2]
    scale = 1.0 / math.sqrt(HEAD_DIM)
    tall_shape = (heads * CAP_BLOCK, width)
    of_head = (iota2(tall_shape, 0) // CAP_BLOCK) == (iota2(tall_shape, 1) // HEAD_DIM)
    at_head = (iota2(tall_shape, 0) // CAP_BLOCK) * HEAD_DIM == iota2(tall_shape, 1)
    gain_grad = jnp.zeros((1, width), F32)
    bias_grad = jnp.zeros((1, width), F32)
    pos_grad = jnp.zeros((seq_len, width), F32)
    for block in range(captions // CAP_BLOCK):
        low = block * CAP_BLOCK
        caps = pl.ds(low, CAP_BLOCK)
        unit, inverse = normalize(input_rows(emb_ref, pos, block, rows_per_block))
        rows = (unit * gain + bias).astype(BF)
        own, valid = block_masks(code_ref[block : block + 1], heads, seq_len)
        qk = qk_ref[:, caps, :].reshape(heads * CAP_BLOCK, width)
        scores = masked_block_scores(qk, rows, own, valid)
        tall = jnp.concatenate([lse[low : low + CAP_BLOCK]] * heads, axis=0)
        log_total = jnp.sum(jnp.where(at_head, tall, 0.0), -1, keepdims=True)
        tall = jnp.concatenate([prod[low : low + CAP_BLOCK]] * heads, axis=0)
        row_sum = jnp.sum(jnp.where(of_head, tall, 0.0), -1, keepdims=True)
        probs = jnp.where(own, jnp.exp(scores - log_total), 0.0)
        a = a_ref[:, caps, :].reshape(heads * CAP_BLOCK, width)
        dscores = (probs * (nt(a, rows) - row_sum)).astype(BF)
        probs = probs.astype(BF)
        t_ref[:, caps, :] = nn(probs, rows).astype(BF).reshape(heads, CAP_BLOCK, width)
        s_ref[:, caps, :] = (
            (nn(dscores, rows) * scale).astype(BF).reshape(heads, CAP_BLOCK, width)
        )
        drows = tn(probs, a) + tn(dscores, qk)
        gain_grad = gain_grad + jnp.sum(drows * unit, 0, keepdims=True)
        bias_grad = bias_grad + jnp.sum(drows, 0, keepdims=True)
        dx = norm_back(drows, unit, inverse, gain).astype(BF)
        dx_ref[pl.ds(block * rows_per_block, rows_per_block), :] = dx
        pos_grad = pos_grad + jnp.sum(dx.astype(F32).reshape(CAP_BLOCK, seq_len, width), 0)
    small_ref[3:4] = gain_grad
    small_ref[4:5] = bias_grad
    posg_ref[...] = pos_grad
    q = q_ref[...]
    for g in range(groups):
        cols = slice(g * span, (g + 1) * span)
        some = slice(g * HEAD_GROUP, (g + 1) * HEAD_GROUP)
        tall = s_ref[some].reshape(HEAD_GROUP * captions, width)
        piece = nt(tall, wk_ref[cols])
        dq_ref[:, cols] = fold_heads(piece, captions, mask).astype(BF)
        wkv_ref[0, cols] = tn(spread_heads(q, g, mask), tall).astype(BF)
        tall = t_ref[some].reshape(HEAD_GROUP * captions, width)
        wkv_ref[1, cols] = tn(spread_heads(dctx, g, mask), tall).astype(BF)


def slot_sums(key, dx_ref, slots):
    total = None
    step = min(512, dx_ref.shape[0])
    for low in range(0, dx_ref.shape[0], step):
        hit = iota2((slots, step), 0) == key[:, low : low + step]
        piece = nn(jnp.where(hit, 1.0, 0.0).astype(BF), dx_ref[low : low + step])
        total = piece if total is None else total + piece
    return total


def query_back_body(
    parts_ref, x0p_ref, dx1_ref, vec_ref, wq_ref, pick_ref, pos_pick_ref, ownp_ref,
    dx_ref, key_ref, keyp_ref,
    wq_grad_ref, dxp_ref, posg_ref, small_ref, send_ref,
):
    slots, width = send_ref.shape
    dq = parts_ref[0].astype(F32)
    for i in range(1, parts_ref.shape[0]):
        dq = dq + parts_ref[i].astype(F32)
    dq = dq.astype(BF)
    gain = vec_ref[0:1]
    unit, inverse = normalize(x0p_ref[...])
    h1 = (unit * gain + vec_ref[1:2]).astype(BF)
    wq_grad_ref[...] = tn(h1, nn(dq, pick_ref[...]).astype(BF))
    owned = ownp_ref[...]
    dh1 = nn(dq, wq_ref[...]) * owned
    small_ref[0:1] = jnp.sum(dh1 * unit, 0, keepdims=True)
    small_ref[1:2] = jnp.sum(dh1, 0, keepdims=True)
    dxp = (dx1_ref[...] * owned + norm_back(dh1, unit, inverse, gain)).astype(BF)
    dxp_ref[...] = dxp
    posg_ref[...] = tn(pos_pick_ref[...], dxp)
    send = slot_sums(key_ref[...], dx_ref, slots) + slot_sums(keyp_ref[...], dxp_ref, slots)
    send_ref[...] = send.astype(BF)


def send_body(dx_ref, dxp_ref, key_ref, keyp_ref, send_ref):
    slots = send_ref.shape[0]
    send = slot_sums(key_ref[...], dx_ref, slots) + slot_sums(keyp_ref[...], dxp_ref, slots)
    send_ref[...] = send.astype(BF)


def place_body(row_ref, got_ref, table_ref):
    shape = (table_ref.shape[0], got_ref.shape[0])
    hit = iota2(shape, 0) == row_ref[...]
    table_ref[...] = nn(jnp.where(hit, 1.0, 0.0).astype(BF), got_ref[...])


def on_device(
    token_ids, lengths, images, table, pos_table, ln1_gain, ln1_bias, w_qkv, w_out, b_out,
    ln2_gain, ln2_bias, w_up, b_up, w_down, b_down, w_head,
):
    n_mp, n_dp = lax.axis_size("mp"), lax.axis_size("dp")
    mp_rank, dp_rank = lax.axis_index("mp"), lax.axis_index("dp")
    captions, seq_len = token_ids.shape
    rows = captions * seq_len
    vocab_part, width = table.shape
    heads = width // HEAD_DIM
    own_width = width // n_mp
    ff = w_up.shape[1]
    owner_rows = vocab_part // n_dp
    slot_cap = -(-rows // (n_dp * n_mp * 16)) * 16
    slots = n_dp * slot_cap
    chunk = width // n_dp
    n_all = captions * n_dp

    gather = functools.partial(lax.all_gather, axis_name="mp", axis=0)
    wq_t, wk_t, wv_t = (gather(w_qkv[t].T, tiled=True) for t in range(3))
    wo = gather(w_out, tiled=True)
    image_f = images.astype(F32)
    image_unit = (
        image_f * lax.rsqrt(jnp.sum(image_f * image_f, -1, keepdims=True) + EPS)
    ).astype(BF)
    all_image = lax.all_gather(image_unit, ("dp", "mp"), axis=0, tiled=True)
    vecs = jnp.stack(
        [ln1_gain, ln1_bias, b_out, ln2_gain, ln2_bias, b_down]
    ).astype(F32)
    vecs = jnp.concatenate([vecs, jnp.stack([b_up, b_up]).astype(F32)], 0)

    ids = token_ids.reshape(rows)
    local = ids - mp_rank * vocab_part
    owned = jnp.logical_and(local >= 0, local < vocab_part)
    valid = jnp.arange(seq_len)[None, :] < lengths[:, None]
    code = jnp.where(owned.reshape(captions, seq_len), jnp.where(valid, 2, 1), 0)
    code = code.astype(I32).reshape(captions // CAP_BLOCK, CAP_BLOCK * seq_len)
    end_pick = jnp.arange(seq_len)[None, :] == (lengths - 1)[:, None]
    pos_pick = end_pick.astype(BF)
    own_pick = (
        jnp.arange(width)[:, None] == (mp_rank * own_width + jnp.arange(own_width))[None, :]
    ).astype(BF)

    order = jnp.arange(rows, dtype=I32)
    first_at = jnp.min(jnp.where(ids[:, None] == ids[None, :], order[None, :], rows), 1)
    is_first = first_at == order
    owner = ids // owner_rows
    slot = jnp.sum(
        (
            is_first[None, :]
            & (owner[None, :] == owner[:, None])
            & (order[None, :] < first_at[:, None])
        ).astype(I32),
        1,
    )
    most = jnp.max(slot) + 1
    dest = jnp.where(owned, local // owner_rows, -1)
    end_ids = jnp.sum(jnp.where(end_pick, token_ids, 0), 1)
    end_slot = jnp.sum(jnp.where(end_pick, slot.reshape(captions, seq_len), 0), 1)
    end_local = end_ids - mp_rank * vocab_part
    end_owned = jnp.logical_and(end_local >= 0, end_local < vocab_part)
    end_dest = jnp.where(end_owned, end_local // owner_rows, -1)

    def keys_of(turn):
        def key(dests, slot_of):
            place = slot_of - turn * slot_cap
            inside = (dests >= 0) & (place >= 0) & (place < slot_cap)
            return jnp.where(inside, dests * slot_cap + place, -1)

        return key(dest, slot), key(end_dest, end_slot)

    def rows_of(key):
        hit = (key[None, :] == jnp.arange(slots)[:, None]) & is_first[None, :]
        row = jnp.sum(jnp.where(hit, local % owner_rows + 1, 0), 1) - 1
        return row.reshape(n_dp, slot_cap)

    key, end_key = keys_of(0)
    notes = jnp.concatenate([rows_of(key), jnp.full((n_dp, slot_cap), most, I32)], 1)
    notes = lax.all_to_all(notes, "dp", 0, 0, tiled=True)
    turns = -(-jnp.max(notes[:, slot_cap:]) // slot_cap)
    got_rows = notes[:, :slot_cap].reshape(1, slots)

    one_hot = (local[:, None] == jnp.arange(vocab_part, dtype=I32)[None, :]).astype(BF)
    emb = jnp.dot(one_hot, table, preferred_element_type=F32).astype(BF)
    emb_end = jnp.sum(
        emb.reshape(captions, seq_len, width).astype(F32) * end_pick[:, :, None], 1
    ).astype(BF)
    emb_parts = gather(emb_end)

    pay, qk, x0p, q = vmem_call(
        attend_body,
        [
            ((captions, width + 128), BF),
            ((heads, captions, width), BF),
            ((captions, width), F32),
            ((captions, width), BF),
        ],
        [emb_parts, pos_pick, pos_table, vecs, emb, code, wq_t, wk_t, wv_t],
        [pltpu.VMEM((heads, captions, width), BF)],
    )
    ctx, lse, x1, u, part = vmem_call(
        hidden_body,
        [
            ((captions, width), F32),
            ((captions, width), F32),
            ((captions, width), F32),
            ((captions, ff), F32),
            ((captions, width), BF),
        ],
        [gather(pay), x0p, vecs, wo, w_up, w_down],
    )
    diag = (dp_rank * captions + jnp.arange(captions, dtype=I32))[:, None]
    pooled, proj, powers, sums = vmem_call(
        logits_body,
        [
            ((captions, width), BF),
            ((captions, width), F32),
            ((captions, n_all), F32),
            ((1, n_all + 128), F32),
        ],
        [gather(part), x1, vecs, w_head, all_image, diag],
    )
    all_sums = lax.all_to_all(
        jnp.broadcast_to(sums, (n_dp, n_all + 128)), "dp", 0, 0, tiled=True
    )
    loss, dpooled, part, grads_one, small_one = vmem_call(
        loss_body,
        [
            ((1, 128), F32),
            ((captions, width), F32),
            ((captions, width), BF),
            ((width, 2 * ff + own_width), BF),
            ((2, width), F32),
        ],
        [all_sums, powers, proj, pooled, all_image, diag, x1, u, vecs, w_head, w_up, w_down, own_pick],
    )
    grads_one = lax.all_to_all(
        grads_one.reshape(n_dp, chunk, 2 * ff + own_width), "dp", 0, 0, tiled=True
    )
    dx1, dq_part, wout_t, wkv_part, dx, pos_one, small_two = vmem_call(
        attend_back_body,
        [
            ((captions, width), F32),
            ((captions, width), BF),
            ((width, own_width), F32),
            ((2, width, width), BF),
            ((rows, width), BF),
            ((seq_len, width), F32),
            ((5, width), F32),
        ],
        [
            gather(part), dpooled, x1, ctx, lse, q, qk, emb, code, pos_table, vecs, wo, wk_t, wv_t,
            own_pick,
        ],
        [pltpu.VMEM((heads, captions, width), BF)] * 3,
    )
    dq_parts = gather(dq_part)
    wq_grad, dxp, pos_two, small_three, send = vmem_call(
        query_back_body,
        [
            ((width, own_width), F32),
            ((captions, width), BF),
            ((seq_len, width), F32),
            ((2, width), F32),
            ((slots, width), BF),
        ],
        [
            dq_parts, x0p, dx1, vecs, wq_t, own_pick, pos_pick,
            end_owned.astype(F32)[:, None], dx, key[None, :], end_key[None, :],
        ],
    )

    def deliver(sent, row):
        got = lax.all_to_all(sent, "dp", 0, 0, tiled=True)
        return vmem_call(place_body, [((owner_rows, width), F32)], [row, got])[0]

    table_grad = deliver(send, got_rows)

    def another(carry):
        turn, total = carry
        key, end_key = keys_of(turn)
        row = lax.all_to_all(rows_of(key), "dp", 0, 0, tiled=True).reshape(1, slots)
        sent = vmem_call(
            send_body, [((slots, width), BF)], [dx, dxp, key[None, :], end_key[None, :]]
        )[0]
        return turn + 1, total + deliver(sent, row)

    _, table_grad = lax.while_loop(
        lambda carry: carry[0] < turns, another, (jnp.int32(1), table_grad)
    )

    wkv = lax.all_to_all(
        wkv_part.reshape(2, n_mp, own_width, width), "mp", 1, 1, tiled=True
    )
    wkv = jnp.sum(wkv.astype(F32), 1)
    first_owner = (mp_rank == 0).astype(F32)
    shared = jnp.stack(
        [small_one[0], small_two[0], small_two[1], small_two[2]], 1
    ) * first_owner
    shared = jnp.concatenate(
        [
            shared,
            (small_two[3] + small_three[0])[:, None],
            (small_two[4] + small_three[1])[:, None],
            (pos_one + pos_two).T,
        ],
        1,
    )
    shared = lax.psum(shared, "mp")
    small = jnp.concatenate([shared, small_one[1][:, None]], 1)
    small_high = small.astype(BF)
    small_low = (small - small_high.astype(F32)).astype(BF)
    grads_two = jnp.concatenate(
        [wq_grad, wkv[0].T, wkv[1].T, wout_t], 1
    ).astype(BF)
    grads_two = jnp.concatenate([grads_two, small_high, small_low], 1)
    total_width = grads_two.shape[1]
    grads_two = lax.all_to_all(
        grads_two.reshape(n_dp, chunk, total_width), "dp", 0, 0, tiled=True
    )
    one = jnp.sum(grads_one.astype(F32), 0)
    two = jnp.sum(grads_two.astype(F32), 0)
    base = 4 * own_width
    n_small = 7 + seq_len
    small = two[:, base : base + n_small] + two[:, base + n_small :]
    w_head_grad = lax.all_gather(one[:, 2 * ff :], "mp", axis=1, tiled=True)
    qkv_grad = jnp.stack([two[:, t * own_width : (t + 1) * own_width] for t in range(3)])
    return (
        loss[0, 0],
        table_grad,
        small[:, 6 : 6 + seq_len].T,
        small[:, 4],
        small[:, 5],
        qkv_grad,
        two[:, 3 * own_width : base].T,
        small[:, 3],
        small[:, 1],
        small[:, 2],
        one[:, ff : 2 * ff],
        small[:, 6 + seq_len],
        one[:, :ff].T,
        small[:, 0],
        w_head_grad,
    )


def solution(mesh):
    placed = (
        P("dp", None),
        P("dp"),
        P(("dp", "mp"), None),
        P("mp", None),
        P(),
        P(),
        P(),
        P(None, None, "mp"),
        P("mp", None),
        P(),
        P(),
        P(),
        P(None, "mp"),
        P("mp"),
        P("mp", None),
        P(),
        P(),
    )
    return jax.shard_map(
        on_device,
        mesh=mesh,
        in_specs=placed,
        out_specs=(
            P(),
            P(("mp", "dp"), None),
            P(None, "dp"),
            P("dp"),
            P("dp"),
            P(None, "dp", "mp"),
            P("mp", "dp"),
            P("dp"),
            P("dp"),
            P("dp"),
            P("dp", "mp"),
            P(("mp", "dp")),
            P("mp", "dp"),
            P("dp"),
            P("dp", None),
        ),
        check_vma=False,
    )
```

```python
import functools
import math

import jax
import jax.numpy as jnp
from jax import lax
from jax.experimental import pallas as pl
from jax.experimental.pallas import tpu as pltpu
from jax.sharding import PartitionSpec as P

HEAD_DIM = 64
LOGIT_SCALE = 50.0
EPS = 1e-06
MASK_FILL = -1000000000.0
NO_KEY = -1e30
BF = jnp.bfloat16
F32 = jnp.float32
I32 = jnp.int32
GELU_C = math.sqrt(2.0 / math.pi)
CAP_BLOCK = 16
SMALLS = 32
NOTES = 16
VALID_BIT = 1 << 20
END_BIT = 1 << 21
NOTE_BASE = 32
VMEM_LIMIT = 40 * 1024 * 1024


def nn(a, b):
    return lax.dot_general(a, b, (((1,), (0,)), ((), ())), preferred_element_type=F32)


def nt(a, b):
    return lax.dot_general(a, b, (((1,), (1,)), ((), ())), preferred_element_type=F32)


def tn(a, b):
    return lax.dot_general(a, b, (((0,), (0,)), ((), ())), preferred_element_type=F32)


def normalize(rows):
    centred = rows - jnp.mean(rows, -1, keepdims=True)
    inverse = lax.rsqrt(jnp.mean(centred * centred, -1, keepdims=True) + EPS)
    return centred * inverse, inverse


def norm_back(upstream, unit, inverse, gain):
    scaled = upstream * gain
    mean_scaled = jnp.mean(scaled, -1, keepdims=True)
    mean_unit = jnp.mean(scaled * unit, -1, keepdims=True)
    return inverse * (scaled - mean_scaled - unit * mean_unit)


def iota2(shape, dim):
    return lax.broadcasted_iota(I32, shape, dim)


class Late:
    def __init__(self, ref, pairs, sems):
        self.ref = ref
        self.copies = [
            pltpu.make_async_copy(src, dst, sem) for (src, dst), sem in zip(pairs, sems)
        ]
        self.waiting = set(range(len(self.copies)))

    def start(self):
        for copy in self.copies:
            copy.start()

    def wait(self, part=None):
        for k in sorted(self.waiting) if part is None else [part]:
            if k in self.waiting:
                self.copies[k].wait()
                self.waiting.discard(k)
        return self.ref

    def value(self):
        return self.wait()[...]


def fetch(array, parts=1, axis=0):
    return ("blocks", [array], parts, axis)


def fetch_weight(shards, which):
    return ("weight", list(shards), which, 0)


def vmem_call(body, outs, meta, args, late=(), scratch=()):
    vmem = pl.BlockSpec(memory_space=pltpu.VMEM)
    hbm = pl.BlockSpec(memory_space=pltpu.HBM)
    sources, buffers, counts = [], [], []
    for kind, arrays, parts, axis in late:
        sources += arrays
        if kind == "weight":
            _, rows, width = arrays[0].shape
            buffers.append(pltpu.VMEM((rows * len(arrays), width), arrays[0].dtype))
            counts.append(len(arrays))
        else:
            buffers.append(pltpu.VMEM(arrays[0].shape, arrays[0].dtype))
            counts.append(parts)

    staged = [k for k, o in enumerate(outs) if len(o) > 2 and o[2]]

    def kernel(meta_ref, *refs):
        arg_refs, refs = refs[: len(args)], refs[len(args) :]
        source_refs, refs = refs[: len(sources)], refs[len(sources) :]
        out_refs, refs = refs[: len(outs)], refs[len(outs) :]
        buffer_refs, refs = refs[: len(buffers)], refs[len(buffers) :]
        sems, stage_sems, refs = refs[0], refs[1], refs[2:]
        stages, refs = refs[: len(staged)], refs[len(staged) :]
        targets = list(out_refs)
        for k, stage in zip(staged, stages):
            targets[k] = stage
        handles, at, place = [], 0, 0
        for (kind, arrays, parts, axis), buffer in zip(late, buffer_refs):
            if kind == "weight":
                rows = arrays[0].shape[1]
                pairs = []
                for k in range(len(arrays)):
                    low = pl.multiple_of((meta_ref[0] ^ k) * rows, rows)
                    pairs.append((source_refs[place + k].at[parts], buffer.at[pl.ds(low, rows)]))
                place += len(arrays)
            else:
                size = arrays[0].shape[axis] // parts
                pairs = []
                for k in range(parts):
                    cut = (slice(None),) * axis + (pl.ds(k * size, size),)
                    pairs.append((source_refs[place].at[cut], buffer.at[cut]))
                place += 1
            handles.append(Late(buffer, pairs, [sems.at[at + k] for k in range(len(pairs))]))
            at += len(pairs)
        for handle in handles:
            handle.start()
        body(meta_ref, *arg_refs, *handles, *targets, *refs)
        copies = [
            pltpu.make_async_copy(stage, out_refs[k], stage_sems.at[i])
            for i, (k, stage) in enumerate(zip(staged, stages))
        ]
        for copy in copies:
            copy.start()
        for handle in handles:
            handle.wait()
        for copy in copies:
            copy.wait()

    return pl.pallas_call(
        kernel,
        out_shape=[
            pltpu.HBM(*o[:2]) if len(o) > 2 else jax.ShapeDtypeStruct(*o) for o in outs
        ],
        in_specs=[pl.BlockSpec(memory_space=pltpu.SMEM)]
        + [vmem] * len(args)
        + [hbm] * len(sources),
        out_specs=[hbm if len(o) > 2 else vmem for o in outs],
        scratch_shapes=[
            *buffers,
            pltpu.SemaphoreType.DMA((max(1, sum(counts)),)),
            pltpu.SemaphoreType.DMA((max(1, len(staged)),)),
            *(pltpu.VMEM(*outs[k][:2]) for k in staged),
            *scratch,
        ],
        compiler_params=pltpu.CompilerParams(vmem_limit_bytes=VMEM_LIMIT),
        cost_estimate=pl.CostEstimate(flops=1, bytes_accessed=1, transcendentals=0),
    )(meta, *args, *(pltpu.with_memory_space_constraint(x, pltpu.HBM) for x in sources))


def halve(total, axis, bit):
    count = lax.axis_size(axis)
    pairs = [(i, i ^ bit) for i in range(count)]
    halves = total.reshape((total.shape[0] // 2, 2) + total.shape[1:])
    mine = (lax.axis_index(axis) // bit) % 2
    sent = lax.dynamic_index_in_dim(halves, 1 - mine, 1, keepdims=False)
    kept = lax.dynamic_index_in_dim(halves, mine, 1, keepdims=False)
    total = kept.astype(F32) + lax.ppermute(sent, axis, pairs).astype(F32)
    return total.astype(BF) if 2 * bit < count else total


def bits_of(axis):
    count = lax.axis_size(axis)
    return [1 << k for k in range(count.bit_length() - 1)]


def after(x, *others):
    return lax.optimization_barrier((x, others))[0]


def everyone(x, axis, before):
    count = lax.axis_size(axis)
    have = {0: x}
    bit = count // 2
    while bit:
        pairs = [(i, i ^ bit) for i in range(count)]
        for k, v in list(have.items()):
            have[k | bit] = lax.ppermute(after(v, before) if k else v, axis, pairs)
        bit //= 2
    return [have[k] for k in range(count)]


def everyone_direct(x, axis):
    count = lax.axis_size(axis)
    return [x] + [
        lax.ppermute(x, axis, [(i, i ^ k) for i in range(count)]) for k in range(1, count)
    ]


def own_columns(start, width, own_width):
    shape = (width, own_width)
    hit = iota2(shape, 0) == start + iota2(shape, 1)
    return jnp.where(hit, 1.0, 0.0).astype(BF)


def unpack(packed):
    return packed % VALID_BIT, packed // VALID_BIT % 2 > 0, packed // END_BIT > 0


def own_code(packed, rank, vocab_part):
    ids, valid, _ = unpack(packed)
    return jnp.where(ids // vocab_part == rank, jnp.where(valid, 2, 1), 0)


def head_mask(captions, span):
    shape = (span // HEAD_DIM * captions, span)
    return (iota2(shape, 0) // captions) == (iota2(shape, 1) // HEAD_DIM)


def spread_heads(rows, group, mask):
    span = mask.shape[1]
    part = rows[:, group * span : (group + 1) * span].astype(F32)
    tall = jnp.concatenate([part] * (span // HEAD_DIM), axis=0)
    return jnp.where(mask, tall, 0.0).astype(BF)


def fold_heads(tall, captions, mask):
    kept = jnp.where(mask, tall, 0.0)
    total = kept[:captions]
    for h in range(1, tall.shape[0] // captions):
        total = total + kept[h * captions : (h + 1) * captions]
    return total


def block_masks(code, heads, seq_len):
    shape = (heads * CAP_BLOCK, CAP_BLOCK * seq_len)
    same = (iota2(shape, 0) % CAP_BLOCK) == (iota2(shape, 1) // seq_len)
    own = jnp.logical_and(same, code > 0)
    return own, jnp.logical_and(same, code > 1)


def masked_block_scores(qk, rows, own, valid):
    raw = nt(qk, rows)
    return jnp.where(own, jnp.where(valid, raw, MASK_FILL), NO_KEY)


def attend_body(n_mp, vocab_part, *refs):
    end_refs, refs = refs[1 : 1 + n_mp], refs[:1] + refs[1 + n_mp :]
    (
        meta_ref, pos_pick_ref, pos_ref, vec_ref, packed_ref,
        wq, wk, emb, wv,
        pay_ref, qk_out, x0p_ref, q_ref, rows_out, unit_out, inv_out,
        qk_ref, rows_ref, unit_ref, inv_ref, t_ref, sems,
    ) = refs
    captions, width = x0p_ref.shape
    heads = width // HEAD_DIM
    span = width // n_mp
    per_group = span // HEAD_DIM
    seq_len = pos_ref.shape[0]
    block_rows = CAP_BLOCK * seq_len
    gain, bias = vec_ref[0:1], vec_ref[1:2]
    pos = pos_ref[...].astype(F32)
    pooled_in = nn(pos_pick_ref[...], pos_ref[...])
    for end_ref in end_refs:
        pooled_in = pooled_in + end_ref[...].astype(F32)
    pending = []

    def write_back(src, dst):
        copy = pltpu.make_async_copy(src, dst, sems.at[len(pending)])
        copy.start()
        pending.append(copy)

    x0p_ref[...] = pooled_in
    unit, _ = normalize(pooled_in)
    q = nt((unit * gain + bias).astype(BF), wq.value()).astype(BF)
    q_ref[...] = q
    mask = head_mask(captions, span)
    scale = 1.0 / math.sqrt(HEAD_DIM)
    wk_ref = wk.wait()
    for g in range(n_mp):
        some = slice(g * per_group, (g + 1) * per_group)
        tall = nn(spread_heads(q, g, mask), wk_ref[g * span : (g + 1) * span]) * scale
        qk_ref[some] = tall.astype(BF).reshape(per_group, captions, width)
        write_back(qk_ref.at[some], qk_out.at[some])
    lane = iota2((heads, CAP_BLOCK, 128), 2)
    head_of = iota2((heads, CAP_BLOCK, 128), 0)
    for block in range(captions // CAP_BLOCK):
        caps = pl.ds(block * CAP_BLOCK, CAP_BLOCK)
        here = pl.ds(block * block_rows, block_rows)
        x0 = emb.wait(block)[here, :].astype(F32) + jnp.concatenate([pos] * CAP_BLOCK, axis=0)
        unit, inverse = normalize(x0)
        unit_ref[here, :] = unit.astype(BF)
        write_back(unit_ref.at[here], unit_out.at[here])
        inv_ref[here, :] = jnp.broadcast_to(inverse, (block_rows, 128))
        write_back(inv_ref.at[here], inv_out.at[here])
        rows = (unit * gain + bias).astype(BF)
        rows_ref[here, :] = rows
        write_back(rows_ref.at[here], rows_out.at[here])
        code = own_code(packed_ref[:, block * block_rows : (block + 1) * block_rows], meta_ref[0], vocab_part)
        own, valid = block_masks(code, heads, seq_len)
        qk = qk_ref[:, caps, :].reshape(heads * CAP_BLOCK, width)
        scores = masked_block_scores(qk, rows, own, valid)
        top = jnp.max(scores, -1, keepdims=True)
        weights = jnp.where(own, jnp.exp(scores - top), 0.0)
        total = jnp.sum(weights, -1, keepdims=True)
        some = total > 0.0
        total = jnp.where(some, total, 1.0)
        log_total = jnp.where(some, top + jnp.log(total), NO_KEY)
        mixed = nn((weights / total).astype(BF), rows)
        t_ref[:, caps, :] = mixed.astype(BF).reshape(heads, CAP_BLOCK, width)
        first = log_total.astype(BF).astype(F32)
        second = (log_total - first).astype(BF).astype(F32)
        third = log_total - first - second
        stat = jnp.zeros((heads, CAP_BLOCK, 128), F32)
        for k, piece in enumerate((first, second, third)):
            stat = stat + jnp.where(
                lane == head_of + 16 * k, piece.reshape(heads, CAP_BLOCK, 1), 0.0
            )
        pay_ref[caps, width:] = jnp.sum(stat, 0).astype(BF)
    wv_ref = wv.wait()
    for g in range(n_mp):
        tall = t_ref[g * per_group : (g + 1) * per_group].reshape(per_group * captions, width)
        piece = nt(tall, wv_ref[g * span : (g + 1) * span])
        pay_ref[:, g * span : (g + 1) * span] = fold_heads(piece, captions, mask).astype(BF)
    for copy in pending:
        copy.wait()


def hidden_body(
    meta_ref, pay_ref, vec_ref, x0p, wo, wup, wdown,
    ctx_ref, lse_ref, x1_ref, u_ref, part_ref,
):
    n_mp = pay_ref.shape[0]
    captions, width = ctx_ref.shape
    shape = (128, width)
    stat_row, head = iota2(shape, 0), iota2(shape, 1) // HEAD_DIM
    picks = jnp.logical_and(stat_row % 16 == head, stat_row < 48)
    expand = jnp.where(picks, 1.0, 0.0).astype(BF)
    logs = [nn(pay_ref[i, :, width:], expand) for i in range(n_mp)]
    top = functools.reduce(jnp.maximum, logs)
    total = jnp.zeros_like(top)
    ctx = jnp.zeros_like(top)
    for i in range(n_mp):
        weight = jnp.exp(logs[i] - top)
        total = total + weight
        ctx = ctx + weight * pay_ref[i, :, :width].astype(F32)
    ctx = ctx / total
    ctx_ref[...] = ctx
    lse_ref[...] = top + jnp.log(total)
    x1 = x0p.value() + nn(ctx.astype(BF), wo.value()) + vec_ref[2:3]
    x1_ref[...] = x1
    unit, _ = normalize(x1)
    h2 = (unit * vec_ref[3:4] + vec_ref[4:5]).astype(BF)
    u = nn(h2, wup.value()) + vec_ref[6:7]
    u_ref[...] = u
    hidden = (0.5 * u * (1.0 + jnp.tanh(GELU_C * (u + 0.044715 * u * u * u)))).astype(BF)
    part_ref[...] = nn(hidden, wdown.value()).astype(BF)


def logits_body(
    meta_ref, parts_ref, vec_ref, x1, wh, images,
    pooled_ref, proj_ref, e_ref, sums_ref,
):
    x2 = x1.value() + vec_ref[5:6]
    for i in range(parts_ref.shape[0]):
        x2 = x2 + parts_ref[i].astype(F32)
    pooled = x2.astype(BF)
    pooled_ref[...] = pooled
    proj = nn(pooled, wh.value())
    proj_ref[...] = proj
    text = (proj * lax.rsqrt(jnp.sum(proj * proj, -1, keepdims=True) + EPS)).astype(BF)
    logits = LOGIT_SCALE * nt(text, images.value())
    powers = jnp.exp(logits)
    e_ref[...] = powers
    n_all = powers.shape[1]
    is_diag = iota2(logits.shape, 1) == meta_ref[1] + iota2(logits.shape, 0)
    rows = jnp.log(jnp.sum(powers, -1, keepdims=True))
    rows = rows - 2.0 * jnp.sum(jnp.where(is_diag, logits, 0.0), -1, keepdims=True)
    cols = jnp.sum(powers, 0, keepdims=True)
    rows = jnp.broadcast_to(jnp.sum(rows, 0, keepdims=True), (1, 128))
    for i in range(sums_ref.shape[0]):
        sums_ref[i, :, :n_all] = cols
        sums_ref[i, :, n_all:] = rows


def loss_body(
    meta_ref, sums_ref, vec_ref, e, images, proj, wh, u, wdown, wup, x1, pooled,
    loss_ref, dpooled_ref, part_ref, down_ref, up_ref, small_ref,
):
    width = dpooled_ref.shape[1]
    sums = jnp.sum(sums_ref[...], 0)
    n_all = sums.shape[1] - 128
    cols = sums[:, :n_all]
    loss = jnp.sum(jnp.log(cols), -1, keepdims=True) + sums[:, n_all : n_all + 1]
    loss_ref[...] = jnp.broadcast_to(loss * (0.5 / n_all), (1, 128))
    powers = e.value()
    row_inv = 1.0 / jnp.sum(powers, -1, keepdims=True)
    is_diag = iota2(powers.shape, 1) == meta_ref[1] + iota2(powers.shape, 0)
    grad = powers * row_inv + powers * (1.0 / cols) - jnp.where(is_diag, 2.0, 0.0)
    grad = (grad * (0.5 / n_all)).astype(BF)
    dtext = LOGIT_SCALE * nn(grad, images.value())
    proj = proj.value()
    inv = lax.rsqrt(jnp.sum(proj * proj, -1, keepdims=True) + EPS)
    along = jnp.sum(proj * dtext, -1, keepdims=True)
    dproj = (inv * dtext - inv * inv * inv * proj * along).astype(BF)
    dpooled = nt(dproj, wh.value())
    dpooled_ref[...] = dpooled
    dy = dpooled.astype(BF)
    u = u.value()
    th = jnp.tanh(GELU_C * (u + 0.044715 * u * u * u))
    slope = 0.5 * (1.0 + th) + 0.5 * u * (1.0 - th * th) * (
        GELU_C * (1.0 + 3.0 * 0.044715 * u * u)
    )
    du = (nt(dy, wdown.value()) * slope).astype(BF)
    part_ref[...] = nt(du, wup.value()).astype(BF)
    hidden = (0.5 * u * (1.0 + th)).astype(BF)
    unit, _ = normalize(x1.value())
    h2 = (unit * vec_ref[3:4] + vec_ref[4:5]).astype(BF)
    ff = u.shape[1]
    own_width = down_ref.shape[1] - ff
    pick = own_columns(meta_ref[0] * own_width, width, own_width)
    down_ref[:, :ff] = tn(dy, hidden).astype(BF)
    up_ref[...] = tn(h2, du).astype(BF)
    down_ref[:, ff:] = tn(pooled.value(), nn(dproj, pick).astype(BF)).astype(BF)
    small_ref[0:1] = jnp.sum(dy.astype(F32), 0, keepdims=True)
    small_ref[1:2] = jnp.sum(du.astype(F32), 0, keepdims=True)


def attend_back_body(
    vocab_part, meta_ref, parts_ref, packed_ref, vec_ref, dpooled_ref, x1, ctx, wo, wv, lse, qk_all, rows_all, wk, q,
    dx1_ref, dq_ref, wout_ref, wkv_ref, a_ref, probs_ref, ds_ref, small_ref,
    t_ref, s_ref,
):
    n_mp = parts_ref.shape[0]
    captions, width = dpooled_ref.shape
    heads = width // HEAD_DIM
    span = width // n_mp
    per_group = span // HEAD_DIM
    block_rows = rows_all.ref.shape[0] // (captions // CAP_BLOCK)
    seq_len = block_rows // CAP_BLOCK
    rank = meta_ref[0]
    dh2 = parts_ref[0].astype(F32)
    for i in range(1, n_mp):
        dh2 = dh2 + parts_ref[i].astype(F32)
    unit2, inv2 = normalize(x1.value())
    small_ref[0:1] = jnp.sum(dh2 * unit2, 0, keepdims=True)
    small_ref[1:2] = jnp.sum(dh2, 0, keepdims=True)
    dx1 = dpooled_ref[...] + norm_back(dh2, unit2, inv2, vec_ref[3:4])
    dx1_ref[...] = dx1
    da = dx1.astype(BF)
    small_ref[2:3] = jnp.sum(da.astype(F32), 0, keepdims=True)
    ctx = ctx.value()
    pick = own_columns(rank * span, width, span)
    wout_ref[...] = tn(da, nn(ctx.astype(BF), pick).astype(BF)).astype(BF)
    dctx = nt(da, wo.value()).astype(BF)
    mask = head_mask(captions, span)
    wv_ref = wv.wait()
    for g in range(n_mp):
        tall = nn(spread_heads(dctx, g, mask), wv_ref[g * span : (g + 1) * span])
        a_ref[g * per_group : (g + 1) * per_group] = tall.astype(BF).reshape(
            per_group, captions, width
        )
    prod = dctx.astype(F32) * ctx
    lse = lse.value()
    scale = 1.0 / math.sqrt(HEAD_DIM)
    tall_shape = (heads * CAP_BLOCK, width)
    of_head = (iota2(tall_shape, 0) // CAP_BLOCK) == (iota2(tall_shape, 1) // HEAD_DIM)
    at_head = (iota2(tall_shape, 0) // CAP_BLOCK) * HEAD_DIM == iota2(tall_shape, 1)
    for block in range(captions // CAP_BLOCK):
        low = block * CAP_BLOCK
        caps = pl.ds(low, CAP_BLOCK)
        rows = rows_all.wait(block)[pl.ds(block * block_rows, block_rows), :]
        code = own_code(packed_ref[:, block * block_rows : (block + 1) * block_rows], meta_ref[0], vocab_part)
        own, valid = block_masks(code, heads, seq_len)
        qk = qk_all.wait(block)[:, caps, :].reshape(heads * CAP_BLOCK, width)
        scores = masked_block_scores(qk, rows, own, valid)
        tall = jnp.concatenate([lse[low : low + CAP_BLOCK]] * heads, axis=0)
        log_total = jnp.sum(jnp.where(at_head, tall, 0.0), -1, keepdims=True)
        tall = jnp.concatenate([prod[low : low + CAP_BLOCK]] * heads, axis=0)
        row_sum = jnp.sum(jnp.where(of_head, tall, 0.0), -1, keepdims=True)
        probs = jnp.where(own, jnp.exp(scores - log_total), 0.0)
        a = a_ref[:, caps, :].reshape(heads * CAP_BLOCK, width)
        dscores = (probs * (nt(a, rows) - row_sum)).astype(BF)
        probs = probs.astype(BF)
        probs_ref[block] = probs
        ds_ref[block] = dscores
        t_ref[:, caps, :] = nn(probs, rows).astype(BF).reshape(heads, CAP_BLOCK, width)
        s_ref[:, caps, :] = (
            (nn(dscores, rows) * scale).astype(BF).reshape(heads, CAP_BLOCK, width)
        )
    q = q.value()
    wk_ref = wk.wait()
    for g in range(n_mp):
        some = slice(g * per_group, (g + 1) * per_group)
        tall = s_ref[some].reshape(per_group * captions, width)
        piece = nt(tall, wk_ref[g * span : (g + 1) * span])
        dq_ref[:, g * span : (g + 1) * span] = fold_heads(piece, captions, mask).astype(BF)
        wkv_ref[g, :, :span] = tn(tall, spread_heads(q, g, mask)).astype(BF)
        tall = t_ref[some].reshape(per_group * captions, width)
        wkv_ref[g, :, span:] = tn(tall, spread_heads(dctx, g, mask)).astype(BF)


def slot_body(owner_rows, n_dp, meta_ref, packed_ref, out_ref):
    rows = packed_ref.shape[1]
    side = 128
    ids, _, _ = unpack(packed_ref[...])
    owner = ids // owner_rows
    order = iota2((1, rows), 1)

    def columns(row, k):
        piece = row[:, k * side : (k + 1) * side].astype(F32)
        return jnp.transpose(jnp.broadcast_to(piece, (side, side))).astype(I32)

    def tall(column):
        return jnp.concatenate([column] * (rows // side), axis=1)

    first_at = jnp.full((1, rows), rows, I32)
    for k in range(rows // side):
        there = k * side + iota2((side, rows), 0)
        hit = jnp.where(tall(columns(ids, k)) == ids, there, rows)
        first_at = jnp.minimum(first_at, jnp.min(hit, 0, keepdims=True))
    is_first = first_at == order
    first_owner = jnp.where(is_first, owner, -1)
    slot = jnp.zeros((1, rows), I32)
    for k in range(rows // side):
        there = k * side + iota2((side, rows), 0)
        ahead = jnp.logical_and(tall(columns(first_owner, k)) == owner, there < first_at)
        slot = slot + jnp.sum(jnp.where(ahead, 1, 0), 0, keepdims=True)
    here = owner - meta_ref[0] * n_dp
    dest = jnp.where(jnp.logical_and(here >= 0, here < n_dp), here, -1)
    most = jnp.max(slot.astype(F32), 1, keepdims=True).astype(I32) + 1
    out_ref[0:1] = slot
    out_ref[1:2] = dest
    out_ref[2:3] = jnp.where(is_first, ids % owner_rows + 1, 0)
    out_ref[3:4] = jnp.broadcast_to(most, (1, rows))
    out_ref[4:8] = jnp.zeros((4, rows), I32)


def slot_sums(turn, slot_cap, seq_len, slots_ref, packed_ref, dx_ref, n_dp):
    slots = n_dp * slot_cap
    rows = dx_ref.shape[0]
    step = min(512, rows)
    captions_per_step = step // seq_len
    total, digits, pooled = None, None, []
    for low in range(0, rows, step):
        cut = slice(low, low + step)
        place = slots_ref[0:1, cut] - turn * slot_cap
        dest, row = slots_ref[1:2, cut], slots_ref[2:3, cut]
        inside = jnp.logical_and(dest >= 0, jnp.logical_and(place >= 0, place < slot_cap))
        key = jnp.where(inside, dest * slot_cap + place, -1)
        hit = jnp.where(iota2((slots, step), 0) == key, 1.0, 0.0).astype(BF)
        piece = nn(hit, dx_ref[cut])
        total = piece if total is None else total + piece
        which = iota2((16, step), 0)
        value = jnp.where(which == 0, row // NOTE_BASE, jnp.where(which == 1, row % NOTE_BASE, 0))
        piece = nt(value.astype(F32).astype(BF), hit)
        digits = piece if digits is None else digits + piece
        _, _, is_end = unpack(packed_ref[:, cut])
        caption = iota2((captions_per_step, step), 1) // seq_len
        mark = jnp.logical_and(caption == iota2((captions_per_step, step), 0), is_end)
        pooled.append(nt(hit, jnp.where(mark, 1.0, 0.0).astype(BF)))
    return total, digits, jnp.concatenate(pooled, axis=1).astype(BF)


def rows_back_body(
    slot_cap, meta_ref, probs_ref, ds_ref, a_ref, vec_ref, slots_ref, packed_ref, qk_all, unit_all, inv_all,
    dx_out, posg_ref, small_ref, seg_ref, digits_ref, pooled_ref, dx_ref, sems,
):
    blocks = probs_ref.shape[0]
    heads = a_ref.shape[0]
    seq_len, width = posg_ref.shape
    block_rows = dx_ref.shape[0] // blocks
    gain = vec_ref[0:1]
    pending = []
    gain_grad = jnp.zeros((1, width), F32)
    bias_grad = jnp.zeros((1, width), F32)
    pos_grad = jnp.zeros((seq_len, width), F32)
    for block in range(blocks):
        caps = pl.ds(block * CAP_BLOCK, CAP_BLOCK)
        here = pl.ds(block * block_rows, block_rows)
        a = a_ref[:, caps, :].reshape(heads * CAP_BLOCK, width)
        qk = qk_all.wait(block)[:, caps, :].reshape(heads * CAP_BLOCK, width)
        unit = unit_all.wait(block)[here, :].astype(F32)
        drows = tn(probs_ref[block], a) + tn(ds_ref[block], qk)
        gain_grad = gain_grad + jnp.sum(drows * unit, 0, keepdims=True)
        bias_grad = bias_grad + jnp.sum(drows, 0, keepdims=True)
        dx = norm_back(drows, unit, inv_all.wait(block)[here, 0:1], gain).astype(BF)
        dx_ref[here, :] = dx
        copy = pltpu.make_async_copy(dx_ref.at[here], dx_out.at[here], sems.at[block])
        copy.start()
        pending.append(copy)
        pos_grad = pos_grad + jnp.sum(dx.astype(F32).reshape(CAP_BLOCK, seq_len, width), 0)
    small_ref[0:1] = gain_grad
    small_ref[1:2] = bias_grad
    posg_ref[...] = pos_grad
    seg_ref[...], digits_ref[...], pooled_ref[...] = slot_sums(
        0, slot_cap, seq_len, slots_ref, packed_ref, dx_ref, seg_ref.shape[0] // slot_cap
    )
    for copy in pending:
        copy.wait()


def query_back_body(
    meta_ref, parts_ref, dx1_ref, vec_ref, pos_pick_ref, own_pick_ref, slots_ref,
    seg_ref, digits_ref, pooled_ref, pos_one_ref, small_one_ref, small_two_ref, small_three_ref, x0p, wq,
    dxp_ref, send_ref, rows_ref, smalls_ref,
):
    n_mp = parts_ref.shape[0]
    captions, width = dx1_ref.shape
    n_dp = send_ref.shape[0]
    slots = seg_ref.shape[0]
    slot_cap = slots // n_dp
    lanes = send_ref.shape[2]
    span = width // n_mp
    rank = meta_ref[0]
    dq = parts_ref[0].astype(F32)
    for i in range(1, n_mp):
        dq = dq + parts_ref[i].astype(F32)
    dq = dq.astype(BF)
    gain = vec_ref[0:1]
    unit, inverse = normalize(x0p.value())
    h1 = (unit * gain + vec_ref[1:2]).astype(BF)
    owned = jnp.sum(own_pick_ref[...].astype(F32), -1, keepdims=True)
    dh1 = nn(dq, wq.value()) * owned
    dxp = (dx1_ref[...] * owned + norm_back(dh1, unit, inverse, gain)).astype(BF)
    dxp_ref[...] = dxp
    seq_len = pos_one_ref.shape[0]
    smalls_ref[...] = jnp.zeros_like(smalls_ref)
    smalls_ref[:seq_len] = pos_one_ref[...] + tn(pos_pick_ref[...], dxp)
    at = seq_len
    smalls_ref[at : at + 1] = small_three_ref[0:1] + jnp.sum(dh1 * unit, 0, keepdims=True)
    smalls_ref[at + 1 : at + 2] = small_three_ref[1:2] + jnp.sum(dh1, 0, keepdims=True)
    smalls_ref[at + 2 : at + 5] = small_two_ref[...]
    smalls_ref[at + 5 : at + 7] = small_one_ref[...]
    smalls = smalls_ref[...]
    high = smalls.astype(BF)
    low = (smalls - high.astype(F32)).astype(BF)
    shape = (SMALLS, lanes)
    place = iota2(shape, 1) - span - iota2(shape, 0)
    pick = own_columns(rank * span, width, lanes)
    keep = iota2((captions, lanes), 1) < span
    own_dq = jnp.where(keep, nn(dq, pick), 0.0).astype(BF)
    rows_ref[...] = (
        tn(h1, own_dq)
        + tn(high, jnp.where(place == 0, 1.0, 0.0).astype(BF))
        + tn(low, jnp.where(place == SMALLS, 1.0, 0.0).astype(BF))
    )
    seg = (seg_ref[...] + nn(pooled_ref[...], dxp)).astype(BF)
    most = slots_ref[3:4, :lanes]
    which = iota2((NOTES, lanes), 0)
    most = jnp.where(which == 2, most // NOTE_BASE, most % NOTE_BASE).astype(F32)
    chunk = width // n_dp
    base = (width // lanes) * slot_cap
    for i in range(n_dp):
        for j in range(width // lanes):
            send_ref[i, j * slot_cap : (j + 1) * slot_cap, :] = seg[
                i * slot_cap : (i + 1) * slot_cap, j * lanes : (j + 1) * lanes
            ]
        send_ref[i, base : base + chunk, :] = rows_ref[pl.ds(i * chunk, chunk), :].astype(BF)
        extra = send_ref.shape[1] - NOTES
        if base + chunk < extra:
            send_ref[i, base + chunk : extra, :] = jnp.zeros((extra - base - chunk, lanes), BF)
        digits = digits_ref[:, i * slot_cap : (i + 1) * slot_cap]
        note = jnp.concatenate([digits, jnp.zeros((NOTES, lanes - slot_cap), F32)], axis=1)
        send_ref[i, extra:, :] = jnp.where(which < 2, note, most).astype(BF)


def send_body(slot_cap, meta_ref, dx_ref, dxp_ref, slots_ref, packed_ref, send_ref, digits_ref):
    n_dp, _, lanes = send_ref.shape
    width = dx_ref.shape[1]
    seq_len = dx_ref.shape[0] // dxp_ref.shape[0]
    seg, digits_ref[...], pooled = slot_sums(
        meta_ref[0], slot_cap, seq_len, slots_ref, packed_ref, dx_ref, n_dp
    )
    seg = (seg + nn(pooled, dxp_ref[...])).astype(BF)
    for i in range(n_dp):
        for j in range(width // lanes):
            send_ref[i, j * slot_cap : (j + 1) * slot_cap, :] = seg[
                i * slot_cap : (i + 1) * slot_cap, j * lanes : (j + 1) * lanes
            ]


def place_rows(row, got_ref, table_ref, slot_cap, lanes):
    n_dp = got_ref.shape[0]
    shape = (table_ref.shape[0], n_dp * slot_cap)
    hit = jnp.where(iota2(shape, 0) == row, 1.0, 0.0).astype(BF)
    for j in range(table_ref.shape[1] // lanes):
        cut = slice(j * slot_cap, (j + 1) * slot_cap)
        rows = jnp.concatenate([got_ref[i, cut, :] for i in range(n_dp)], axis=0)
        table_ref[:, j * lanes : (j + 1) * lanes] = nn(hit, rows)


def place_body(slot_cap, chunk, meta_ref, got_ref, table_ref, rest_ref, most_ref, row_ref):
    lanes = got_ref.shape[2]
    extra = got_ref.shape[1] - NOTES
    most = jnp.zeros((1, 128), F32)
    for i in range(got_ref.shape[0]):
        note = got_ref[i, extra:, :].astype(F32)
        at = slice(i * slot_cap, (i + 1) * slot_cap)
        row_ref[:, at] = note[0:1, :slot_cap] * float(NOTE_BASE) + note[1:2, :slot_cap] - 1.0
        most = jnp.maximum(most, note[2:3, :128] * float(NOTE_BASE) + note[3:4, :128])
    most_ref[...] = most
    place_rows(row_ref[...].astype(I32), got_ref, table_ref, slot_cap, lanes)
    base = table_ref.shape[1] // lanes * slot_cap
    total = got_ref[0, base : base + chunk, :].astype(F32)
    for i in range(1, got_ref.shape[0]):
        total = total + got_ref[i, base : base + chunk, :].astype(F32)
    rest_ref[...] = total


def place_more_body(meta_ref, row_ref, got_ref, old_ref, table_ref):
    lanes = got_ref.shape[2]
    slot_cap = got_ref.shape[1] // (table_ref.shape[1] // lanes)
    place_rows(row_ref[...], got_ref, table_ref, slot_cap, lanes)
    table_ref[...] += old_ref[...]


def on_device(
    token_ids, lengths, images, table, pos_table, ln1_gain, ln1_bias, w_qkv, w_out, b_out,
    ln2_gain, ln2_bias, w_up, b_up, w_down, b_down, w_head,
):
    n_mp, n_dp = lax.axis_size("mp"), lax.axis_size("dp")
    mp_rank, dp_rank = lax.axis_index("mp"), lax.axis_index("dp")
    captions, seq_len = token_ids.shape
    rows = captions * seq_len
    vocab_part, width = table.shape
    heads = width // HEAD_DIM
    own_width = width // n_mp
    ff = w_up.shape[1]
    owner_rows = vocab_part // n_dp
    slot_cap = -(-rows // (n_dp * n_mp * 16)) * 16
    slots = n_dp * slot_cap
    chunk = width // n_dp
    lanes = own_width + 2 * SMALLS
    n_all = captions * n_dp
    blocks = captions // CAP_BLOCK
    meta = jnp.stack([mp_rank, dp_rank * captions]).astype(I32)

    gather = functools.partial(lax.all_gather, axis_name="mp", axis=0)
    turned = jnp.swapaxes(w_qkv, 1, 2)
    shard = jnp.concatenate([turned, w_out[None]])
    image_f = images.astype(F32)
    image_unit = (
        image_f * lax.rsqrt(jnp.sum(image_f * image_f, -1, keepdims=True) + EPS)
    ).astype(BF)
    all_image = lax.all_gather(image_unit, ("dp", "mp"), axis=0, tiled=True)
    at_row = jnp.arange(8)[:, None]
    vecs = b_up.astype(F32)[None, :]
    for k, vec in enumerate((ln1_gain, ln1_bias, b_out, ln2_gain, ln2_bias, b_down)):
        vecs = jnp.where(at_row == k, vec.astype(F32)[None, :], vecs)

    valid = jnp.arange(seq_len)[None, :] < lengths[:, None]
    end_pick = jnp.arange(seq_len)[None, :] == (lengths - 1)[:, None]
    pos_pick = end_pick.astype(BF)
    local2 = token_ids - mp_rank * vocab_part
    owned2 = jnp.logical_and(local2 >= 0, local2 < vocab_part)
    own_pick = jnp.logical_and(end_pick, owned2).astype(BF)
    end_ids = jnp.sum(jnp.where(end_pick, token_ids, 0), 1)
    end_local = end_ids - mp_rank * vocab_part
    end_owned = jnp.logical_and(end_local >= 0, end_local < vocab_part)

    def look_up(where):
        return jnp.take(table, jnp.clip(where, 0, vocab_part - 1), axis=0, mode="clip")

    end_rows = everyone_direct(jnp.where(end_owned[:, None], look_up(end_local), 0), "mp")
    local = token_ids.reshape(rows) - mp_rank * vocab_part
    emb = look_up(after(local, end_rows[0]))
    shards = everyone(shard, "mp", emb)
    packed = token_ids + jnp.where(valid, VALID_BIT, 0) + jnp.where(end_pick, END_BIT, 0)
    packed = packed.astype(I32).reshape(1, rows)
    slot_table = vmem_call(
        functools.partial(slot_body, owner_rows, n_dp), [((8, rows), I32)], meta, [packed]
    )[0]

    full = pltpu.VMEM((width, width), BF)
    per_head = pltpu.VMEM((heads, captions, width), BF)
    per_head = pltpu.VMEM((heads, captions, width), BF)
    row_buffer = pltpu.VMEM((rows, width), BF)
    dma = pltpu.SemaphoreType.DMA
    wq, wk, wv, wo = (fetch_weight(shards, k) for k in range(4))
    pay, qk, x0p, q, unit_rows, unit, inverse = vmem_call(
        functools.partial(attend_body, n_mp, vocab_part),
        [
            ((captions, width + 128), BF),
            ((heads, captions, width), BF, False),
            ((captions, width), F32, True),
            ((captions, width), BF, True),
            ((rows, width), BF, False),
            ((rows, width), BF, False),
            ((rows, 128), F32, False),
        ],
        meta,
        [*end_rows, pos_pick, pos_table, vecs, packed],
        [wq, wk, fetch(emb, blocks), wv],
        [
            per_head, row_buffer, row_buffer, pltpu.VMEM((rows, 128), F32), per_head,
            dma((n_mp + 3 * blocks,)),
        ],
    )
    ctx, lse, x1, u, part = vmem_call(
        hidden_body,
        [
            ((captions, width), F32, True),
            ((captions, width), F32, True),
            ((captions, width), F32, True),
            ((captions, ff), F32, True),
            ((captions, width), BF),
        ],
        meta,
        [gather(pay), vecs],
        [fetch(x0p), wo, fetch(w_up), fetch(w_down)],
    )
    pooled, proj, powers, sums = vmem_call(
        logits_body,
        [
            ((captions, width), BF, True),
            ((captions, width), F32, True),
            ((captions, n_all), F32, True),
            ((n_dp, 1, n_all + 128), F32),
        ],
        meta,
        [gather(part), vecs],
        [fetch(x1), fetch(w_head), fetch(all_image)],
    )
    all_sums = lax.all_to_all(sums, "dp", 0, 0, tiled=True)
    loss, dpooled, part, down, up, small_one = vmem_call(
        loss_body,
        [
            ((1, 128), F32),
            ((captions, width), F32),
            ((captions, width), BF),
            ((width, ff + own_width), BF),
            ((width, ff), BF),
            ((2, width), F32),
        ],
        meta,
        [all_sums, vecs],
        [
            fetch(powers), fetch(all_image), fetch(proj), fetch(w_head), fetch(u), fetch(w_down),
            fetch(w_up), fetch(x1), fetch(pooled),
        ],
    )
    dp_bits, mp_bits = bits_of("dp"), bits_of("mp")
    down = halve(down.reshape(n_dp, chunk, ff + own_width), "dp", dp_bits[0])
    parts = gather(part)
    up = halve(after(up, parts).reshape(n_dp, chunk, ff), "dp", dp_bits[0])
    dx1, dq_part, wout, wkv, a, probs, dscores, small_two = vmem_call(
        functools.partial(attend_back_body, vocab_part),
        [
            ((captions, width), F32),
            ((captions, width), BF),
            ((width, own_width), BF),
            ((n_mp, width, 2 * own_width), BF),
            ((heads, captions, width), BF),
            ((blocks, heads * CAP_BLOCK, CAP_BLOCK * seq_len), BF),
            ((blocks, heads * CAP_BLOCK, CAP_BLOCK * seq_len), BF),
            ((3, width), F32),
        ],
        meta,
        [parts, packed, vecs, dpooled],
        [
            fetch(x1), fetch(ctx), wo, wv, fetch(lse), fetch(qk, blocks, 1),
            fetch(unit_rows, blocks), wk, fetch(q),
        ],
        [per_head, per_head],
    )
    wkv = halve(wkv, "mp", mp_bits[0])
    dq_parts = gather(after(dq_part, down))
    dx, pos_one, small_three, seg, digits, pooled_slots = vmem_call(
        functools.partial(rows_back_body, slot_cap),
        [
            ((rows, width), BF, False),
            ((seq_len, width), F32),
            ((2, width), F32),
            ((slots, width), F32),
            ((16, slots), F32),
            ((slots, captions), BF),
        ],
        meta,
        [after(probs, dq_parts, wkv, up), dscores, a, vecs, slot_table, packed],
        [fetch(qk, blocks, 1), fetch(unit, blocks), fetch(inverse, blocks)],
        [row_buffer, dma((blocks,))],
    )
    for bit in mp_bits[1:]:
        wkv = halve(wkv, "mp", bit)
    for bit in dp_bits[1:]:
        down = halve(down, "dp", bit)
    for bit in dp_bits[1:]:
        up = halve(up, "dp", bit)
    down, up = down[0], up[0]
    wkvo = jnp.concatenate([wkv[0].astype(BF), wout], 1)
    wkvo = wkvo.reshape(n_dp, chunk, 3 * own_width)
    chunk_pad = -(-chunk // 16) * 16
    send_rows = width // lanes * slot_cap
    dxp, send = vmem_call(
        query_back_body,
        [((captions, width), BF), ((n_dp, send_rows + chunk_pad + NOTES, lanes), BF)],
        meta,
        [
            dq_parts, dx1, vecs, pos_pick, own_pick, slot_table, seg, digits, pooled_slots, pos_one,
            small_one, small_two, small_three,
        ],
        [fetch(x0p), wq],
        [pltpu.VMEM((width, lanes), F32), pltpu.VMEM((SMALLS, width), F32)],
    )
    got = lax.all_to_all(send, "dp", 0, 0, tiled=True)
    table_grad, rest, most_all = vmem_call(
        functools.partial(place_body, slot_cap, chunk),
        [((owner_rows, width), F32), ((chunk, lanes), F32), ((1, 128), F32)],
        meta,
        [got],
        (),
        [pltpu.VMEM((1, slots), F32)],
    )
    most_all = most_all[0, 0].astype(I32)
    small = rest[:, own_width : own_width + SMALLS] + rest[:, own_width + SMALLS :]
    last = gather(jnp.concatenate([down[:, ff:], small, jnp.zeros_like(small)], 1))
    for bit in dp_bits:
        wkvo = halve(wkvo if 2 * bit < n_dp else after(wkvo, last), "dp", bit)
    wkvo = wkvo[0]

    def another(carry):
        turn, total = carry
        sent, digits = vmem_call(
            functools.partial(send_body, slot_cap),
            [((n_dp, send_rows, lanes), BF), ((16, slots), F32)],
            turn.reshape(1),
            [dx, dxp, slot_table, packed],
        )
        row = (digits[0] * NOTE_BASE + digits[1] - 1.0).astype(I32)
        row = lax.all_to_all(row.reshape(n_dp, slot_cap), "dp", 0, 0, tiled=True)
        sent = lax.all_to_all(sent, "dp", 0, 0, tiled=True)
        total = vmem_call(
            place_more_body,
            [((owner_rows, width), F32)],
            meta,
            [row.reshape(1, slots), sent, total],
        )[0]
        return turn + 1, total

    _, table_grad = lax.while_loop(
        lambda carry: carry[0] * slot_cap < most_all, another, (jnp.int32(1), table_grad)
    )
    w_head_grad = jnp.swapaxes(last[:, :, :own_width], 0, 1).reshape(chunk, width)
    shared = jnp.sum(last[:, :, own_width : own_width + SMALLS], 0)
    qkv_grad = jnp.stack(
        [rest[:, :own_width], wkvo[:, :own_width], wkvo[:, own_width : 2 * own_width]]
    )
    return (
        loss[0, 0],
        table_grad,
        shared[:, :seq_len].T,
        shared[:, seq_len],
        shared[:, seq_len + 1],
        qkv_grad,
        wkvo[:, 2 * own_width :].T,
        small[:, seq_len + 4],
        small[:, seq_len + 2],
        small[:, seq_len + 3],
        up,
        small[:, seq_len + 6],
        down[:, :ff].T,
        small[:, seq_len + 5],
        w_head_grad,
    )


def solution(mesh):
    placed = (
        P("dp", None),
        P("dp"),
        P(("dp", "mp"), None),
        P("mp", None),
        P(),
        P(),
        P(),
        P(None, None, "mp"),
        P("mp", None),
        P(),
        P(),
        P(),
        P(None, "mp"),
        P("mp"),
        P("mp", None),
        P(),
        P(),
    )
    return jax.shard_map(
        on_device,
        mesh=mesh,
        in_specs=placed,
        out_specs=(
            P(),
            P(("mp", "dp"), None),
            P(None, "dp"),
            P("dp"),
            P("dp"),
            P(None, "dp", "mp"),
            P("mp", "dp"),
            P("dp"),
            P("dp"),
            P("dp"),
            P("dp", "mp"),
            P(("mp", "dp")),
            P("mp", "dp"),
            P("dp"),
            P("dp", None),
        ),
        check_vma=False,
    )
```

```python
import functools
import math

import jax
import jax.numpy as jnp
from jax import lax
from jax.experimental import pallas as pl
from jax.experimental.pallas import tpu as pltpu
from jax.sharding import PartitionSpec as P

HEAD_DIM = 64
LOGIT_SCALE = 50.0
EPS = 1e-06
MASK_FILL = -1000000000.0
NO_KEY = -1e30
BF = jnp.bfloat16
F32 = jnp.float32
I32 = jnp.int32
GELU_C = math.sqrt(2.0 / math.pi)
CAP_BLOCK = 16
SMALLS = 32
NOTES = 8
VALID_BIT = 1 << 20
END_BIT = 1 << 21
NOTE_BASE = 32
WORK = 920000000
DOWN_BIT = 1
UP_BIT = 2
VMEM_LIMIT = 40 * 1024 * 1024


def nn(a, b):
    return lax.dot_general(a, b, (((1,), (0,)), ((), ())), preferred_element_type=F32)


def nt(a, b):
    return lax.dot_general(a, b, (((1,), (1,)), ((), ())), preferred_element_type=F32)


def tn(a, b):
    return lax.dot_general(a, b, (((0,), (0,)), ((), ())), preferred_element_type=F32)


def normalize(rows):
    centred = rows - jnp.mean(rows, -1, keepdims=True)
    inverse = lax.rsqrt(jnp.mean(centred * centred, -1, keepdims=True) + EPS)
    return centred * inverse, inverse


def norm_back(upstream, unit, inverse, gain):
    scaled = upstream * gain
    mean_scaled = jnp.mean(scaled, -1, keepdims=True)
    mean_unit = jnp.mean(scaled * unit, -1, keepdims=True)
    return inverse * (scaled - mean_scaled - unit * mean_unit)


def iota2(shape, dim):
    return lax.broadcasted_iota(I32, shape, dim)


class Late:
    def __init__(self, ref, pairs, sems):
        self.ref = ref
        self.copies = [
            pltpu.make_async_copy(src, dst, sem) for (src, dst), sem in zip(pairs, sems)
        ]
        self.waiting = set(range(len(self.copies)))

    def start(self):
        for copy in self.copies:
            copy.start()

    def wait(self, part=None):
        for k in sorted(self.waiting) if part is None else [part]:
            if k in self.waiting:
                self.copies[k].wait()
                self.waiting.discard(k)
        return self.ref

    def value(self):
        return self.wait()[...]


def fetch(array, parts=1, axis=0):
    return ("blocks", [array], parts, axis)


def fetch_weight(shards, which):
    return ("weight", list(shards), which, 0)


def vmem_call(body, outs, meta, args, late=(), scratch=(), flops=1):
    vmem = pl.BlockSpec(memory_space=pltpu.VMEM)
    hbm = pl.BlockSpec(memory_space=pltpu.HBM)
    sources, buffers, counts = [], [], []
    for kind, arrays, parts, axis in late:
        sources += arrays
        if kind == "weight":
            _, rows, width = arrays[0].shape
            buffers.append(pltpu.VMEM((rows * len(arrays), width), arrays[0].dtype))
            counts.append(len(arrays))
        else:
            buffers.append(pltpu.VMEM(arrays[0].shape, arrays[0].dtype))
            counts.append(parts)

    staged = [k for k, o in enumerate(outs) if len(o) > 2 and o[2]]

    def kernel(meta_ref, *refs):
        arg_refs, refs = refs[: len(args)], refs[len(args) :]
        source_refs, refs = refs[: len(sources)], refs[len(sources) :]
        out_refs, refs = refs[: len(outs)], refs[len(outs) :]
        buffer_refs, refs = refs[: len(buffers)], refs[len(buffers) :]
        sems, stage_sems, refs = refs[0], refs[1], refs[2:]
        stages, refs = refs[: len(staged)], refs[len(staged) :]
        targets = list(out_refs)
        for k, stage in zip(staged, stages):
            targets[k] = stage
        handles, at, place = [], 0, 0
        for (kind, arrays, parts, axis), buffer in zip(late, buffer_refs):
            if kind == "weight":
                rows = arrays[0].shape[1]
                pairs = []
                for k in range(len(arrays)):
                    low = pl.multiple_of((meta_ref[0] ^ k) * rows, rows)
                    pairs.append((source_refs[place + k].at[parts], buffer.at[pl.ds(low, rows)]))
                place += len(arrays)
            else:
                size = arrays[0].shape[axis] // parts
                pairs = []
                for k in range(parts):
                    cut = (slice(None),) * axis + (pl.ds(k * size, size),)
                    pairs.append((source_refs[place].at[cut], buffer.at[cut]))
                place += 1
            handles.append(Late(buffer, pairs, [sems.at[at + k] for k in range(len(pairs))]))
            at += len(pairs)
        for handle in handles:
            handle.start()
        body(meta_ref, *arg_refs, *handles, *targets, *refs)
        copies = [
            pltpu.make_async_copy(stage, out_refs[k], stage_sems.at[i])
            for i, (k, stage) in enumerate(zip(staged, stages))
        ]
        for copy in copies:
            copy.start()
        for handle in handles:
            handle.wait()
        for copy in copies:
            copy.wait()

    return pl.pallas_call(
        kernel,
        out_shape=[
            pltpu.HBM(*o[:2]) if len(o) > 2 else jax.ShapeDtypeStruct(*o) for o in outs
        ],
        in_specs=[pl.BlockSpec(memory_space=pltpu.SMEM)]
        + [vmem] * len(args)
        + [hbm] * len(sources),
        out_specs=[hbm if len(o) > 2 else vmem for o in outs],
        scratch_shapes=[
            *buffers,
            pltpu.SemaphoreType.DMA((max(1, sum(counts)),)),
            pltpu.SemaphoreType.DMA((max(1, len(staged)),)),
            *(pltpu.VMEM(*outs[k][:2]) for k in staged),
            *scratch,
        ],
        compiler_params=pltpu.CompilerParams(vmem_limit_bytes=VMEM_LIMIT),
        cost_estimate=pl.CostEstimate(flops=flops, bytes_accessed=1, transcendentals=0),
    )(meta, *args, *(pltpu.with_memory_space_constraint(x, pltpu.HBM) for x in sources))


def exchange_half(kept, sent, axis, bit, last):
    count = lax.axis_size(axis)
    got = lax.ppermute(sent, axis, [(i, i ^ bit) for i in range(count)])
    total = kept.astype(F32) + got.astype(F32)
    return total if last else total.astype(BF)


def halve(total, axis, bits, bit):
    low = 1 << bits.index(bit)
    pairs = total.reshape((total.shape[0] // (2 * low), 2, low) + total.shape[1:])
    shape = (total.shape[0] // 2,) + total.shape[1:]
    mine = (lax.axis_index(axis) // bit) % 2
    sent = lax.dynamic_index_in_dim(pairs, 1 - mine, 1, keepdims=False).reshape(shape)
    kept = lax.dynamic_index_in_dim(pairs, mine, 1, keepdims=False).reshape(shape)
    return exchange_half(kept, sent, axis, bit, len(bits) == 1)


def split_blocks(blocks, bit, mine, kept_ref, sent_ref):
    place = 0
    for i in range(len(blocks)):
        if i & bit == 0:
            first, second = blocks[i](), blocks[i | bit]()
            kept_ref[place] = jnp.where(mine == 0, first, second).astype(BF)
            sent_ref[place] = jnp.where(mine == 0, second, first).astype(BF)
            place += 1


def bits_of(axis):
    count = lax.axis_size(axis)
    return [1 << k for k in range(count.bit_length() - 1)]


def after(x, *others):
    return lax.optimization_barrier((x, others))[0]


def everyone(x, axis, before):
    count = lax.axis_size(axis)
    have = {0: x}
    bit = count // 2
    while bit:
        pairs = [(i, i ^ bit) for i in range(count)]
        for k, v in list(have.items()):
            have[k | bit] = lax.ppermute(after(v, before) if k else v, axis, pairs)
        bit //= 2
    return [have[k] for k in range(count)]


def own_columns(start, width, own_width):
    shape = (width, own_width)
    hit = iota2(shape, 0) == start + iota2(shape, 1)
    return jnp.where(hit, 1.0, 0.0).astype(BF)


def unpack(packed):
    return packed % VALID_BIT, packed // VALID_BIT % 2 > 0, packed // END_BIT > 0


def own_code(packed, rank, vocab_part):
    ids, valid, _ = unpack(packed)
    return jnp.where(ids // vocab_part == rank, jnp.where(valid, 2, 1), 0)


def head_mask(captions, span):
    shape = (span // HEAD_DIM * captions, span)
    return (iota2(shape, 0) // captions) == (iota2(shape, 1) // HEAD_DIM)


def spread_heads(rows, group, mask):
    span = mask.shape[1]
    part = rows[:, group * span : (group + 1) * span].astype(F32)
    tall = jnp.concatenate([part] * (span // HEAD_DIM), axis=0)
    return jnp.where(mask, tall, 0.0).astype(BF)


def fold_heads(tall, captions, mask):
    kept = jnp.where(mask, tall, 0.0)
    total = kept[:captions]
    for h in range(1, tall.shape[0] // captions):
        total = total + kept[h * captions : (h + 1) * captions]
    return total


def block_masks(code, heads, seq_len):
    shape = (heads * CAP_BLOCK, CAP_BLOCK * seq_len)
    same = (iota2(shape, 0) % CAP_BLOCK) == (iota2(shape, 1) // seq_len)
    own = jnp.logical_and(same, code > 0)
    return own, jnp.logical_and(same, code > 1)


def masked_block_scores(qk, rows, own, valid):
    raw = nt(qk, rows)
    return jnp.where(own, jnp.where(valid, raw, MASK_FILL), NO_KEY)


def rows_body(
    vocab_part, meta_ref, pos_ref, vec_ref, packed_ref, emb,
    end_ref, rows_out, unit_out, inv_out, rows_ref, unit_ref, inv_ref, sems,
):
    captions = end_ref.shape[0]
    seq_len = pos_ref.shape[0]
    block_rows = CAP_BLOCK * seq_len
    gain, bias = vec_ref[0:1], vec_ref[1:2]
    pos = jnp.concatenate([pos_ref[...].astype(F32)] * CAP_BLOCK, axis=0)
    pending = []

    def write_back(src, dst):
        copy = pltpu.make_async_copy(src, dst, sems.at[len(pending)])
        copy.start()
        pending.append(copy)

    for block in range(captions // CAP_BLOCK):
        here = pl.ds(block * block_rows, block_rows)
        packed = packed_ref[:, block * block_rows : (block + 1) * block_rows]
        low = emb.wait(block)[here, :]
        ids, _, is_end = unpack(packed)
        shape = (CAP_BLOCK, block_rows)
        mark = jnp.logical_and(is_end, ids // vocab_part == meta_ref[0])
        mark = jnp.logical_and(iota2(shape, 0) == iota2(shape, 1) // seq_len, mark)
        ends = nn(jnp.where(mark, 1.0, 0.0).astype(BF), low)
        end_ref[block * CAP_BLOCK : (block + 1) * CAP_BLOCK] = ends.astype(BF)
        unit, inverse = normalize(low.astype(F32) + pos)
        unit_ref[here, :] = unit.astype(BF)
        write_back(unit_ref.at[here], unit_out.at[here])
        inv_ref[here, :] = jnp.broadcast_to(inverse, (block_rows, 128))
        write_back(inv_ref.at[here], inv_out.at[here])
        rows_ref[here, :] = (unit * gain + bias).astype(BF)
        write_back(rows_ref.at[here], rows_out.at[here])
    for copy in pending:
        copy.wait()


def attend_body(
    vocab_part, meta_ref, ends_ref, pos_pick_ref, pos_ref, vec_ref, packed_ref, wq, wk, rows_all, wv,
    pay_ref, qk_out, x0p_ref, q_ref, qk_ref, t_ref, sems,
):
    n_mp = ends_ref.shape[0]
    captions, width = x0p_ref.shape
    heads = width // HEAD_DIM
    span = width // n_mp
    per_group = span // HEAD_DIM
    seq_len = pos_ref.shape[0]
    block_rows = CAP_BLOCK * seq_len
    gain, bias = vec_ref[0:1], vec_ref[1:2]
    pooled_in = nn(pos_pick_ref[...], pos_ref[...])
    for i in range(n_mp):
        pooled_in = pooled_in + ends_ref[i].astype(F32)
    pending = []
    x0p_ref[...] = pooled_in
    unit, _ = normalize(pooled_in)
    q = nt((unit * gain + bias).astype(BF), wq.value()).astype(BF)
    q_ref[...] = q
    mask = head_mask(captions, span)
    scale = 1.0 / math.sqrt(HEAD_DIM)
    wk_ref = wk.wait()
    for g in range(n_mp):
        some = slice(g * per_group, (g + 1) * per_group)
        tall = nn(spread_heads(q, g, mask), wk_ref[g * span : (g + 1) * span]) * scale
        qk_ref[some] = tall.astype(BF).reshape(per_group, captions, width)
        copy = pltpu.make_async_copy(qk_ref.at[some], qk_out.at[some], sems.at[g])
        copy.start()
        pending.append(copy)
    lane = iota2((heads, CAP_BLOCK, 128), 2)
    head_of = iota2((heads, CAP_BLOCK, 128), 0)
    for block in range(captions // CAP_BLOCK):
        caps = pl.ds(block * CAP_BLOCK, CAP_BLOCK)
        here = pl.ds(block * block_rows, block_rows)
        rows = rows_all.wait(block)[here, :]
        code = own_code(packed_ref[:, block * block_rows : (block + 1) * block_rows], meta_ref[0], vocab_part)
        own, valid = block_masks(code, heads, seq_len)
        qk = qk_ref[:, caps, :].reshape(heads * CAP_BLOCK, width)
        scores = masked_block_scores(qk, rows, own, valid)
        top = jnp.max(scores, -1, keepdims=True)
        weights = jnp.where(own, jnp.exp(scores - top), 0.0)
        total = jnp.sum(weights, -1, keepdims=True)
        some = total > 0.0
        total = jnp.where(some, total, 1.0)
        log_total = jnp.where(some, top + jnp.log(total), NO_KEY)
        mixed = nn((weights / total).astype(BF), rows)
        t_ref[:, caps, :] = mixed.astype(BF).reshape(heads, CAP_BLOCK, width)
        first = log_total.astype(BF).astype(F32)
        second = (log_total - first).astype(BF).astype(F32)
        third = log_total - first - second
        stat = jnp.zeros((heads, CAP_BLOCK, 128), F32)
        for k, piece in enumerate((first, second, third)):
            stat = stat + jnp.where(
                lane == head_of + 16 * k, piece.reshape(heads, CAP_BLOCK, 1), 0.0
            )
        pay_ref[caps, width:] = jnp.sum(stat, 0).astype(BF)
    wv_ref = wv.wait()
    for g in range(n_mp):
        tall = t_ref[g * per_group : (g + 1) * per_group].reshape(per_group * captions, width)
        piece = nt(tall, wv_ref[g * span : (g + 1) * span])
        pay_ref[:, g * span : (g + 1) * span] = fold_heads(piece, captions, mask).astype(BF)
    for copy in pending:
        copy.wait()


def hidden_body(
    meta_ref, pay_ref, vec_ref, x0p, wo, wup, wdown,
    ctx_ref, lse_ref, x1_ref, u_ref, part_ref,
):
    n_mp = pay_ref.shape[0]
    captions, width = ctx_ref.shape
    shape = (128, width)
    stat_row, head = iota2(shape, 0), iota2(shape, 1) // HEAD_DIM
    picks = jnp.logical_and(stat_row % 16 == head, stat_row < 48)
    expand = jnp.where(picks, 1.0, 0.0).astype(BF)
    logs = [nn(pay_ref[i, :, width:], expand) for i in range(n_mp)]
    top = functools.reduce(jnp.maximum, logs)
    total = jnp.zeros_like(top)
    ctx = jnp.zeros_like(top)
    for i in range(n_mp):
        weight = jnp.exp(logs[i] - top)
        total = total + weight
        ctx = ctx + weight * pay_ref[i, :, :width].astype(F32)
    ctx = ctx / total
    ctx_ref[...] = ctx
    lse_ref[...] = top + jnp.log(total)
    x1 = x0p.value() + nn(ctx.astype(BF), wo.value()) + vec_ref[2:3]
    x1_ref[...] = x1
    unit, _ = normalize(x1)
    h2 = (unit * vec_ref[3:4] + vec_ref[4:5]).astype(BF)
    u = nn(h2, wup.value()) + vec_ref[6:7]
    u_ref[...] = u
    hidden = (0.5 * u * (1.0 + jnp.tanh(GELU_C * (u + 0.044715 * u * u * u)))).astype(BF)
    part_ref[...] = nn(hidden, wdown.value()).astype(BF)


def logits_body(
    meta_ref, parts_ref, vec_ref, x1, wh, images,
    pooled_ref, proj_ref, e_ref, sums_ref,
):
    x2 = x1.value() + vec_ref[5:6]
    for i in range(parts_ref.shape[0]):
        x2 = x2 + parts_ref[i].astype(F32)
    pooled = x2.astype(BF)
    pooled_ref[...] = pooled
    proj = nn(pooled, wh.value())
    proj_ref[...] = proj
    text = (proj * lax.rsqrt(jnp.sum(proj * proj, -1, keepdims=True) + EPS)).astype(BF)
    logits = LOGIT_SCALE * nt(text, images.value())
    powers = jnp.exp(logits)
    e_ref[...] = powers
    n_all = powers.shape[1]
    is_diag = iota2(logits.shape, 1) == meta_ref[1] + iota2(logits.shape, 0)
    rows = jnp.log(jnp.sum(powers, -1, keepdims=True))
    rows = rows - 2.0 * jnp.sum(jnp.where(is_diag, logits, 0.0), -1, keepdims=True)
    cols = jnp.sum(powers, 0, keepdims=True)
    rows = jnp.broadcast_to(jnp.sum(rows, 0, keepdims=True), (1, 128))
    for i in range(sums_ref.shape[0]):
        sums_ref[i, :, :n_all] = cols
        sums_ref[i, :, n_all:] = rows


def loss_body(
    meta_ref, sums_ref, vec_ref, e, images, proj, wh, u, wdown, wup, x1, pooled,
    loss_ref, dpooled_ref, part_ref, down_kept, down_sent, up_kept, up_sent, small_ref,
    down_ref, up_ref,
):
    width = dpooled_ref.shape[1]
    sums = jnp.sum(sums_ref[...], 0)
    n_all = sums.shape[1] - 128
    cols = sums[:, :n_all]
    loss = jnp.sum(jnp.log(cols), -1, keepdims=True) + sums[:, n_all : n_all + 1]
    loss_ref[...] = jnp.broadcast_to(loss * (0.5 / n_all), (1, 128))
    powers = e.value()
    row_inv = 1.0 / jnp.sum(powers, -1, keepdims=True)
    is_diag = iota2(powers.shape, 1) == meta_ref[1] + iota2(powers.shape, 0)
    grad = powers * row_inv + powers * (1.0 / cols) - jnp.where(is_diag, 2.0, 0.0)
    grad = (grad * (0.5 / n_all)).astype(BF)
    dtext = LOGIT_SCALE * nn(grad, images.value())
    proj = proj.value()
    inv = lax.rsqrt(jnp.sum(proj * proj, -1, keepdims=True) + EPS)
    along = jnp.sum(proj * dtext, -1, keepdims=True)
    dproj = (inv * dtext - inv * inv * inv * proj * along).astype(BF)
    dpooled = nt(dproj, wh.value())
    dpooled_ref[...] = dpooled
    dy = dpooled.astype(BF)
    u = u.value()
    th = jnp.tanh(GELU_C * (u + 0.044715 * u * u * u))
    slope = 0.5 * (1.0 + th) + 0.5 * u * (1.0 - th * th) * (
        GELU_C * (1.0 + 3.0 * 0.044715 * u * u)
    )
    du = (nt(dy, wdown.value()) * slope).astype(BF)
    part_ref[...] = nt(du, wup.value()).astype(BF)
    hidden = (0.5 * u * (1.0 + th)).astype(BF)
    unit, _ = normalize(x1.value())
    h2 = (unit * vec_ref[3:4] + vec_ref[4:5]).astype(BF)
    ff = u.shape[1]
    own_width = down_ref.shape[1] - ff
    pick = own_columns(meta_ref[0] * own_width, width, own_width)
    down_ref[:, :ff] = tn(dy, hidden)
    up_ref[...] = tn(h2, du)
    down_ref[:, ff:] = tn(pooled.value(), nn(dproj, pick).astype(BF))
    chunk = down_kept.shape[1]
    n_dp = 2 * down_kept.shape[0]
    for ref, bit, kept, sent in (
        (down_ref, DOWN_BIT, down_kept, down_sent),
        (up_ref, UP_BIT, up_kept, up_sent),
    ):
        blocks = [
            functools.partial(lambda ref, i: ref[pl.ds(i * chunk, chunk), :], ref, i)
            for i in range(n_dp)
        ]
        split_blocks(blocks, bit, meta_ref[2] // bit % 2, kept, sent)
    small_ref[0:1] = jnp.sum(dy.astype(F32), 0, keepdims=True)
    small_ref[1:2] = jnp.sum(du.astype(F32), 0, keepdims=True)


def attend_back_body(
    vocab_part, meta_ref, parts_ref, packed_ref, vec_ref, dpooled_ref, x1, ctx, wo, wv, lse, qk_all, rows_all, wk, q,
    dx1_ref, dq_ref, wout_ref, wkv_kept, wkv_sent, a_ref, probs_ref, ds_ref, small_ref,
    t_ref, s_ref, wkv_ref,
):
    n_mp = parts_ref.shape[0]
    captions, width = dpooled_ref.shape
    heads = width // HEAD_DIM
    span = width // n_mp
    per_group = span // HEAD_DIM
    block_rows = rows_all.ref.shape[0] // (captions // CAP_BLOCK)
    seq_len = block_rows // CAP_BLOCK
    rank = meta_ref[0]
    dh2 = parts_ref[0].astype(F32)
    for i in range(1, n_mp):
        dh2 = dh2 + parts_ref[i].astype(F32)
    unit2, inv2 = normalize(x1.value())
    small_ref[0:1] = jnp.sum(dh2 * unit2, 0, keepdims=True)
    small_ref[1:2] = jnp.sum(dh2, 0, keepdims=True)
    dx1 = dpooled_ref[...] + norm_back(dh2, unit2, inv2, vec_ref[3:4])
    dx1_ref[...] = dx1
    da = dx1.astype(BF)
    small_ref[2:3] = jnp.sum(da.astype(F32), 0, keepdims=True)
    ctx = ctx.value()
    pick = own_columns(rank * span, width, span)
    wout_ref[...] = tn(da, nn(ctx.astype(BF), pick).astype(BF)).astype(BF)
    dctx = nt(da, wo.value()).astype(BF)
    mask = head_mask(captions, span)
    wv_ref = wv.wait()
    for g in range(n_mp):
        tall = nn(spread_heads(dctx, g, mask), wv_ref[g * span : (g + 1) * span])
        a_ref[g * per_group : (g + 1) * per_group] = tall.astype(BF).reshape(
            per_group, captions, width
        )
    prod = dctx.astype(F32) * ctx
    lse = lse.value()
    scale = 1.0 / math.sqrt(HEAD_DIM)
    tall_shape = (heads * CAP_BLOCK, width)
    of_head = (iota2(tall_shape, 0) // CAP_BLOCK) == (iota2(tall_shape, 1) // HEAD_DIM)
    at_head = (iota2(tall_shape, 0) // CAP_BLOCK) * HEAD_DIM == iota2(tall_shape, 1)
    for block in range(captions // CAP_BLOCK):
        low = block * CAP_BLOCK
        caps = pl.ds(low, CAP_BLOCK)
        rows = rows_all.wait(block)[pl.ds(block * block_rows, block_rows), :]
        code = own_code(packed_ref[:, block * block_rows : (block + 1) * block_rows], meta_ref[0], vocab_part)
        own, valid = block_masks(code, heads, seq_len)
        qk = qk_all.wait(block)[:, caps, :].reshape(heads * CAP_BLOCK, width)
        scores = masked_block_scores(qk, rows, own, valid)
        tall = jnp.concatenate([lse[low : low + CAP_BLOCK]] * heads, axis=0)
        log_total = jnp.sum(jnp.where(at_head, tall, 0.0), -1, keepdims=True)
        tall = jnp.concatenate([prod[low : low + CAP_BLOCK]] * heads, axis=0)
        row_sum = jnp.sum(jnp.where(of_head, tall, 0.0), -1, keepdims=True)
        probs = jnp.where(own, jnp.exp(scores - log_total), 0.0)
        a = a_ref[:, caps, :].reshape(heads * CAP_BLOCK, width)
        dscores = (probs * (nt(a, rows) - row_sum)).astype(BF)
        probs = probs.astype(BF)
        probs_ref[block] = probs
        ds_ref[block] = dscores
        t_ref[:, caps, :] = nn(probs, rows).astype(BF).reshape(heads, CAP_BLOCK, width)
        s_ref[:, caps, :] = (
            (nn(dscores, rows) * scale).astype(BF).reshape(heads, CAP_BLOCK, width)
        )
    q = q.value()
    wk_ref = wk.wait()
    for g in range(n_mp):
        some = slice(g * per_group, (g + 1) * per_group)
        tall = s_ref[some].reshape(per_group * captions, width)
        piece = nt(tall, wk_ref[g * span : (g + 1) * span])
        dq_ref[:, g * span : (g + 1) * span] = fold_heads(piece, captions, mask).astype(BF)
        wkv_ref[g, :, :span] = tn(tall, spread_heads(q, g, mask)).astype(BF)
        tall = t_ref[some].reshape(per_group * captions, width)
        wkv_ref[g, :, span:] = tn(tall, spread_heads(dctx, g, mask)).astype(BF)
    blocks = [functools.partial(lambda g: wkv_ref[g], g) for g in range(n_mp)]
    split_blocks(blocks, 1, rank % 2, wkv_kept, wkv_sent)


def slot_body(owner_rows, n_dp, meta_ref, packed_ref, out_ref):
    rows = packed_ref.shape[1]
    side = 128
    ids, _, _ = unpack(packed_ref[...])
    owner = ids // owner_rows
    order = iota2((1, rows), 1)

    def columns(row, k):
        piece = row[:, k * side : (k + 1) * side].astype(F32)
        return jnp.transpose(jnp.broadcast_to(piece, (side, side))).astype(I32)

    def tall(column):
        return jnp.concatenate([column] * (rows // side), axis=1)

    first_at = jnp.full((1, rows), rows, I32)
    for k in range(rows // side):
        there = k * side + iota2((side, rows), 0)
        hit = jnp.where(tall(columns(ids, k)) == ids, there, rows)
        first_at = jnp.minimum(first_at, jnp.min(hit, 0, keepdims=True))
    is_first = first_at == order
    first_owner = jnp.where(is_first, owner, -1)
    slot = jnp.zeros((1, rows), I32)
    for k in range(rows // side):
        there = k * side + iota2((side, rows), 0)
        ahead = jnp.logical_and(tall(columns(first_owner, k)) == owner, there < first_at)
        slot = slot + jnp.sum(jnp.where(ahead, 1, 0), 0, keepdims=True)
    here = owner - meta_ref[0] * n_dp
    dest = jnp.where(jnp.logical_and(here >= 0, here < n_dp), here, -1)
    most = jnp.max(slot.astype(F32), 1, keepdims=True).astype(I32) + 1
    out_ref[0:1] = slot
    out_ref[1:2] = dest
    out_ref[2:3] = jnp.where(is_first, ids % owner_rows + 1, 0)
    out_ref[3:4] = jnp.broadcast_to(most, (1, rows))
    out_ref[4:8] = jnp.zeros((4, rows), I32)


def slot_sums(turn, slot_cap, seq_len, slots_ref, packed_ref, dx_ref, n_dp):
    slots = n_dp * slot_cap
    rows = dx_ref.shape[0]
    step = min(512, rows)
    captions_per_step = step // seq_len
    total, digits, pooled = None, None, []
    for low in range(0, rows, step):
        cut = slice(low, low + step)
        place = slots_ref[0:1, cut] - turn * slot_cap
        dest, row = slots_ref[1:2, cut], slots_ref[2:3, cut]
        inside = jnp.logical_and(dest >= 0, jnp.logical_and(place >= 0, place < slot_cap))
        key = jnp.where(inside, dest * slot_cap + place, -1)
        hit = jnp.where(iota2((slots, step), 0) == key, 1.0, 0.0).astype(BF)
        piece = nn(hit, dx_ref[cut])
        total = piece if total is None else total + piece
        which = iota2((16, step), 0)
        value = jnp.where(which == 0, row // NOTE_BASE, jnp.where(which == 1, row % NOTE_BASE, 0))
        piece = nt(value.astype(F32).astype(BF), hit)
        digits = piece if digits is None else digits + piece
        _, _, is_end = unpack(packed_ref[:, cut])
        caption = iota2((captions_per_step, step), 1) // seq_len
        mark = jnp.logical_and(caption == iota2((captions_per_step, step), 0), is_end)
        pooled.append(nt(hit, jnp.where(mark, 1.0, 0.0).astype(BF)))
    return total, digits, jnp.concatenate(pooled, axis=1).astype(BF)


def rows_back_body(
    slot_cap, meta_ref, probs_ref, ds_ref, a_ref, vec_ref, slots_ref, packed_ref, qk_all, unit_all, inv_all,
    dx_out, posg_ref, small_ref, seg_ref, digits_ref, pooled_ref, dx_ref, sems,
):
    blocks = probs_ref.shape[0]
    heads = a_ref.shape[0]
    seq_len, width = posg_ref.shape
    block_rows = dx_ref.shape[0] // blocks
    gain = vec_ref[0:1]
    pending = []
    gain_grad = jnp.zeros((1, width), F32)
    bias_grad = jnp.zeros((1, width), F32)
    pos_grad = jnp.zeros((seq_len, width), F32)
    for block in range(blocks):
        caps = pl.ds(block * CAP_BLOCK, CAP_BLOCK)
        here = pl.ds(block * block_rows, block_rows)
        a = a_ref[:, caps, :].reshape(heads * CAP_BLOCK, width)
        qk = qk_all.wait(block)[:, caps, :].reshape(heads * CAP_BLOCK, width)
        unit = unit_all.wait(block)[here, :].astype(F32)
        drows = tn(probs_ref[block], a) + tn(ds_ref[block], qk)
        gain_grad = gain_grad + jnp.sum(drows * unit, 0, keepdims=True)
        bias_grad = bias_grad + jnp.sum(drows, 0, keepdims=True)
        dx = norm_back(drows, unit, inv_all.wait(block)[here, 0:1], gain).astype(BF)
        dx_ref[here, :] = dx
        copy = pltpu.make_async_copy(dx_ref.at[here], dx_out.at[here], sems.at[block])
        copy.start()
        pending.append(copy)
        pos_grad = pos_grad + jnp.sum(dx.astype(F32).reshape(CAP_BLOCK, seq_len, width), 0)
    small_ref[0:1] = gain_grad
    small_ref[1:2] = bias_grad
    posg_ref[...] = pos_grad
    seg_ref[...], digits_ref[...], pooled_ref[...] = slot_sums(
        0, slot_cap, seq_len, slots_ref, packed_ref, dx_ref, seg_ref.shape[0] // slot_cap
    )
    for copy in pending:
        copy.wait()


def query_back_body(
    meta_ref, parts_ref, dx1_ref, vec_ref, pos_pick_ref, own_pick_ref, slots_ref,
    seg_ref, digits_ref, pooled_ref, pos_one_ref, small_one_ref, small_two_ref, small_three_ref, x0p, wq,
    dxp_ref, send_ref, wq_ref, rest_ref, smalls_ref,
):
    n_mp = parts_ref.shape[0]
    captions, width = dx1_ref.shape
    n_dp = send_ref.shape[0]
    slots = seg_ref.shape[0]
    slot_cap = slots // n_dp
    lanes = send_ref.shape[2]
    span = width // n_mp
    rank = meta_ref[0]
    dq = parts_ref[0].astype(F32)
    for i in range(1, n_mp):
        dq = dq + parts_ref[i].astype(F32)
    dq = dq.astype(BF)
    gain = vec_ref[0:1]
    unit, inverse = normalize(x0p.value())
    h1 = (unit * gain + vec_ref[1:2]).astype(BF)
    owned = jnp.sum(own_pick_ref[...].astype(F32), -1, keepdims=True)
    dh1 = nn(dq, wq.value()) * owned
    dxp = (dx1_ref[...] * owned + norm_back(dh1, unit, inverse, gain)).astype(BF)
    dxp_ref[...] = dxp
    seq_len = pos_one_ref.shape[0]
    smalls_ref[...] = jnp.zeros_like(smalls_ref)
    smalls_ref[:seq_len] = pos_one_ref[...] + tn(pos_pick_ref[...], dxp)
    at = seq_len
    smalls_ref[at : at + 1] = small_three_ref[0:1] + jnp.sum(dh1 * unit, 0, keepdims=True)
    smalls_ref[at + 1 : at + 2] = small_three_ref[1:2] + jnp.sum(dh1, 0, keepdims=True)
    smalls_ref[at + 2 : at + 5] = small_two_ref[...]
    smalls_ref[at + 5 : at + 7] = small_one_ref[...]
    smalls = smalls_ref[...]
    high = smalls.astype(BF)
    low = (smalls - high.astype(F32)).astype(BF)
    wq_ref[...] = tn(h1, nn(dq, own_columns(rank * span, width, span)).astype(BF)).astype(BF)
    shape = (SMALLS, 2 * SMALLS)
    place = iota2(shape, 1) - iota2(shape, 0)
    rest_ref[...] = tn(high, jnp.where(place == 0, 1.0, 0.0).astype(BF)) + tn(
        low, jnp.where(place == SMALLS, 1.0, 0.0).astype(BF)
    )
    seg = (seg_ref[...] + nn(pooled_ref[...], dxp)).astype(BF)
    most = slots_ref[3:4, :lanes]
    which = iota2((NOTES, lanes), 0)
    most = jnp.where(which == 2, most // NOTE_BASE, most % NOTE_BASE).astype(F32)
    chunk = width // n_dp
    base = (width // lanes) * slot_cap
    for i in range(n_dp):
        for j in range(width // lanes):
            send_ref[i, j * slot_cap : (j + 1) * slot_cap, :] = seg[
                i * slot_cap : (i + 1) * slot_cap, j * lanes : (j + 1) * lanes
            ]
        extra = send_ref.shape[1] - NOTES
        tall = extra - base
        if 4 * tall != chunk:
            send_ref[i, base:extra, :] = jnp.zeros((tall, lanes), BF)
        for k in range(4):
            count = min(tall, chunk - k * tall)
            if count > 0:
                send_ref[i, base : base + count, k * 2 * SMALLS : (k + 1) * 2 * SMALLS] = rest_ref[
                    pl.ds(i * chunk + k * tall, count), :
                ].astype(BF)
        digits = digits_ref[:NOTES, i * slot_cap : (i + 1) * slot_cap]
        note = jnp.concatenate([digits, jnp.zeros((NOTES, lanes - slot_cap), F32)], axis=1)
        send_ref[i, extra:, :] = jnp.where(which < 2, note, most).astype(BF)


def send_body(slot_cap, meta_ref, dx_ref, dxp_ref, slots_ref, packed_ref, send_ref, digits_ref):
    n_dp, _, lanes = send_ref.shape
    width = dx_ref.shape[1]
    seq_len = dx_ref.shape[0] // dxp_ref.shape[0]
    seg, digits_ref[...], pooled = slot_sums(
        meta_ref[0], slot_cap, seq_len, slots_ref, packed_ref, dx_ref, n_dp
    )
    seg = (seg + nn(pooled, dxp_ref[...])).astype(BF)
    for i in range(n_dp):
        for j in range(width // lanes):
            send_ref[i, j * slot_cap : (j + 1) * slot_cap, :] = seg[
                i * slot_cap : (i + 1) * slot_cap, j * lanes : (j + 1) * lanes
            ]


def place_rows(row, got_ref, table_ref, slot_cap, lanes):
    n_dp = got_ref.shape[0]
    shape = (table_ref.shape[0], n_dp * slot_cap)
    hit = jnp.where(iota2(shape, 0) == row, 1.0, 0.0).astype(BF)
    for j in range(table_ref.shape[1] // lanes):
        cut = slice(j * slot_cap, (j + 1) * slot_cap)
        rows = jnp.concatenate([got_ref[i, cut, :] for i in range(n_dp)], axis=0)
        table_ref[:, j * lanes : (j + 1) * lanes] = nn(hit, rows)


def place_body(slot_cap, chunk, meta_ref, got_ref, table_ref, rest_ref, most_ref, row_ref):
    lanes = got_ref.shape[2]
    extra = got_ref.shape[1] - NOTES
    most = jnp.zeros((1, 128), F32)
    for i in range(got_ref.shape[0]):
        note = got_ref[i, extra:, :].astype(F32)
        at = slice(i * slot_cap, (i + 1) * slot_cap)
        row_ref[:, at] = note[0:1, :slot_cap] * float(NOTE_BASE) + note[1:2, :slot_cap] - 1.0
        most = jnp.maximum(most, note[2:3, :128] * float(NOTE_BASE) + note[3:4, :128])
    most_ref[...] = most
    place_rows(row_ref[...].astype(I32), got_ref, table_ref, slot_cap, lanes)
    base = table_ref.shape[1] // lanes * slot_cap
    total = got_ref[0, base:extra, :].astype(F32)
    for i in range(1, got_ref.shape[0]):
        total = total + got_ref[i, base:extra, :].astype(F32)
    for k in range(4):
        count = min(extra - base, chunk - k * (extra - base))
        if count > 0:
            cut = slice(k * 2 * SMALLS, k * 2 * SMALLS + SMALLS)
            low = slice(k * 2 * SMALLS + SMALLS, (k + 1) * 2 * SMALLS)
            at = k * (extra - base)
            rest_ref[at : at + count, :] = total[:count, cut] + total[:count, low]


def place_more_body(meta_ref, row_ref, got_ref, old_ref, table_ref):
    lanes = got_ref.shape[2]
    slot_cap = got_ref.shape[1] // (table_ref.shape[1] // lanes)
    place_rows(row_ref[...], got_ref, table_ref, slot_cap, lanes)
    table_ref[...] += old_ref[...]


def on_device(
    token_ids, lengths, images, table, pos_table, ln1_gain, ln1_bias, w_qkv, w_out, b_out,
    ln2_gain, ln2_bias, w_up, b_up, w_down, b_down, w_head,
):
    n_mp, n_dp = lax.axis_size("mp"), lax.axis_size("dp")
    mp_rank, dp_rank = lax.axis_index("mp"), lax.axis_index("dp")
    captions, seq_len = token_ids.shape
    rows = captions * seq_len
    vocab_part, width = table.shape
    heads = width // HEAD_DIM
    own_width = width // n_mp
    ff = w_up.shape[1]
    owner_rows = vocab_part // n_dp
    slot_cap = -(-rows // (n_dp * n_mp * 16)) * 16
    slots = n_dp * slot_cap
    chunk = width // n_dp
    lanes = own_width + 2 * SMALLS
    n_all = captions * n_dp
    blocks = captions // CAP_BLOCK
    meta = jnp.stack([mp_rank, dp_rank * captions, dp_rank]).astype(I32)

    gather = functools.partial(lax.all_gather, axis_name="mp", axis=0)
    turned = jnp.swapaxes(w_qkv, 1, 2)
    shard = jnp.concatenate([turned, w_out[None]])
    image_f = images.astype(F32)
    image_unit = (
        image_f * lax.rsqrt(jnp.sum(image_f * image_f, -1, keepdims=True) + EPS)
    ).astype(BF)
    all_image = lax.all_gather(image_unit, ("dp", "mp"), axis=0, tiled=True)
    at_row = jnp.arange(8)[:, None]
    vecs = b_up.astype(F32)[None, :]
    for k, vec in enumerate((ln1_gain, ln1_bias, b_out, ln2_gain, ln2_bias, b_down)):
        vecs = jnp.where(at_row == k, vec.astype(F32)[None, :], vecs)

    valid = jnp.arange(seq_len)[None, :] < lengths[:, None]
    end_pick = jnp.arange(seq_len)[None, :] == (lengths - 1)[:, None]
    pos_pick = end_pick.astype(BF)
    local2 = token_ids - mp_rank * vocab_part
    owned2 = jnp.logical_and(local2 >= 0, local2 < vocab_part)
    own_pick = jnp.logical_and(end_pick, owned2).astype(BF)
    local = token_ids.reshape(rows) - mp_rank * vocab_part
    emb = jnp.take(table, jnp.clip(local, 0, vocab_part - 1), axis=0, mode="clip")
    shards = everyone(shard, "mp", emb)
    packed = token_ids + jnp.where(valid, VALID_BIT, 0) + jnp.where(end_pick, END_BIT, 0)
    packed = packed.astype(I32).reshape(1, rows)
    per_head = pltpu.VMEM((heads, captions, width), BF)
    per_head = pltpu.VMEM((heads, captions, width), BF)
    row_buffer = pltpu.VMEM((rows, width), BF)
    dma = pltpu.SemaphoreType.DMA
    wq, wk, wv, wo = (fetch_weight(shards, k) for k in range(4))
    ends, unit_rows, unit, inverse = vmem_call(
        functools.partial(rows_body, vocab_part),
        [
            ((captions, width), BF),
            ((rows, width), BF, False),
            ((rows, width), BF, False),
            ((rows, 128), F32, False),
        ],
        meta,
        [pos_table, vecs, packed],
        [fetch(emb, blocks)],
        [row_buffer, row_buffer, pltpu.VMEM((rows, 128), F32), dma((3 * blocks,))],
        flops=WORK * 6,
    )
    pay, qk, x0p, q = vmem_call(
        functools.partial(attend_body, vocab_part),
        [
            ((captions, width + 128), BF),
            ((heads, captions, width), BF, False),
            ((captions, width), F32, True),
            ((captions, width), BF, True),
        ],
        meta,
        [gather(ends), pos_pick, pos_table, vecs, packed],
        [wq, wk, fetch(unit_rows, blocks), wv],
        [per_head, per_head, dma((n_mp,))],
        flops=WORK * 11,
    )
    ctx, lse, x1, u, part = vmem_call(
        hidden_body,
        [
            ((captions, width), F32, True),
            ((captions, width), F32, True),
            ((captions, width), F32, True),
            ((captions, ff), F32, True),
            ((captions, width), BF),
        ],
        meta,
        [gather(pay), vecs],
        [fetch(x0p), wo, fetch(w_up), fetch(w_down)],
        flops=WORK * 4,
    )
    pooled, proj, powers, sums = vmem_call(
        logits_body,
        [
            ((captions, width), BF, True),
            ((captions, width), F32, True),
            ((captions, n_all), F32, True),
            ((n_dp, 1, n_all + 128), F32),
        ],
        meta,
        [gather(part), vecs],
        [fetch(x1), fetch(w_head), fetch(all_image)],
        flops=WORK * 5,
    )
    all_sums = lax.all_to_all(sums, "dp", 0, 0, tiled=True)
    slot_table = vmem_call(
        functools.partial(slot_body, owner_rows, n_dp),
        [((8, rows), I32)],
        meta,
        [after(packed, sums)],
        flops=WORK * 7,
    )[0]
    loss, dpooled, part, *halves, small_one = vmem_call(
        loss_body,
        [
            ((1, 128), F32),
            ((captions, width), F32),
            ((captions, width), BF),
            *[((n_dp // 2, chunk, ff + own_width), BF)] * 2,
            *[((n_dp // 2, chunk, ff), BF)] * 2,
            ((2, width), F32),
        ],
        meta,
        [after(all_sums, slot_table), vecs],
        [
            fetch(powers), fetch(all_image), fetch(proj), fetch(w_head), fetch(u), fetch(w_down),
            fetch(w_up), fetch(x1), fetch(pooled),
        ],
        [pltpu.VMEM((width, ff + own_width), F32), pltpu.VMEM((width, ff), F32)],
        flops=WORK * 8,
    )
    dp_bits, mp_bits = bits_of("dp"), bits_of("mp")

    def next_half(total, bits):
        total = halve(total, "dp", bits, bits[0])
        bits.pop(0)
        return total

    one_step = len(dp_bits) == 1
    down = exchange_half(*halves[:2], "dp", DOWN_BIT, one_step)
    up = exchange_half(*halves[2:], "dp", UP_BIT, one_step)
    down_bits = [bit for bit in dp_bits if bit != DOWN_BIT]
    up_bits = [bit for bit in dp_bits if bit != UP_BIT]
    parts = gather(part)
    dx1, dq_part, wout, wkv_kept, wkv_sent, a, probs, dscores, small_two = vmem_call(
        functools.partial(attend_back_body, vocab_part),
        [
            ((captions, width), F32),
            ((captions, width), BF),
            ((width, own_width), BF),
            *[((n_mp // 2, width, 2 * own_width), BF)] * 2,
            ((heads, captions, width), BF),
            ((blocks, heads * CAP_BLOCK, CAP_BLOCK * seq_len), BF),
            ((blocks, heads * CAP_BLOCK, CAP_BLOCK * seq_len), BF),
            ((3, width), F32),
        ],
        meta,
        [parts, packed, vecs, dpooled],
        [
            fetch(x1), fetch(ctx), wo, wv, fetch(lse), fetch(qk, blocks, 1),
            fetch(unit_rows, blocks), wk, fetch(q),
        ],
        [per_head, per_head, pltpu.VMEM((n_mp, width, 2 * own_width), BF)],
        flops=WORK * 13,
    )
    wkv = exchange_half(wkv_kept, wkv_sent, "mp", 1, len(mp_bits) == 1)
    dq_parts = gather(dq_part)
    dx, pos_one, small_three, seg, digits, pooled_slots = vmem_call(
        functools.partial(rows_back_body, slot_cap),
        [
            ((rows, width), BF, False),
            ((seq_len, width), F32),
            ((2, width), F32),
            ((slots, width), F32),
            ((16, slots), F32),
            ((slots, captions), BF),
        ],
        meta,
        [after(probs, dq_parts, wkv), dscores, a, vecs, slot_table, packed],
        [fetch(qk, blocks, 1), fetch(unit, blocks), fetch(inverse, blocks)],
        [row_buffer, dma((blocks,))],
        flops=WORK * 12,
    )
    for k in range(1, len(mp_bits)):
        wkv = halve(wkv, "mp", mp_bits[k:], mp_bits[k])
    down, up = next_half(down, down_bits), next_half(up, up_bits)
    rest_rows = -(-chunk // 32) * 8
    send_rows = width // lanes * slot_cap
    dxp, send, wq_grad = vmem_call(
        query_back_body,
        [
            ((captions, width), BF),
            ((n_dp, send_rows + rest_rows + NOTES, lanes), BF),
            ((width, own_width), BF),
        ],
        meta,
        [
            dq_parts, dx1, vecs, pos_pick, own_pick, slot_table, seg, digits, pooled_slots, pos_one,
            small_one, small_two, small_three,
        ],
        [fetch(x0p), wq],
        [pltpu.VMEM((width, 2 * SMALLS), F32), pltpu.VMEM((SMALLS, width), F32)],
        flops=WORK * 4,
    )
    got = lax.all_to_all(send, "dp", 0, 0, tiled=True)
    wkvo = jnp.concatenate([wkv[0].astype(BF), wout, wq_grad], 1)
    wkvo = wkvo.reshape(n_dp, chunk, 4 * own_width)
    bits = list(dp_bits)
    wkvo = next_half(wkvo, bits)
    while down_bits:
        down = next_half(down, down_bits)
    while up_bits:
        up = next_half(up, up_bits)
    down, up = down[0], up[0]
    table_grad, rest, most_all = vmem_call(
        functools.partial(place_body, slot_cap, chunk),
        [((owner_rows, width), F32), ((chunk, SMALLS), F32), ((1, 128), F32)],
        meta,
        [got],
        (),
        [pltpu.VMEM((1, slots), F32)],
        flops=WORK * 3,
    )
    most_all = most_all[0, 0].astype(I32)
    small = rest
    last = gather(jnp.concatenate([down[:, ff:], small, jnp.zeros_like(small)], 1))
    while bits:
        wkvo = next_half(wkvo if len(bits) > 1 else after(wkvo, last), bits)
    wkvo = wkvo[0]

    def another(carry):
        turn, total = carry
        sent, digits = vmem_call(
            functools.partial(send_body, slot_cap),
            [((n_dp, send_rows, lanes), BF), ((16, slots), F32)],
            turn.reshape(1),
            [dx, dxp, slot_table, packed],
        )
        row = (digits[0] * NOTE_BASE + digits[1] - 1.0).astype(I32)
        row = lax.all_to_all(row.reshape(n_dp, slot_cap), "dp", 0, 0, tiled=True)
        sent = lax.all_to_all(sent, "dp", 0, 0, tiled=True)
        total = vmem_call(
            place_more_body,
            [((owner_rows, width), F32)],
            meta,
            [row.reshape(1, slots), sent, total],
        )[0]
        return turn + 1, total

    _, table_grad = lax.while_loop(
        lambda carry: carry[0] * slot_cap < most_all, another, (jnp.int32(1), table_grad)
    )
    w_head_grad = jnp.swapaxes(last[:, :, :own_width], 0, 1).reshape(chunk, width)
    shared = jnp.sum(last[:, :, own_width : own_width + SMALLS], 0)
    qkv_grad = jnp.stack(
        [wkvo[:, k * own_width : (k + 1) * own_width] for k in (3, 0, 1)]
    )
    return (
        loss[0, 0],
        table_grad,
        shared[:, :seq_len].T,
        shared[:, seq_len],
        shared[:, seq_len + 1],
        qkv_grad,
        wkvo[:, 2 * own_width : 3 * own_width].T,
        small[:, seq_len + 4],
        small[:, seq_len + 2],
        small[:, seq_len + 3],
        up,
        small[:, seq_len + 6],
        down[:, :ff].T,
        small[:, seq_len + 5],
        w_head_grad,
    )


def solution(mesh):
    placed = (
        P("dp", None),
        P("dp"),
        P(("dp", "mp"), None),
        P("mp", None),
        P(),
        P(),
        P(),
        P(None, None, "mp"),
        P("mp", None),
        P(),
        P(),
        P(),
        P(None, "mp"),
        P("mp"),
        P("mp", None),
        P(),
        P(),
    )
    return jax.shard_map(
        on_device,
        mesh=mesh,
        in_specs=placed,
        out_specs=(
            P(),
            P(("mp", "dp"), None),
            P(None, "dp"),
            P("dp"),
            P("dp"),
            P(None, "dp", "mp"),
            P("mp", "dp"),
            P("dp"),
            P("dp"),
            P("dp"),
            P("dp", "mp"),
            P(("mp", "dp")),
            P("mp", "dp"),
            P("dp"),
            P("dp", None),
        ),
        check_vma=False,
    )
```

```python
import functools
import math

import jax
import jax.numpy as jnp
from jax import lax
from jax.experimental import pallas as pl
from jax.experimental.pallas import tpu as pltpu
from jax.sharding import PartitionSpec as P

HEAD_DIM = 64
LOGIT_SCALE = 50.0
EPS = 1e-06
MASK_FILL = -1000000000.0
NO_KEY = -1e30
BF = jnp.bfloat16
F32 = jnp.float32
I32 = jnp.int32
GELU_C = math.sqrt(2.0 / math.pi)
CAP_BLOCK = 16
SMALLS = 32
NOTES = 8
VALID_BIT = 1 << 20
END_BIT = 1 << 21
NOTE_BASE = 32
WORK = 920000000
DOWN_BIT = 1
UP_BIT = 2


def nn(a, b):
    return lax.dot_general(a, b, (((1,), (0,)), ((), ())), preferred_element_type=F32)


def nt(a, b):
    return lax.dot_general(a, b, (((1,), (1,)), ((), ())), preferred_element_type=F32)


def tn(a, b):
    return lax.dot_general(a, b, (((0,), (0,)), ((), ())), preferred_element_type=F32)


def normalize(rows):
    centred = rows - jnp.mean(rows, -1, keepdims=True)
    inverse = lax.rsqrt(jnp.mean(centred * centred, -1, keepdims=True) + EPS)
    return centred * inverse, inverse


def norm_back(upstream, unit, inverse, gain):
    scaled = upstream * gain
    mean_scaled = jnp.mean(scaled, -1, keepdims=True)
    mean_unit = jnp.mean(scaled * unit, -1, keepdims=True)
    return inverse * (scaled - mean_scaled - unit * mean_unit)


def iota2(shape, dim):
    return lax.broadcasted_iota(I32, shape, dim)


class Late:
    def __init__(self, ref, pairs, sems):
        self.ref = ref
        self.copies = [
            pltpu.make_async_copy(src, dst, sem) for (src, dst), sem in zip(pairs, sems)
        ]
        self.waiting = set(range(len(self.copies)))

    def start(self):
        for copy in self.copies:
            copy.start()

    def wait(self, part=None):
        for k in sorted(self.waiting) if part is None else [part]:
            if k in self.waiting:
                self.copies[k].wait()
                self.waiting.discard(k)
        return self.ref

    def value(self):
        return self.wait()[...]


def fetch(array, parts=1, axis=0):
    return ("blocks", [array], parts, axis)


def fetch_weight(shards, which):
    return ("weight", list(shards), which, 0)


def vmem_call(body, outs, meta, args, late=(), scratch=(), flops=1, mib=40):
    vmem = pl.BlockSpec(memory_space=pltpu.VMEM)
    hbm = pl.BlockSpec(memory_space=pltpu.HBM)
    sources, buffers, counts = [], [], []
    for kind, arrays, parts, axis in late:
        sources += arrays
        if kind == "weight":
            _, rows, width = arrays[0].shape
            buffers.append(pltpu.VMEM((rows * len(arrays), width), arrays[0].dtype))
            counts.append(len(arrays))
        else:
            buffers.append(pltpu.VMEM(arrays[0].shape, arrays[0].dtype))
            counts.append(parts)

    staged = [k for k, o in enumerate(outs) if len(o) > 2 and o[2]]

    def kernel(meta_ref, *refs):
        arg_refs, refs = refs[: len(args)], refs[len(args) :]
        source_refs, refs = refs[: len(sources)], refs[len(sources) :]
        out_refs, refs = refs[: len(outs)], refs[len(outs) :]
        buffer_refs, refs = refs[: len(buffers)], refs[len(buffers) :]
        sems, stage_sems, refs = refs[0], refs[1], refs[2:]
        stages, refs = refs[: len(staged)], refs[len(staged) :]
        targets = list(out_refs)
        for k, stage in zip(staged, stages):
            targets[k] = stage
        handles, at, place = [], 0, 0
        for (kind, arrays, parts, axis), buffer in zip(late, buffer_refs):
            if kind == "weight":
                rows = arrays[0].shape[1]
                pairs = []
                for k in range(len(arrays)):
                    low = pl.multiple_of((meta_ref[0] ^ k) * rows, rows)
                    pairs.append((source_refs[place + k].at[parts], buffer.at[pl.ds(low, rows)]))
                place += len(arrays)
            else:
                size = arrays[0].shape[axis] // parts
                pairs = []
                for k in range(parts):
                    cut = (slice(None),) * axis + (pl.ds(k * size, size),)
                    pairs.append((source_refs[place].at[cut], buffer.at[cut]))
                place += 1
            handles.append(Late(buffer, pairs, [sems.at[at + k] for k in range(len(pairs))]))
            at += len(pairs)
        for handle in handles:
            handle.start()
        body(meta_ref, *arg_refs, *handles, *targets, *refs)
        copies = [
            pltpu.make_async_copy(stage, out_refs[k], stage_sems.at[i])
            for i, (k, stage) in enumerate(zip(staged, stages))
        ]
        for copy in copies:
            copy.start()
        for handle in handles:
            handle.wait()
        for copy in copies:
            copy.wait()

    return pl.pallas_call(
        kernel,
        out_shape=[
            pltpu.HBM(*o[:2]) if len(o) > 2 else jax.ShapeDtypeStruct(*o) for o in outs
        ],
        in_specs=[pl.BlockSpec(memory_space=pltpu.SMEM)]
        + [vmem] * len(args)
        + [hbm] * len(sources),
        out_specs=[hbm if len(o) > 2 else vmem for o in outs],
        scratch_shapes=[
            *buffers,
            pltpu.SemaphoreType.DMA((max(1, sum(counts)),)),
            pltpu.SemaphoreType.DMA((max(1, len(staged)),)),
            *(pltpu.VMEM(*outs[k][:2]) for k in staged),
            *scratch,
        ],
        compiler_params=pltpu.CompilerParams(vmem_limit_bytes=mib << 20),
        cost_estimate=pl.CostEstimate(flops=flops, bytes_accessed=1, transcendentals=0),
    )(meta, *args, *(pltpu.with_memory_space_constraint(x, pltpu.HBM) for x in sources))


def exchange_half(kept, sent, axis, bit, last):
    count = lax.axis_size(axis)
    got = lax.ppermute(sent, axis, [(i, i ^ bit) for i in range(count)])
    total = kept.astype(F32) + got.astype(F32)
    return total if last else total.astype(BF)


def halve(total, axis, bits, bit):
    low = 1 << bits.index(bit)
    pairs = total.reshape((total.shape[0] // (2 * low), 2, low) + total.shape[1:])
    shape = (total.shape[0] // 2,) + total.shape[1:]
    mine = (lax.axis_index(axis) // bit) % 2
    sent = lax.dynamic_index_in_dim(pairs, 1 - mine, 1, keepdims=False).reshape(shape)
    kept = lax.dynamic_index_in_dim(pairs, mine, 1, keepdims=False).reshape(shape)
    return exchange_half(kept, sent, axis, bit, len(bits) == 1)


def split_blocks(blocks, bit, mine, kept_ref, sent_ref):
    place = 0
    for i in range(len(blocks)):
        if i & bit == 0:
            first, second = blocks[i](), blocks[i | bit]()
            kept_ref[place] = jnp.where(mine == 0, first, second).astype(BF)
            sent_ref[place] = jnp.where(mine == 0, second, first).astype(BF)
            place += 1


def bits_of(axis):
    count = lax.axis_size(axis)
    return [1 << k for k in range(count.bit_length() - 1)]


def after(x, *others):
    return lax.optimization_barrier((x, others))[0]


def everyone(x, axis, before):
    count = lax.axis_size(axis)
    have = {0: x}
    bit = count // 2
    while bit:
        pairs = [(i, i ^ bit) for i in range(count)]
        for k, v in list(have.items()):
            have[k | bit] = lax.ppermute(after(v, before) if k else v, axis, pairs)
        bit //= 2
    return [have[k] for k in range(count)]


def own_columns(start, width, own_width):
    shape = (width, own_width)
    hit = iota2(shape, 0) == start + iota2(shape, 1)
    return jnp.where(hit, 1.0, 0.0).astype(BF)


def unpack(packed):
    return packed % VALID_BIT, packed // VALID_BIT % 2 > 0, packed // END_BIT > 0


def own_code(packed, rank, vocab_part):
    ids, valid, _ = unpack(packed)
    return jnp.where(ids // vocab_part == rank, jnp.where(valid, 2, 1), 0)


def head_mask(captions, span):
    shape = (span // HEAD_DIM * captions, span)
    return (iota2(shape, 0) // captions) == (iota2(shape, 1) // HEAD_DIM)


def spread_heads(rows, group, mask):
    span = mask.shape[1]
    part = rows[:, group * span : (group + 1) * span].astype(F32)
    tall = jnp.concatenate([part] * (span // HEAD_DIM), axis=0)
    return jnp.where(mask, tall, 0.0).astype(BF)


def fold_heads(tall, captions, mask):
    kept = jnp.where(mask, tall, 0.0)
    total = kept[:captions]
    for h in range(1, tall.shape[0] // captions):
        total = total + kept[h * captions : (h + 1) * captions]
    return total


def same_caption(heads, seq_len):
    shape = (heads * CAP_BLOCK, CAP_BLOCK * seq_len)
    return (iota2(shape, 0) % CAP_BLOCK) == (iota2(shape, 1) // seq_len)


def rows_body(
    vocab_part, meta_ref, pos_ref, vec_ref, packed_ref, emb,
    end_ref, rows_out, unit_out, inv_out, rows_ref, unit_ref, inv_ref, sems,
):
    captions = end_ref.shape[0]
    seq_len = pos_ref.shape[0]
    block_rows = CAP_BLOCK * seq_len
    gain, bias = vec_ref[0:1], vec_ref[1:2]
    pos = jnp.concatenate([pos_ref[...].astype(F32)] * CAP_BLOCK, axis=0)
    pending = []

    def write_back(src, dst):
        copy = pltpu.make_async_copy(src, dst, sems.at[len(pending)])
        copy.start()
        pending.append(copy)

    for block in range(captions // CAP_BLOCK):
        here = pl.ds(block * block_rows, block_rows)
        packed = packed_ref[:, block * block_rows : (block + 1) * block_rows]
        low = emb.wait(block)[here, :]
        ids, _, is_end = unpack(packed)
        shape = (CAP_BLOCK, block_rows)
        mark = jnp.logical_and(is_end, ids // vocab_part == meta_ref[0])
        mark = jnp.logical_and(iota2(shape, 0) == iota2(shape, 1) // seq_len, mark)
        ends = nn(jnp.where(mark, 1.0, 0.0).astype(BF), low)
        end_ref[block * CAP_BLOCK : (block + 1) * CAP_BLOCK] = ends.astype(BF)
        unit, inverse = normalize(low.astype(F32) + pos)
        unit_ref[here, :] = unit.astype(BF)
        write_back(unit_ref.at[here], unit_out.at[here])
        inv_ref[here, :] = jnp.broadcast_to(inverse, (block_rows, 128))
        write_back(inv_ref.at[here], inv_out.at[here])
        rows_ref[here, :] = (unit * gain + bias).astype(BF)
        write_back(rows_ref.at[here], rows_out.at[here])
    for copy in pending:
        copy.wait()


def attend_body(
    vocab_part, meta_ref, ends_ref, pos_pick_ref, pos_ref, vec_ref, packed_ref, wq, wk, rows_all, wv,
    pay_ref, qk_out, x0p_ref, q_ref, qk_ref, t_ref, sems,
):
    n_mp = ends_ref.shape[0]
    captions, width = x0p_ref.shape
    heads = width // HEAD_DIM
    span = width // n_mp
    per_group = span // HEAD_DIM
    seq_len = pos_ref.shape[0]
    block_rows = CAP_BLOCK * seq_len
    gain, bias = vec_ref[0:1], vec_ref[1:2]
    pooled_in = nn(pos_pick_ref[...], pos_ref[...])
    for i in range(n_mp):
        pooled_in = pooled_in + ends_ref[i].astype(F32)
    pending = []
    x0p_ref[...] = pooled_in
    unit, _ = normalize(pooled_in)
    q = nt((unit * gain + bias).astype(BF), wq.value()).astype(BF)
    q_ref[...] = q
    mask = head_mask(captions, span)
    scale = 1.0 / math.sqrt(HEAD_DIM)
    wk_ref = wk.wait()
    for g in range(n_mp):
        some = slice(g * per_group, (g + 1) * per_group)
        tall = nn(spread_heads(q, g, mask), wk_ref[g * span : (g + 1) * span]) * scale
        qk_ref[some] = tall.astype(BF).reshape(per_group, captions, width)
        copy = pltpu.make_async_copy(qk_ref.at[some], qk_out.at[some], sems.at[g])
        copy.start()
        pending.append(copy)
    lane = iota2((heads, CAP_BLOCK, 128), 2)
    head_of = iota2((heads, CAP_BLOCK, 128), 0)
    rows_ref = rows_all.wait()
    blocks = range(captions // CAP_BLOCK)
    cuts = [pl.ds(block * block_rows, block_rows) for block in blocks]
    caps = [pl.ds(block * CAP_BLOCK, CAP_BLOCK) for block in blocks]
    raw = [
        nt(qk_ref[:, caps[block], :].reshape(heads * CAP_BLOCK, width), rows_ref[cuts[block], :])
        for block in blocks
    ]
    same = same_caption(heads, seq_len)
    code = own_code(packed_ref[...], meta_ref[0], vocab_part)
    log_totals, weights = [], []
    for block in blocks:
        here = code[:, block * block_rows : (block + 1) * block_rows]
        own = jnp.logical_and(same, here > 0)
        scores = jnp.where(own, jnp.where(here > 1, raw[block], MASK_FILL), NO_KEY)
        top = jnp.max(scores, -1, keepdims=True)
        power = jnp.where(own, jnp.exp(scores - top), 0.0)
        total = jnp.sum(power, -1, keepdims=True)
        some = total > 0.0
        total = jnp.where(some, total, 1.0)
        log_totals.append(jnp.where(some, top + jnp.log(total), NO_KEY))
        weights.append((power * (1.0 / total)).astype(BF))
    for block in blocks:
        mixed = nn(weights[block], rows_ref[cuts[block], :])
        t_ref[:, caps[block], :] = mixed.astype(BF).reshape(heads, CAP_BLOCK, width)
    for block in blocks:
        log_total = log_totals[block]
        first = log_total.astype(BF).astype(F32)
        second = (log_total - first).astype(BF).astype(F32)
        third = log_total - first - second
        stat = jnp.zeros((heads, CAP_BLOCK, 128), F32)
        for k, piece in enumerate((first, second, third)):
            stat = stat + jnp.where(
                lane == head_of + 16 * k, piece.reshape(heads, CAP_BLOCK, 1), 0.0
            )
        pay_ref[caps[block], width:] = jnp.sum(stat, 0).astype(BF)
    wv_ref = wv.wait()
    for g in range(n_mp):
        tall = t_ref[g * per_group : (g + 1) * per_group].reshape(per_group * captions, width)
        piece = nt(tall, wv_ref[g * span : (g + 1) * span])
        pay_ref[:, g * span : (g + 1) * span] = fold_heads(piece, captions, mask).astype(BF)
    for copy in pending:
        copy.wait()


def hidden_body(
    meta_ref, pay_ref, vec_ref, x0p, wo, wup, wdown,
    ctx_ref, lse_ref, x1_ref, u_ref, part_ref,
):
    n_mp = pay_ref.shape[0]
    captions, width = ctx_ref.shape
    shape = (128, width)
    stat_row, head = iota2(shape, 0), iota2(shape, 1) // HEAD_DIM
    picks = jnp.logical_and(stat_row % 16 == head, stat_row < 48)
    expand = jnp.where(picks, 1.0, 0.0).astype(BF)
    logs = [nn(pay_ref[i, :, width:], expand) for i in range(n_mp)]
    top = functools.reduce(jnp.maximum, logs)
    total = jnp.zeros_like(top)
    ctx = jnp.zeros_like(top)
    for i in range(n_mp):
        weight = jnp.exp(logs[i] - top)
        total = total + weight
        ctx = ctx + weight * pay_ref[i, :, :width].astype(F32)
    ctx = ctx / total
    ctx_ref[...] = ctx
    lse_ref[...] = top + jnp.log(total)
    x1 = x0p.value() + nn(ctx.astype(BF), wo.value()) + vec_ref[2:3]
    x1_ref[...] = x1
    unit, _ = normalize(x1)
    h2 = (unit * vec_ref[3:4] + vec_ref[4:5]).astype(BF)
    u = nn(h2, wup.value()) + vec_ref[6:7]
    u_ref[...] = u
    hidden = (0.5 * u * (1.0 + jnp.tanh(GELU_C * (u + 0.044715 * u * u * u)))).astype(BF)
    part_ref[...] = nn(hidden, wdown.value()).astype(BF)


def logits_body(
    meta_ref, parts_ref, vec_ref, x1, wh, images,
    pooled_ref, proj_ref, e_ref, sums_ref,
):
    x2 = x1.value() + vec_ref[5:6]
    for i in range(parts_ref.shape[0]):
        x2 = x2 + parts_ref[i].astype(F32)
    pooled = x2.astype(BF)
    pooled_ref[...] = pooled
    proj = nn(pooled, wh.value())
    proj_ref[...] = proj
    text = (proj * lax.rsqrt(jnp.sum(proj * proj, -1, keepdims=True) + EPS)).astype(BF)
    logits = LOGIT_SCALE * nt(text, images.value())
    powers = jnp.exp(logits)
    e_ref[...] = powers
    n_all = powers.shape[1]
    is_diag = iota2(logits.shape, 1) == meta_ref[1] + iota2(logits.shape, 0)
    rows = jnp.log(jnp.sum(powers, -1, keepdims=True))
    rows = rows - 2.0 * jnp.sum(jnp.where(is_diag, logits, 0.0), -1, keepdims=True)
    cols = jnp.sum(powers, 0, keepdims=True)
    rows = jnp.broadcast_to(jnp.sum(rows, 0, keepdims=True), (1, 128))
    for i in range(sums_ref.shape[0]):
        sums_ref[i, :, :n_all] = cols
        sums_ref[i, :, n_all:] = rows


def loss_body(
    meta_ref, sums_ref, vec_ref, e, images, proj, wh, u, wdown, wup, x1, pooled,
    loss_ref, dpooled_ref, part_ref, down_kept, down_sent, up_kept, up_sent, small_ref,
    down_ref, up_ref,
):
    width = dpooled_ref.shape[1]
    sums = jnp.sum(sums_ref[...], 0)
    n_all = sums.shape[1] - 128
    cols = sums[:, :n_all]
    loss = jnp.sum(jnp.log(cols), -1, keepdims=True) + sums[:, n_all : n_all + 1]
    loss_ref[...] = jnp.broadcast_to(loss * (0.5 / n_all), (1, 128))
    powers = e.value()
    row_inv = 1.0 / jnp.sum(powers, -1, keepdims=True)
    is_diag = iota2(powers.shape, 1) == meta_ref[1] + iota2(powers.shape, 0)
    grad = powers * row_inv + powers * (1.0 / cols) - jnp.where(is_diag, 2.0, 0.0)
    grad = (grad * (0.5 / n_all)).astype(BF)
    dtext = LOGIT_SCALE * nn(grad, images.value())
    proj = proj.value()
    inv = lax.rsqrt(jnp.sum(proj * proj, -1, keepdims=True) + EPS)
    along = jnp.sum(proj * dtext, -1, keepdims=True)
    dproj = (inv * dtext - inv * inv * inv * proj * along).astype(BF)
    dpooled = nt(dproj, wh.value())
    dpooled_ref[...] = dpooled
    dy = dpooled.astype(BF)
    u = u.value()
    th = jnp.tanh(GELU_C * (u + 0.044715 * u * u * u))
    slope = 0.5 * (1.0 + th) + 0.5 * u * (1.0 - th * th) * (
        GELU_C * (1.0 + 3.0 * 0.044715 * u * u)
    )
    du = (nt(dy, wdown.value()) * slope).astype(BF)
    part_ref[...] = nt(du, wup.value()).astype(BF)
    hidden = (0.5 * u * (1.0 + th)).astype(BF)
    unit, _ = normalize(x1.value())
    h2 = (unit * vec_ref[3:4] + vec_ref[4:5]).astype(BF)
    ff = u.shape[1]
    own_width = down_ref.shape[1] - ff
    pick = own_columns(meta_ref[0] * own_width, width, own_width)
    down_ref[:, :ff] = tn(dy, hidden)
    up_ref[...] = tn(h2, du)
    down_ref[:, ff:] = tn(pooled.value(), nn(dproj, pick).astype(BF))
    chunk = down_kept.shape[1]
    n_dp = 2 * down_kept.shape[0]
    for ref, bit, kept, sent in (
        (down_ref, DOWN_BIT, down_kept, down_sent),
        (up_ref, UP_BIT, up_kept, up_sent),
    ):
        blocks = [
            functools.partial(lambda ref, i: ref[pl.ds(i * chunk, chunk), :], ref, i)
            for i in range(n_dp)
        ]
        split_blocks(blocks, bit, meta_ref[2] // bit % 2, kept, sent)
    small_ref[0:1] = jnp.sum(dy.astype(F32), 0, keepdims=True)
    small_ref[1:2] = jnp.sum(du.astype(F32), 0, keepdims=True)


def attend_back_body(
    vocab_part, meta_ref, parts_ref, packed_ref, vec_ref, dpooled_ref, x1, ctx, wo, wv, lse, qk_all, rows_all, wk, q,
    dx1_ref, wout_ref, kept_ref, sent_one, sent_two, a_ref, probs_ref, ds_ref, small_ref,
    t_ref, s_ref, wkv_ref, dq_ref,
):
    n_mp = wkv_ref.shape[0]
    captions, width = dpooled_ref.shape
    heads = width // HEAD_DIM
    span = width // n_mp
    per_group = span // HEAD_DIM
    block_rows = rows_all.ref.shape[0] // (captions // CAP_BLOCK)
    seq_len = block_rows // CAP_BLOCK
    rank = meta_ref[0]
    dh2 = parts_ref[0].astype(F32)
    for i in range(1, parts_ref.shape[0]):
        dh2 = dh2 + parts_ref[i].astype(F32)
    unit2, inv2 = normalize(x1.value())
    small_ref[0:1] = jnp.sum(dh2 * unit2, 0, keepdims=True)
    small_ref[1:2] = jnp.sum(dh2, 0, keepdims=True)
    dx1 = dpooled_ref[...] + norm_back(dh2, unit2, inv2, vec_ref[3:4])
    dx1_ref[...] = dx1
    da = dx1.astype(BF)
    small_ref[2:3] = jnp.sum(da.astype(F32), 0, keepdims=True)
    ctx = ctx.value()
    pick = own_columns(rank * span, width, span)
    wout_ref[...] = tn(da, nn(ctx.astype(BF), pick).astype(BF)).astype(BF)
    dctx = nt(da, wo.value()).astype(BF)
    mask = head_mask(captions, span)
    wv_ref = wv.wait()
    for g in range(n_mp):
        tall = nn(spread_heads(dctx, g, mask), wv_ref[g * span : (g + 1) * span])
        a_ref[g * per_group : (g + 1) * per_group] = tall.astype(BF).reshape(
            per_group, captions, width
        )
    prod = dctx.astype(F32) * ctx
    lse = lse.value()
    scale = 1.0 / math.sqrt(HEAD_DIM)
    tall_shape = (heads * CAP_BLOCK, width)
    of_head = (iota2(tall_shape, 0) // CAP_BLOCK) == (iota2(tall_shape, 1) // HEAD_DIM)
    at_head = (iota2(tall_shape, 0) // CAP_BLOCK) * HEAD_DIM == iota2(tall_shape, 1)
    rows_ref, qk_ref = rows_all.wait(), qk_all.wait()
    same = same_caption(heads, seq_len)
    code = own_code(packed_ref[...], rank, vocab_part)
    tall = (heads * CAP_BLOCK, width)
    blocks = range(captions // CAP_BLOCK)
    cuts = [pl.ds(block * block_rows, block_rows) for block in blocks]
    caps = [pl.ds(block * CAP_BLOCK, CAP_BLOCK) for block in blocks]
    raw = [nt(qk_ref[:, caps[block], :].reshape(tall), rows_ref[cuts[block], :]) for block in blocks]
    pulled = [nt(a_ref[:, caps[block], :].reshape(tall), rows_ref[cuts[block], :]) for block in blocks]
    probs_all, ds_all = [], []
    for block in blocks:
        low = block * CAP_BLOCK
        here = code[:, block * block_rows : (block + 1) * block_rows]
        own = jnp.logical_and(same, here > 0)
        scores = jnp.where(here > 1, raw[block], MASK_FILL)
        spread = jnp.concatenate([lse[low : low + CAP_BLOCK]] * heads, axis=0)
        log_total = jnp.sum(jnp.where(at_head, spread, 0.0), -1, keepdims=True)
        spread = jnp.concatenate([prod[low : low + CAP_BLOCK]] * heads, axis=0)
        row_sum = jnp.sum(jnp.where(of_head, spread, 0.0), -1, keepdims=True)
        probs = jnp.where(own, jnp.exp(scores - log_total), 0.0)
        dscores = (probs * (pulled[block] - row_sum)).astype(BF)
        probs = probs.astype(BF)
        probs_ref[block] = probs
        ds_ref[block] = dscores
        probs_all.append(probs)
        ds_all.append(dscores)
    for block in blocks:
        rows = rows_ref[cuts[block], :]
        t_ref[:, caps[block], :] = (
            nn(probs_all[block], rows).astype(BF).reshape(heads, CAP_BLOCK, width)
        )
        s_ref[:, caps[block], :] = (
            (nn(ds_all[block], rows) * scale).astype(BF).reshape(heads, CAP_BLOCK, width)
        )
    q = q.value()
    wk_ref = wk.wait()
    for g in range(n_mp):
        some = slice(g * per_group, (g + 1) * per_group)
        tall = s_ref[some].reshape(per_group * captions, width)
        piece = nt(tall, wk_ref[g * span : (g + 1) * span])
        dq_ref[:, g * span : (g + 1) * span] = fold_heads(piece, captions, mask).astype(BF)
        wkv_ref[g, :, :span] = tn(tall, spread_heads(q, g, mask)).astype(BF)
        tall = t_ref[some].reshape(per_group * captions, width)
        wkv_ref[g, :, span:] = tn(tall, spread_heads(dctx, g, mask)).astype(BF)
    half = sent_one.shape[0]

    def put(low, piece):
        inside = min(max(half - low, 0), piece.shape[0])
        if inside > 0:
            sent_one[low : low + inside] = piece[:inside]
        if inside < piece.shape[0]:
            sent_two[low + inside - half : low + piece.shape[0] - half] = piece[inside:]

    for g in range(0, n_mp, 2):
        at = slice(g // 2 * width, (g // 2 + 1) * width)
        first, second = wkv_ref[g], wkv_ref[g + 1]
        kept_ref[at] = jnp.where(rank % 2 == 0, first, second)
        put(g // 2 * width, jnp.where(rank % 2 == 0, second, first))
    for k in range(n_mp // 2):
        at = slice(n_mp // 2 * width + k * captions, n_mp // 2 * width + (k + 1) * captions)
        piece = dq_ref[:, 2 * k * span : 2 * (k + 1) * span]
        kept_ref[at] = piece
        put(n_mp // 2 * width + k * captions, piece)


def between_body(meta_ref, kept_ref, got_one, got_two, kept_out, sent_out):
    block = kept_ref.shape[0] - kept_out.shape[0]
    half = got_one.shape[0]

    def total(low, high):
        parts = []
        if low < half:
            parts.append(got_one[low : min(high, half)])
        if high > half:
            parts.append(got_two[max(low, half) - half : high - half])
        got = parts[0] if len(parts) == 1 else jnp.concatenate(parts, axis=0)
        return kept_ref[low:high].astype(F32) + got.astype(F32)

    first, second = total(0, block), total(block, 2 * block)
    both = total(2 * block, kept_ref.shape[0]).astype(BF)
    upper = meta_ref[0] // 2 % 2
    kept_out[:block] = jnp.where(upper == 0, first, second).astype(BF)
    sent_out[:block] = jnp.where(upper == 0, second, first).astype(BF)
    kept_out[block:] = both
    sent_out[block:] = both


def slot_body(owner_rows, n_dp, meta_ref, packed_ref, out_ref):
    rows = packed_ref.shape[1]
    side = 128
    ids, _, _ = unpack(packed_ref[...])
    owner = ids // owner_rows
    order = iota2((1, rows), 1)

    def columns(row, k):
        piece = row[:, k * side : (k + 1) * side].astype(F32)
        return jnp.transpose(jnp.broadcast_to(piece, (side, side))).astype(I32)

    def tall(column):
        return jnp.concatenate([column] * (rows // side), axis=1)

    first_at = jnp.full((1, rows), rows, I32)
    for k in range(rows // side):
        there = k * side + iota2((side, rows), 0)
        hit = jnp.where(tall(columns(ids, k)) == ids, there, rows)
        first_at = jnp.minimum(first_at, jnp.min(hit, 0, keepdims=True))
    is_first = first_at == order
    first_owner = jnp.where(is_first, owner, -1)
    slot = jnp.zeros((1, rows), I32)
    for k in range(rows // side):
        there = k * side + iota2((side, rows), 0)
        ahead = jnp.logical_and(tall(columns(first_owner, k)) == owner, there < first_at)
        slot = slot + jnp.sum(jnp.where(ahead, 1, 0), 0, keepdims=True)
    here = owner - meta_ref[0] * n_dp
    dest = jnp.where(jnp.logical_and(here >= 0, here < n_dp), here, -1)
    most = jnp.max(slot.astype(F32), 1, keepdims=True).astype(I32) + 1
    out_ref[0:1] = slot
    out_ref[1:2] = dest
    out_ref[2:3] = jnp.where(is_first, ids % owner_rows + 1, 0)
    out_ref[3:4] = jnp.broadcast_to(most, (1, rows))
    out_ref[4:8] = jnp.zeros((4, rows), I32)


def slot_sums(turn, slot_cap, seq_len, slots_ref, packed_ref, dx_ref, n_dp):
    slots = n_dp * slot_cap
    rows = dx_ref.shape[0]
    step = min(512, rows)
    captions_per_step = step // seq_len
    total, digits, pooled = None, None, []
    for low in range(0, rows, step):
        cut = slice(low, low + step)
        place = slots_ref[0:1, cut] - turn * slot_cap
        dest, row = slots_ref[1:2, cut], slots_ref[2:3, cut]
        inside = jnp.logical_and(dest >= 0, jnp.logical_and(place >= 0, place < slot_cap))
        key = jnp.where(inside, dest * slot_cap + place, -1)
        hit = jnp.where(iota2((slots, step), 0) == key, 1.0, 0.0).astype(BF)
        piece = nn(hit, dx_ref[cut])
        total = piece if total is None else total + piece
        which = iota2((16, step), 0)
        value = jnp.where(which == 0, row // NOTE_BASE, jnp.where(which == 1, row % NOTE_BASE, 0))
        piece = nt(value.astype(F32).astype(BF), hit)
        digits = piece if digits is None else digits + piece
        _, _, is_end = unpack(packed_ref[:, cut])
        caption = iota2((captions_per_step, step), 1) // seq_len
        mark = jnp.logical_and(caption == iota2((captions_per_step, step), 0), is_end)
        pooled.append(nt(hit, jnp.where(mark, 1.0, 0.0).astype(BF)))
    return total, digits, jnp.concatenate(pooled, axis=1).astype(BF)


def rows_back_body(
    slot_cap, meta_ref, probs_ref, ds_ref, a_ref, vec_ref, slots_ref, packed_ref, qk_all, unit_all, inv_all,
    dx_out, posg_ref, small_ref, seg_ref, digits_ref, pooled_ref, dx_ref, sems,
):
    blocks = probs_ref.shape[0]
    heads = a_ref.shape[0]
    seq_len, width = posg_ref.shape
    block_rows = dx_ref.shape[0] // blocks
    gain = vec_ref[0:1]
    qk_ref, unit_ref, inv_ref = qk_all.wait(), unit_all.wait(), inv_all.wait()
    pending = []
    gain_grad = jnp.zeros((1, width), F32)
    bias_grad = jnp.zeros((1, width), F32)
    pos_grad = jnp.zeros((seq_len, width), F32)
    for block in range(blocks):
        caps = pl.ds(block * CAP_BLOCK, CAP_BLOCK)
        here = pl.ds(block * block_rows, block_rows)
        a = a_ref[:, caps, :].reshape(heads * CAP_BLOCK, width)
        qk = qk_ref[:, caps, :].reshape(heads * CAP_BLOCK, width)
        unit = unit_ref[here, :].astype(F32)
        drows = tn(probs_ref[block], a) + tn(ds_ref[block], qk)
        gain_grad = gain_grad + jnp.sum(drows * unit, 0, keepdims=True)
        bias_grad = bias_grad + jnp.sum(drows, 0, keepdims=True)
        dx = norm_back(drows, unit, inv_ref[here, 0:1], gain).astype(BF)
        dx_ref[here, :] = dx
        pos_grad = pos_grad + jnp.sum(dx.astype(F32).reshape(CAP_BLOCK, seq_len, width), 0)
    for block in range(blocks):
        here = pl.ds(block * block_rows, block_rows)
        copy = pltpu.make_async_copy(dx_ref.at[here], dx_out.at[here], sems.at[block])
        copy.start()
        pending.append(copy)
    small_ref[0:1] = gain_grad
    small_ref[1:2] = bias_grad
    posg_ref[...] = pos_grad
    seg_ref[...], digits_ref[...], pooled_ref[...] = slot_sums(
        0, slot_cap, seq_len, slots_ref, packed_ref, dx_ref, seg_ref.shape[0] // slot_cap
    )
    for copy in pending:
        copy.wait()


def query_back_body(
    n_mp, meta_ref, kept_ref, got_ref, wout_ref, dx1_ref, vec_ref, pos_pick_ref, own_pick_ref, slots_ref,
    seg_ref, digits_ref, pooled_ref, pos_one_ref, small_one_ref, small_two_ref, small_three_ref, x0p, wq,
    dxp_ref, send_ref, kept_out, sent_out, rest_ref, smalls_ref, all_ref,
):
    captions, width = dx1_ref.shape
    n_dp = send_ref.shape[0]
    slots = seg_ref.shape[0]
    slot_cap = slots // n_dp
    lanes = send_ref.shape[2]
    span = width // n_mp
    rank = meta_ref[0]
    total = kept_ref[...].astype(F32) + got_ref[...].astype(F32)
    all_ref[:, : 2 * span] = total[:width]
    all_ref[:, 2 * span : 3 * span] = wout_ref[...].astype(F32)
    dq = jnp.concatenate(
        [total[width + k * captions : width + (k + 1) * captions] for k in range(n_mp // 2)], axis=1
    ).astype(BF)
    gain = vec_ref[0:1]
    unit, inverse = normalize(x0p.value())
    h1 = (unit * gain + vec_ref[1:2]).astype(BF)
    owned = jnp.sum(own_pick_ref[...].astype(F32), -1, keepdims=True)
    dh1 = nn(dq, wq.value()) * owned
    dxp = (dx1_ref[...] * owned + norm_back(dh1, unit, inverse, gain)).astype(BF)
    dxp_ref[...] = dxp
    seq_len = pos_one_ref.shape[0]
    smalls_ref[...] = jnp.zeros_like(smalls_ref)
    smalls_ref[:seq_len] = pos_one_ref[...] + tn(pos_pick_ref[...], dxp)
    at = seq_len
    smalls_ref[at : at + 1] = small_three_ref[0:1] + jnp.sum(dh1 * unit, 0, keepdims=True)
    smalls_ref[at + 1 : at + 2] = small_three_ref[1:2] + jnp.sum(dh1, 0, keepdims=True)
    smalls_ref[at + 2 : at + 5] = small_two_ref[...]
    smalls_ref[at + 5 : at + 7] = small_one_ref[...]
    smalls = smalls_ref[...]
    high = smalls.astype(BF)
    low = (smalls - high.astype(F32)).astype(BF)
    all_ref[:, 3 * span :] = tn(h1, nn(dq, own_columns(rank * span, width, span)).astype(BF))
    chunk = width // n_dp
    blocks = [
        functools.partial(lambda i: all_ref[pl.ds(i * chunk, chunk), :], i) for i in range(n_dp)
    ]
    split_blocks(blocks, DOWN_BIT, meta_ref[2] // DOWN_BIT % 2, kept_out, sent_out)
    shape = (SMALLS, 2 * SMALLS)
    place = iota2(shape, 1) - iota2(shape, 0)
    rest_ref[...] = tn(high, jnp.where(place == 0, 1.0, 0.0).astype(BF)) + tn(
        low, jnp.where(place == SMALLS, 1.0, 0.0).astype(BF)
    )
    seg = (seg_ref[...] + nn(pooled_ref[...], dxp)).astype(BF)
    most = slots_ref[3:4, :lanes]
    which = iota2((NOTES, lanes), 0)
    most = jnp.where(which == 2, most // NOTE_BASE, most % NOTE_BASE).astype(F32)
    chunk = width // n_dp
    base = (width // lanes) * slot_cap
    for i in range(n_dp):
        for j in range(width // lanes):
            send_ref[i, j * slot_cap : (j + 1) * slot_cap, :] = seg[
                i * slot_cap : (i + 1) * slot_cap, j * lanes : (j + 1) * lanes
            ]
        extra = send_ref.shape[1] - NOTES
        tall = extra - base
        if 4 * tall != chunk:
            send_ref[i, base:extra, :] = jnp.zeros((tall, lanes), BF)
        for k in range(4):
            count = min(tall, chunk - k * tall)
            if count > 0:
                send_ref[i, base : base + count, k * 2 * SMALLS : (k + 1) * 2 * SMALLS] = rest_ref[
                    pl.ds(i * chunk + k * tall, count), :
                ].astype(BF)
        digits = digits_ref[:NOTES, i * slot_cap : (i + 1) * slot_cap]
        note = jnp.concatenate([digits, jnp.zeros((NOTES, lanes - slot_cap), F32)], axis=1)
        send_ref[i, extra:, :] = jnp.where(which < 2, note, most).astype(BF)


def send_body(slot_cap, meta_ref, dx_ref, dxp_ref, slots_ref, packed_ref, send_ref, digits_ref):
    n_dp, _, lanes = send_ref.shape
    width = dx_ref.shape[1]
    seq_len = dx_ref.shape[0] // dxp_ref.shape[0]
    seg, digits_ref[...], pooled = slot_sums(
        meta_ref[0], slot_cap, seq_len, slots_ref, packed_ref, dx_ref, n_dp
    )
    seg = (seg + nn(pooled, dxp_ref[...])).astype(BF)
    for i in range(n_dp):
        for j in range(width // lanes):
            send_ref[i, j * slot_cap : (j + 1) * slot_cap, :] = seg[
                i * slot_cap : (i + 1) * slot_cap, j * lanes : (j + 1) * lanes
            ]


def place_rows(row, got_ref, table_ref, slot_cap, lanes):
    n_dp = got_ref.shape[0]
    shape = (table_ref.shape[0], n_dp * slot_cap)
    hit = jnp.where(iota2(shape, 0) == row, 1.0, 0.0).astype(BF)
    for j in range(table_ref.shape[1] // lanes):
        cut = slice(j * slot_cap, (j + 1) * slot_cap)
        rows = jnp.concatenate([got_ref[i, cut, :] for i in range(n_dp)], axis=0)
        table_ref[:, j * lanes : (j + 1) * lanes] = nn(hit, rows)


def place_body(slot_cap, chunk, meta_ref, got_ref, table_ref, rest_ref, most_ref, row_ref):
    lanes = got_ref.shape[2]
    extra = got_ref.shape[1] - NOTES
    most = jnp.zeros((1, 128), F32)
    for i in range(got_ref.shape[0]):
        note = got_ref[i, extra:, :].astype(F32)
        at = slice(i * slot_cap, (i + 1) * slot_cap)
        row_ref[:, at] = note[0:1, :slot_cap] * float(NOTE_BASE) + note[1:2, :slot_cap] - 1.0
        most = jnp.maximum(most, note[2:3, :128] * float(NOTE_BASE) + note[3:4, :128])
    most_ref[...] = most
    place_rows(row_ref[...].astype(I32), got_ref, table_ref, slot_cap, lanes)
    base = table_ref.shape[1] // lanes * slot_cap
    total = got_ref[0, base:extra, :].astype(F32)
    for i in range(1, got_ref.shape[0]):
        total = total + got_ref[i, base:extra, :].astype(F32)
    for k in range(4):
        count = min(extra - base, chunk - k * (extra - base))
        if count > 0:
            cut = slice(k * 2 * SMALLS, k * 2 * SMALLS + SMALLS)
            low = slice(k * 2 * SMALLS + SMALLS, (k + 1) * 2 * SMALLS)
            at = k * (extra - base)
            rest_ref[at : at + count, :] = total[:count, cut] + total[:count, low]


def place_more_body(meta_ref, row_ref, got_ref, old_ref, table_ref):
    lanes = got_ref.shape[2]
    slot_cap = got_ref.shape[1] // (table_ref.shape[1] // lanes)
    place_rows(row_ref[...], got_ref, table_ref, slot_cap, lanes)
    table_ref[...] += old_ref[...]


def on_device(
    token_ids, lengths, images, table, pos_table, ln1_gain, ln1_bias, w_qkv, w_out, b_out,
    ln2_gain, ln2_bias, w_up, b_up, w_down, b_down, w_head,
):
    n_mp, n_dp = lax.axis_size("mp"), lax.axis_size("dp")
    mp_rank, dp_rank = lax.axis_index("mp"), lax.axis_index("dp")
    captions, seq_len = token_ids.shape
    rows = captions * seq_len
    vocab_part, width = table.shape
    heads = width // HEAD_DIM
    own_width = width // n_mp
    ff = w_up.shape[1]
    owner_rows = vocab_part // n_dp
    slot_cap = -(-rows // (n_dp * n_mp * 16)) * 16
    slots = n_dp * slot_cap
    chunk = width // n_dp
    lanes = own_width + 2 * SMALLS
    n_all = captions * n_dp
    blocks = captions // CAP_BLOCK
    meta = jnp.stack([mp_rank, dp_rank * captions, dp_rank]).astype(I32)

    gather = functools.partial(lax.all_gather, axis_name="mp", axis=0)
    turned = jnp.swapaxes(w_qkv, 1, 2)
    shard = jnp.concatenate([turned, w_out[None]])
    image_f = images.astype(F32)
    image_unit = (
        image_f * lax.rsqrt(jnp.sum(image_f * image_f, -1, keepdims=True) + EPS)
    ).astype(BF)
    all_image = lax.all_gather(image_unit, ("dp", "mp"), axis=0, tiled=True)
    at_row = jnp.arange(8)[:, None]
    vecs = b_up.astype(F32)[None, :]
    for k, vec in enumerate((ln1_gain, ln1_bias, b_out, ln2_gain, ln2_bias, b_down)):
        vecs = jnp.where(at_row == k, vec.astype(F32)[None, :], vecs)

    valid = jnp.arange(seq_len)[None, :] < lengths[:, None]
    end_pick = jnp.arange(seq_len)[None, :] == (lengths - 1)[:, None]
    pos_pick = end_pick.astype(BF)
    local2 = token_ids - mp_rank * vocab_part
    owned2 = jnp.logical_and(local2 >= 0, local2 < vocab_part)
    own_pick = jnp.logical_and(end_pick, owned2).astype(BF)
    local = token_ids.reshape(rows) - mp_rank * vocab_part
    local = after(local, image_unit)
    emb = jnp.take(table, jnp.clip(local, 0, vocab_part - 1), axis=0, mode="clip")
    packed = token_ids + jnp.where(valid, VALID_BIT, 0) + jnp.where(end_pick, END_BIT, 0)
    packed = packed.astype(I32).reshape(1, rows)
    per_head = pltpu.VMEM((heads, captions, width), BF)
    per_head = pltpu.VMEM((heads, captions, width), BF)
    row_buffer = pltpu.VMEM((rows, width), BF)
    dma = pltpu.SemaphoreType.DMA
    ends, unit_rows, unit, inverse = vmem_call(
        functools.partial(rows_body, vocab_part),
        [
            ((captions, width), BF),
            ((rows, width), BF, False),
            ((rows, width), BF, False),
            ((rows, 128), F32, False),
        ],
        meta,
        [pos_table, vecs, packed],
        [fetch(emb, blocks)],
        [row_buffer, row_buffer, pltpu.VMEM((rows, 128), F32), dma((3 * blocks,))],
        flops=WORK,
        mib=28,
    )
    shards = everyone(shard, "mp", ends)
    wq, wk, wv, wo = (fetch_weight(shards, k) for k in range(4))
    pay, qk, x0p, q = vmem_call(
        functools.partial(attend_body, vocab_part),
        [
            ((captions, width + 128), BF),
            ((heads, captions, width), BF, False),
            ((captions, width), F32, True),
            ((captions, width), BF, True),
        ],
        meta,
        [gather(ends), pos_pick, pos_table, vecs, packed],
        [wq, wk, fetch(unit_rows, blocks), wv],
        [per_head, per_head, dma((n_mp,))],
        flops=WORK,
        mib=28,
    )
    ctx, lse, x1, u, part = vmem_call(
        hidden_body,
        [
            ((captions, width), F32, True),
            ((captions, width), F32, True),
            ((captions, width), F32, True),
            ((captions, ff), F32, True),
            ((captions, width), BF),
        ],
        meta,
        [gather(pay), vecs],
        [fetch(x0p), wo, fetch(w_up), fetch(w_down)],
        flops=WORK,
        mib=20,
    )
    pooled, proj, powers, sums = vmem_call(
        logits_body,
        [
            ((captions, width), BF, True),
            ((captions, width), F32, True),
            ((captions, n_all), F32, True),
            ((n_dp, 1, n_all + 128), F32),
        ],
        meta,
        [gather(part), vecs],
        [fetch(x1), fetch(w_head), fetch(all_image)],
        flops=WORK * 5,
    )
    all_sums = lax.all_to_all(sums, "dp", 0, 0, tiled=True)
    slot_table = vmem_call(
        functools.partial(slot_body, owner_rows, n_dp),
        [((8, rows), I32)],
        meta,
        [after(packed, sums)],
        flops=WORK * 7,
        mib=20,
    )[0]
    loss, dpooled, part, *halves, small_one = vmem_call(
        loss_body,
        [
            ((1, 128), F32),
            ((captions, width), F32),
            ((captions, width), BF),
            *[((n_dp // 2, chunk, ff + own_width), BF)] * 2,
            *[((n_dp // 2, chunk, ff), BF)] * 2,
            ((2, width), F32),
        ],
        meta,
        [after(all_sums, slot_table), vecs],
        [
            fetch(powers), fetch(all_image), fetch(proj), fetch(w_head), fetch(u), fetch(w_down),
            fetch(w_up), fetch(x1), fetch(pooled),
        ],
        [pltpu.VMEM((width, ff + own_width), F32), pltpu.VMEM((width, ff), F32)],
        flops=WORK * 8,
    )
    dp_bits = bits_of("dp")

    def next_half(total, bits):
        total = halve(total, "dp", bits, bits[0])
        bits.pop(0)
        return total

    one_step = len(dp_bits) == 1
    down = exchange_half(*halves[:2], "dp", DOWN_BIT, one_step)
    up = exchange_half(*halves[2:], "dp", UP_BIT, one_step)
    down_bits = [bit for bit in dp_bits if bit != DOWN_BIT]
    up_bits = [bit for bit in dp_bits if bit != UP_BIT]
    for bit in bits_of("mp"):
        part = part + lax.ppermute(part, "mp", [(i, i ^ bit) for i in range(n_mp)])
    parts = part[None]
    pair_rows = n_mp // 2 * (width + captions)
    dx1, wout, kept, *sent, a, probs, dscores, small_two = vmem_call(
        functools.partial(attend_back_body, vocab_part),
        [
            ((captions, width), F32),
            ((width, own_width), BF),
            ((pair_rows, 2 * own_width), BF),
            *[((pair_rows // 2, 2 * own_width), BF)] * 2,
            ((heads, captions, width), BF),
            ((blocks, heads * CAP_BLOCK, CAP_BLOCK * seq_len), BF),
            ((blocks, heads * CAP_BLOCK, CAP_BLOCK * seq_len), BF),
            ((3, width), F32),
        ],
        meta,
        [parts, packed, vecs, dpooled],
        [
            fetch(x1), fetch(ctx), wo, wv, fetch(lse), fetch(qk, blocks, 1),
            fetch(unit_rows, blocks), wk, fetch(q),
        ],
        [
            per_head, per_head, pltpu.VMEM((n_mp, width, 2 * own_width), BF),
            pltpu.VMEM((captions, width), BF),
        ],
        flops=WORK * 13,
    )
    got = [lax.ppermute(x, "mp", [(i, i ^ 1) for i in range(n_mp)]) for x in sent]
    last_rows = pair_rows - width
    kept, sent = vmem_call(
        between_body, [((last_rows, 2 * own_width), BF)] * 2, meta, [kept, *got], flops=WORK * 2, mib=12
    )
    got = lax.ppermute(sent, "mp", [(i, i ^ 2) for i in range(n_mp)])
    dx, pos_one, small_three, seg, digits, pooled_slots = vmem_call(
        functools.partial(rows_back_body, slot_cap),
        [
            ((rows, width), BF, False),
            ((seq_len, width), F32),
            ((2, width), F32),
            ((slots, width), F32),
            ((16, slots), F32),
            ((slots, captions), BF),
        ],
        meta,
        [after(probs, sent), dscores, a, vecs, slot_table, packed],
        [fetch(qk, blocks, 1), fetch(unit, blocks), fetch(inverse, blocks)],
        [row_buffer, dma((blocks,))],
        flops=WORK * 12,
        mib=32,
    )
    down, up = next_half(down, down_bits), next_half(up, up_bits)
    rest_rows = -(-chunk // 32) * 8
    send_rows = width // lanes * slot_cap
    dxp, send, kept, sent = vmem_call(
        functools.partial(query_back_body, n_mp),
        [
            ((captions, width), BF),
            ((n_dp, send_rows + rest_rows + NOTES, lanes), BF),
            *[((n_dp // 2, chunk, 4 * own_width), BF)] * 2,
        ],
        meta,
        [
            kept, got, wout, dx1, vecs, pos_pick, own_pick, slot_table, seg, digits, pooled_slots, pos_one,
            small_one, small_two, small_three,
        ],
        [fetch(x0p), wq],
        [
            pltpu.VMEM((width, 2 * SMALLS), F32), pltpu.VMEM((SMALLS, width), F32),
            pltpu.VMEM((width, 4 * own_width), F32),
        ],
        flops=WORK * 4,
        mib=24,
    )
    got = lax.all_to_all(send, "dp", 0, 0, tiled=True)
    wkvo = exchange_half(kept, sent, "dp", DOWN_BIT, one_step)
    bits = [bit for bit in dp_bits if bit != DOWN_BIT]
    while len(bits) > 1:
        wkvo = next_half(wkvo, bits)
    while down_bits:
        down = next_half(down, down_bits)
    while up_bits:
        up = next_half(up, up_bits)
    down, up = lax.optimization_barrier((down[0], up[0]))
    table_grad, rest, most_all = vmem_call(
        functools.partial(place_body, slot_cap, chunk),
        [((owner_rows, width), F32), ((chunk, SMALLS), F32), ((1, 128), F32)],
        meta,
        [got],
        (),
        [pltpu.VMEM((1, slots), F32)],
        flops=WORK * 3,
        mib=20,
    )
    most_all = most_all[0, 0].astype(I32)
    small = rest
    last = gather(jnp.concatenate([down[:, ff:], small, jnp.zeros_like(small)], 1))
    wkvo = lax.optimization_barrier(next_half(wkvo, bits)[0])

    def another(carry):
        turn, total = carry
        sent, digits = vmem_call(
            functools.partial(send_body, slot_cap),
            [((n_dp, send_rows, lanes), BF), ((16, slots), F32)],
            turn.reshape(1),
            [dx, dxp, slot_table, packed],
        )
        row = (digits[0] * NOTE_BASE + digits[1] - 1.0).astype(I32)
        row = lax.all_to_all(row.reshape(n_dp, slot_cap), "dp", 0, 0, tiled=True)
        sent = lax.all_to_all(sent, "dp", 0, 0, tiled=True)
        total = vmem_call(
            place_more_body,
            [((owner_rows, width), F32)],
            meta,
            [row.reshape(1, slots), sent, total],
        )[0]
        return turn + 1, total

    _, table_grad = lax.while_loop(
        lambda carry: carry[0] * slot_cap < most_all, another, (jnp.int32(1), table_grad)
    )
    w_head_grad = jnp.swapaxes(last[:, :, :own_width], 0, 1).reshape(chunk, width)
    shared = jnp.sum(last[:, :, own_width : own_width + SMALLS], 0)
    qkv_grad = jnp.stack(
        [wkvo[:, k * own_width : (k + 1) * own_width] for k in (3, 0, 1)]
    )
    return (
        loss[0, 0],
        table_grad,
        shared[:, :seq_len].T,
        shared[:, seq_len],
        shared[:, seq_len + 1],
        qkv_grad,
        wkvo[:, 2 * own_width : 3 * own_width].T,
        small[:, seq_len + 4],
        small[:, seq_len + 2],
        small[:, seq_len + 3],
        up,
        small[:, seq_len + 6],
        down[:, :ff].T,
        small[:, seq_len + 5],
        w_head_grad,
    )


def solution(mesh):
    placed = (
        P("dp", None),
        P("dp"),
        P(("dp", "mp"), None),
        P("mp", None),
        P(),
        P(),
        P(),
        P(None, None, "mp"),
        P("mp", None),
        P(),
        P(),
        P(),
        P(None, "mp"),
        P("mp"),
        P("mp", None),
        P(),
        P(),
    )
    return jax.shard_map(
        on_device,
        mesh=mesh,
        in_specs=placed,
        out_specs=(
            P(),
            P(("mp", "dp"), None),
            P(None, "dp"),
            P("dp"),
            P("dp"),
            P(None, "dp", "mp"),
            P("mp", "dp"),
            P("dp"),
            P("dp"),
            P("dp"),
            P("dp", "mp"),
            P(("mp", "dp")),
            P("mp", "dp"),
            P("dp"),
            P("dp", None),
        ),
        check_vma=False,
    )
```

```python
import functools
import math

import jax
import jax.numpy as jnp
from jax import lax
from jax.experimental import pallas as pl
from jax.experimental.pallas import tpu as pltpu
from jax.sharding import PartitionSpec as P

HEAD_DIM = 64
LOGIT_SCALE = 50.0
EPS = 1e-06
MASK_FILL = -1000000000.0
NO_KEY = -1e30
BF = jnp.bfloat16
F32 = jnp.float32
I32 = jnp.int32
GELU_C = math.sqrt(2.0 / math.pi)
CAP_BLOCK = 16
SMALLS = 32
NOTES = 8
HALF = 4
VALID_BIT = 1 << 20
END_BIT = 1 << 21
NOTE_BASE = 32
WORK = 920000000
DOWN_BIT = 1
UP_BIT = 2


def nn(a, b):
    return lax.dot_general(a, b, (((1,), (0,)), ((), ())), preferred_element_type=F32)


def nt(a, b):
    return lax.dot_general(a, b, (((1,), (1,)), ((), ())), preferred_element_type=F32)


def tn(a, b):
    return lax.dot_general(a, b, (((0,), (0,)), ((), ())), preferred_element_type=F32)


def normalize(rows):
    centred = rows - jnp.mean(rows, -1, keepdims=True)
    inverse = lax.rsqrt(jnp.mean(centred * centred, -1, keepdims=True) + EPS)
    return centred * inverse, inverse


def norm_back(upstream, unit, inverse, gain):
    scaled = upstream * gain
    mean_scaled = jnp.mean(scaled, -1, keepdims=True)
    mean_unit = jnp.mean(scaled * unit, -1, keepdims=True)
    return inverse * (scaled - mean_scaled - unit * mean_unit)


def iota2(shape, dim):
    return lax.broadcasted_iota(I32, shape, dim)


class Late:
    def __init__(self, ref, pairs, sems):
        self.ref = ref
        self.copies = [
            pltpu.make_async_copy(src, dst, sem) for (src, dst), sem in zip(pairs, sems)
        ]
        self.waiting = set(range(len(self.copies)))

    def start(self):
        for copy in self.copies:
            copy.start()

    def wait(self, part=None):
        for k in sorted(self.waiting) if part is None else [part]:
            if k in self.waiting:
                self.copies[k].wait()
                self.waiting.discard(k)
        return self.ref

    def value(self):
        return self.wait()[...]


def fetch(array, parts=1, axis=0):
    return ("blocks", [array], parts, axis)


def fetch_weight(shards, which):
    return ("weight", list(shards), which, 0)


def vmem_call(body, outs, meta, args, late=(), scratch=(), flops=1, mib=40):
    vmem = pl.BlockSpec(memory_space=pltpu.VMEM)
    hbm = pl.BlockSpec(memory_space=pltpu.HBM)
    sources, buffers, counts = [], [], []
    for kind, arrays, parts, axis in late:
        sources += arrays
        if kind == "weight":
            _, rows, width = arrays[0].shape
            buffers.append(pltpu.VMEM((rows * len(arrays), width), arrays[0].dtype))
            counts.append(len(arrays))
        else:
            buffers.append(pltpu.VMEM(arrays[0].shape, arrays[0].dtype))
            counts.append(parts)

    staged = [k for k, o in enumerate(outs) if len(o) > 2 and o[2]]

    def kernel(meta_ref, *refs):
        arg_refs, refs = refs[: len(args)], refs[len(args) :]
        source_refs, refs = refs[: len(sources)], refs[len(sources) :]
        out_refs, refs = refs[: len(outs)], refs[len(outs) :]
        buffer_refs, refs = refs[: len(buffers)], refs[len(buffers) :]
        sems, stage_sems, refs = refs[0], refs[1], refs[2:]
        stages, refs = refs[: len(staged)], refs[len(staged) :]
        targets = list(out_refs)
        for k, stage in zip(staged, stages):
            targets[k] = stage
        handles, at, place = [], 0, 0
        for (kind, arrays, parts, axis), buffer in zip(late, buffer_refs):
            if kind == "weight":
                rows = arrays[0].shape[1]
                pairs = []
                for k in range(len(arrays)):
                    low = pl.multiple_of((meta_ref[0] ^ k) * rows, rows)
                    pairs.append((source_refs[place + k].at[parts], buffer.at[pl.ds(low, rows)]))
                place += len(arrays)
            else:
                size = arrays[0].shape[axis] // parts
                pairs = []
                for k in range(parts):
                    cut = (slice(None),) * axis + (pl.ds(k * size, size),)
                    pairs.append((source_refs[place].at[cut], buffer.at[cut]))
                place += 1
            handles.append(Late(buffer, pairs, [sems.at[at + k] for k in range(len(pairs))]))
            at += len(pairs)
        for handle in handles:
            handle.start()
        body(meta_ref, *arg_refs, *handles, *targets, *refs)
        copies = [
            pltpu.make_async_copy(stage, out_refs[k], stage_sems.at[i])
            for i, (k, stage) in enumerate(zip(staged, stages))
        ]
        for copy in copies:
            copy.start()
        for handle in handles:
            handle.wait()
        for copy in copies:
            copy.wait()

    return pl.pallas_call(
        kernel,
        out_shape=[
            pltpu.HBM(*o[:2]) if len(o) > 2 else jax.ShapeDtypeStruct(*o) for o in outs
        ],
        in_specs=[pl.BlockSpec(memory_space=pltpu.SMEM)]
        + [vmem] * len(args)
        + [hbm] * len(sources),
        out_specs=[hbm if len(o) > 2 else vmem for o in outs],
        scratch_shapes=[
            *buffers,
            pltpu.SemaphoreType.DMA((max(1, sum(counts)),)),
            pltpu.SemaphoreType.DMA((max(1, len(staged)),)),
            *(pltpu.VMEM(*outs[k][:2]) for k in staged),
            *scratch,
        ],
        compiler_params=pltpu.CompilerParams(vmem_limit_bytes=mib << 20),
        cost_estimate=pl.CostEstimate(flops=flops, bytes_accessed=1, transcendentals=0),
    )(meta, *args, *(pltpu.with_memory_space_constraint(x, pltpu.HBM) for x in sources))


def exchange_half(kept, sent, axis, bit, last):
    count = lax.axis_size(axis)
    got = lax.ppermute(sent, axis, [(i, i ^ bit) for i in range(count)])
    total = kept.astype(F32) + got.astype(F32)
    return total if last else total.astype(BF)


def halve(total, axis, bits, bit):
    low = 1 << bits.index(bit)
    pairs = total.reshape((total.shape[0] // (2 * low), 2, low) + total.shape[1:])
    shape = (total.shape[0] // 2,) + total.shape[1:]
    mine = (lax.axis_index(axis) // bit) % 2
    sent = lax.dynamic_index_in_dim(pairs, 1 - mine, 1, keepdims=False).reshape(shape)
    kept = lax.dynamic_index_in_dim(pairs, mine, 1, keepdims=False).reshape(shape)
    return exchange_half(kept, sent, axis, bit, len(bits) == 1)


def split_blocks(blocks, bit, mine, kept_ref, sent_ref):
    place = 0
    for i in range(len(blocks)):
        if i & bit == 0:
            first, second = blocks[i](), blocks[i | bit]()
            kept_ref[place] = jnp.where(mine == 0, first, second).astype(BF)
            sent_ref[place] = jnp.where(mine == 0, second, first).astype(BF)
            place += 1


def bits_of(axis):
    count = lax.axis_size(axis)
    return [1 << k for k in range(count.bit_length() - 1)]


def after(x, *others):
    return lax.optimization_barrier((x, others))[0]


def everyone(x, axis, before):
    count = lax.axis_size(axis)
    have = {0: x}
    bit = count // 2
    while bit:
        pairs = [(i, i ^ bit) for i in range(count)]
        for k, v in list(have.items()):
            have[k | bit] = lax.ppermute(after(v, before) if k else v, axis, pairs)
        bit //= 2
    return [have[k] for k in range(count)]


def own_columns(start, width, own_width):
    shape = (width, own_width)
    hit = iota2(shape, 0) == start + iota2(shape, 1)
    return jnp.where(hit, 1.0, 0.0).astype(BF)


def unpack(packed):
    return packed % VALID_BIT, packed // VALID_BIT % 2 > 0, packed // END_BIT > 0


def own_code(packed, rank, vocab_part):
    ids, valid, _ = unpack(packed)
    return jnp.where(ids // vocab_part == rank, jnp.where(valid, 2, 1), 0)


def head_mask(captions, span):
    shape = (span // HEAD_DIM * captions, span)
    return (iota2(shape, 0) // captions) == (iota2(shape, 1) // HEAD_DIM)


def spread_heads(rows, group, mask):
    span = mask.shape[1]
    part = rows[:, group * span : (group + 1) * span].astype(F32)
    tall = jnp.concatenate([part] * (span // HEAD_DIM), axis=0)
    return jnp.where(mask, tall, 0.0).astype(BF)


def fold_heads(tall, captions, mask):
    kept = jnp.where(mask, tall, 0.0)
    total = kept[:captions]
    for h in range(1, tall.shape[0] // captions):
        total = total + kept[h * captions : (h + 1) * captions]
    return total


def same_caption(heads, seq_len):
    shape = (heads * CAP_BLOCK, CAP_BLOCK * seq_len)
    return (iota2(shape, 0) % CAP_BLOCK) == (iota2(shape, 1) // seq_len)


def rows_body(
    vocab_part, meta_ref, pos_ref, vec_ref, packed_ref, emb,
    end_ref, rows_out, unit_out, inv_out, rows_ref, unit_ref, inv_ref, sems,
):
    captions = end_ref.shape[0]
    seq_len = pos_ref.shape[0]
    block_rows = CAP_BLOCK * seq_len
    gain, bias = vec_ref[0:1], vec_ref[1:2]
    pos = jnp.concatenate([pos_ref[...].astype(F32)] * CAP_BLOCK, axis=0)
    pending = []

    def write_back(src, dst):
        copy = pltpu.make_async_copy(src, dst, sems.at[len(pending)])
        copy.start()
        pending.append(copy)

    blocks = captions // CAP_BLOCK
    for block in range(blocks):
        here = pl.ds(block * block_rows, block_rows)
        if block % HALF == 0:
            for k in range(block, min(block + HALF, blocks)):
                emb.wait(k)
        packed = packed_ref[:, block * block_rows : (block + 1) * block_rows]
        low = emb.ref[here, :]
        ids, _, is_end = unpack(packed)
        shape = (CAP_BLOCK, block_rows)
        mark = jnp.logical_and(is_end, ids // vocab_part == meta_ref[0])
        mark = jnp.logical_and(iota2(shape, 0) == iota2(shape, 1) // seq_len, mark)
        ends = nn(jnp.where(mark, 1.0, 0.0).astype(BF), low)
        end_ref[block * CAP_BLOCK : (block + 1) * CAP_BLOCK] = ends.astype(BF)
        unit, inverse = normalize(low.astype(F32) + pos)
        unit_ref[here, :] = unit.astype(BF)
        inv_ref[here, :] = jnp.broadcast_to(inverse, (block_rows, 128))
        rows_ref[here, :] = (unit * gain + bias).astype(BF)
        if block % HALF == HALF - 1 or block == blocks - 1:
            low_row = block // HALF * HALF * block_rows
            done = pl.ds(low_row, (block + 1) * block_rows - low_row)
            write_back(unit_ref.at[done], unit_out.at[done])
            write_back(inv_ref.at[done], inv_out.at[done])
            write_back(rows_ref.at[done], rows_out.at[done])
    for copy in pending:
        copy.wait()


def attend_body(
    vocab_part, meta_ref, ends_ref, pos_pick_ref, pos_ref, vec_ref, packed_ref, wq, wk, rows_all, wv,
    pay_ref, qk_out, x0p_ref, q_ref, qk_ref, t_ref, sems,
):
    n_mp = ends_ref.shape[0]
    captions, width = x0p_ref.shape
    heads = width // HEAD_DIM
    span = width // n_mp
    per_group = span // HEAD_DIM
    seq_len = pos_ref.shape[0]
    block_rows = CAP_BLOCK * seq_len
    gain, bias = vec_ref[0:1], vec_ref[1:2]
    pooled_in = nn(pos_pick_ref[...], pos_ref[...])
    for i in range(n_mp):
        pooled_in = pooled_in + ends_ref[i].astype(F32)
    pending = []
    x0p_ref[...] = pooled_in
    unit, _ = normalize(pooled_in)
    q = nt((unit * gain + bias).astype(BF), wq.value()).astype(BF)
    q_ref[...] = q
    mask = head_mask(captions, span)
    scale = 1.0 / math.sqrt(HEAD_DIM)
    wk_ref = wk.wait()
    for g in range(n_mp):
        some = slice(g * per_group, (g + 1) * per_group)
        tall = nn(spread_heads(q, g, mask), wk_ref[g * span : (g + 1) * span]) * scale
        qk_ref[some] = tall.astype(BF).reshape(per_group, captions, width)
        copy = pltpu.make_async_copy(qk_ref.at[some], qk_out.at[some], sems.at[g])
        copy.start()
        pending.append(copy)
    lane = iota2((heads, CAP_BLOCK, 128), 2)
    head_of = iota2((heads, CAP_BLOCK, 128), 0)
    rows_ref = rows_all.wait()
    blocks = range(captions // CAP_BLOCK)
    cuts = [pl.ds(block * block_rows, block_rows) for block in blocks]
    caps = [pl.ds(block * CAP_BLOCK, CAP_BLOCK) for block in blocks]
    raw = [
        nt(qk_ref[:, caps[block], :].reshape(heads * CAP_BLOCK, width), rows_ref[cuts[block], :])
        for block in blocks
    ]
    same = same_caption(heads, seq_len)
    code = own_code(packed_ref[...], meta_ref[0], vocab_part)
    log_totals, weights = [], []
    for block in blocks:
        here = code[:, block * block_rows : (block + 1) * block_rows]
        own = jnp.logical_and(same, here > 0)
        scores = jnp.where(own, jnp.where(here > 1, raw[block], MASK_FILL), NO_KEY)
        top = jnp.max(scores, -1, keepdims=True)
        power = jnp.where(own, jnp.exp(scores - top), 0.0)
        total = jnp.sum(power, -1, keepdims=True)
        some = total > 0.0
        total = jnp.where(some, total, 1.0)
        log_totals.append(jnp.where(some, top + jnp.log(total), NO_KEY))
        weights.append((power * (1.0 / total)).astype(BF))
    for block in blocks:
        mixed = nn(weights[block], rows_ref[cuts[block], :])
        t_ref[:, caps[block], :] = mixed.astype(BF).reshape(heads, CAP_BLOCK, width)
    for block in blocks:
        log_total = log_totals[block]
        first = log_total.astype(BF).astype(F32)
        second = (log_total - first).astype(BF).astype(F32)
        third = log_total - first - second
        stat = jnp.zeros((heads, CAP_BLOCK, 128), F32)
        for k, piece in enumerate((first, second, third)):
            stat = stat + jnp.where(
                lane == head_of + 16 * k, piece.reshape(heads, CAP_BLOCK, 1), 0.0
            )
        pay_ref[caps[block], width:] = jnp.sum(stat, 0).astype(BF)
    wv_ref = wv.wait()
    for g in range(n_mp):
        tall = t_ref[g * per_group : (g + 1) * per_group].reshape(per_group * captions, width)
        piece = nt(tall, wv_ref[g * span : (g + 1) * span])
        pay_ref[:, g * span : (g + 1) * span] = fold_heads(piece, captions, mask).astype(BF)
    for copy in pending:
        copy.wait()


def hidden_body(
    meta_ref, pay_ref, vec_ref, x0p, wo, wup, wdown,
    ctx_ref, lse_ref, x1_ref, u_ref, part_ref,
):
    n_mp = pay_ref.shape[0]
    captions, width = ctx_ref.shape
    shape = (128, width)
    stat_row, head = iota2(shape, 0), iota2(shape, 1) // HEAD_DIM
    picks = jnp.logical_and(stat_row % 16 == head, stat_row < 48)
    expand = jnp.where(picks, 1.0, 0.0).astype(BF)
    logs = [nn(pay_ref[i, :, width:], expand) for i in range(n_mp)]
    top = functools.reduce(jnp.maximum, logs)
    total = jnp.zeros_like(top)
    ctx = jnp.zeros_like(top)
    for i in range(n_mp):
        weight = jnp.exp(logs[i] - top)
        total = total + weight
        ctx = ctx + weight * pay_ref[i, :, :width].astype(F32)
    ctx = ctx / total
    ctx_ref[...] = ctx
    lse_ref[...] = top + jnp.log(total)
    x1 = x0p.value() + nn(ctx.astype(BF), wo.value()) + vec_ref[2:3]
    x1_ref[...] = x1
    unit, _ = normalize(x1)
    h2 = (unit * vec_ref[3:4] + vec_ref[4:5]).astype(BF)
    u = nn(h2, wup.value()) + vec_ref[6:7]
    u_ref[...] = u
    hidden = (0.5 * u * (1.0 + jnp.tanh(GELU_C * (u + 0.044715 * u * u * u)))).astype(BF)
    part_ref[...] = nn(hidden, wdown.value()).astype(BF)


def logits_body(
    meta_ref, parts_ref, vec_ref, x1, wh, images,
    pooled_ref, proj_ref, e_ref, sums_ref,
):
    x2 = x1.value() + vec_ref[5:6]
    for i in range(parts_ref.shape[0]):
        x2 = x2 + parts_ref[i].astype(F32)
    pooled = x2.astype(BF)
    pooled_ref[...] = pooled
    proj = nn(pooled, wh.value())
    proj_ref[...] = proj
    text = (proj * lax.rsqrt(jnp.sum(proj * proj, -1, keepdims=True) + EPS)).astype(BF)
    logits = LOGIT_SCALE * nt(text, images.value())
    powers = jnp.exp(logits)
    e_ref[...] = powers
    n_all = powers.shape[1]
    is_diag = iota2(logits.shape, 1) == meta_ref[1] + iota2(logits.shape, 0)
    rows = jnp.log(jnp.sum(powers, -1, keepdims=True))
    rows = rows - 2.0 * jnp.sum(jnp.where(is_diag, logits, 0.0), -1, keepdims=True)
    cols = jnp.sum(powers, 0, keepdims=True)
    rows = jnp.broadcast_to(jnp.sum(rows, 0, keepdims=True), (1, 128))
    for i in range(sums_ref.shape[0]):
        sums_ref[i, :, :n_all] = cols
        sums_ref[i, :, n_all:] = rows


def loss_body(
    meta_ref, sums_ref, vec_ref, e, images, proj, wh, u, wdown, wup,
    loss_ref, dpooled_ref, part_ref, du_ref, dproj_ref,
):
    sums = jnp.sum(sums_ref[...], 0)
    n_all = sums.shape[1] - 128
    cols = sums[:, :n_all]
    loss = jnp.sum(jnp.log(cols), -1, keepdims=True) + sums[:, n_all : n_all + 1]
    loss_ref[...] = jnp.broadcast_to(loss * (0.5 / n_all), (1, 128))
    powers = e.value()
    row_inv = 1.0 / jnp.sum(powers, -1, keepdims=True)
    is_diag = iota2(powers.shape, 1) == meta_ref[1] + iota2(powers.shape, 0)
    grad = powers * row_inv + powers * (1.0 / cols) - jnp.where(is_diag, 2.0, 0.0)
    grad = (grad * (0.5 / n_all)).astype(BF)
    dtext = LOGIT_SCALE * nn(grad, images.value())
    proj = proj.value()
    inv = lax.rsqrt(jnp.sum(proj * proj, -1, keepdims=True) + EPS)
    along = jnp.sum(proj * dtext, -1, keepdims=True)
    dproj = (inv * dtext - inv * inv * inv * proj * along).astype(BF)
    dproj_ref[...] = dproj
    dpooled = nt(dproj, wh.value())
    dpooled_ref[...] = dpooled
    u = u.value()
    th = jnp.tanh(GELU_C * (u + 0.044715 * u * u * u))
    slope = 0.5 * (1.0 + th) + 0.5 * u * (1.0 - th * th) * (
        GELU_C * (1.0 + 3.0 * 0.044715 * u * u)
    )
    du = (nt(dpooled.astype(BF), wdown.value()) * slope).astype(BF)
    du_ref[...] = du
    part_ref[...] = nt(du, wup.value()).astype(BF)


def weights_body(
    meta_ref, vec_ref, dpooled_ref, du_ref, dproj_ref, u, x1, pooled,
    down_kept, down_sent, up_kept, up_sent, small_ref, down_ref, up_ref,
):
    width = dpooled_ref.shape[1]
    dy, du, dproj = dpooled_ref[...].astype(BF), du_ref[...], dproj_ref[...]
    u = u.value()
    th = jnp.tanh(GELU_C * (u + 0.044715 * u * u * u))
    hidden = (0.5 * u * (1.0 + th)).astype(BF)
    unit, _ = normalize(x1.value())
    h2 = (unit * vec_ref[3:4] + vec_ref[4:5]).astype(BF)
    ff = u.shape[1]
    own_width = down_ref.shape[1] - ff
    pick = own_columns(meta_ref[0] * own_width, width, own_width)
    kind = down_ref.dtype
    down_ref[:, :ff] = tn(dy, hidden).astype(kind)
    up_ref[...] = tn(h2, du).astype(kind)
    down_ref[:, ff:] = tn(pooled.value(), nn(dproj, pick).astype(BF)).astype(kind)
    chunk = down_kept.shape[1]
    n_dp = 2 * down_kept.shape[0]
    for ref, bit, kept, sent in (
        (down_ref, DOWN_BIT, down_kept, down_sent),
        (up_ref, UP_BIT, up_kept, up_sent),
    ):
        blocks = [
            functools.partial(lambda ref, i: ref[pl.ds(i * chunk, chunk), :], ref, i)
            for i in range(n_dp)
        ]
        split_blocks(blocks, bit, meta_ref[2] // bit % 2, kept, sent)
    small_ref[0:1] = jnp.sum(dy.astype(F32), 0, keepdims=True)
    small_ref[1:2] = jnp.sum(du.astype(F32), 0, keepdims=True)


def attend_back_body(
    vocab_part, meta_ref, parts_ref, packed_ref, vec_ref, dpooled_ref, x1, ctx, wo, wv, lse, qk_all, rows_all, wk, q,
    dx1_ref, wout_ref, kept_ref, sent_one, sent_two, a_ref, probs_ref, ds_ref, small_ref,
    t_ref, s_ref, wkv_ref, dq_ref,
):
    n_mp = wkv_ref.shape[0]
    captions, width = dpooled_ref.shape
    heads = width // HEAD_DIM
    span = width // n_mp
    per_group = span // HEAD_DIM
    block_rows = rows_all.ref.shape[0] // (captions // CAP_BLOCK)
    seq_len = block_rows // CAP_BLOCK
    rank = meta_ref[0]
    dh2 = parts_ref[0].astype(F32)
    for i in range(1, parts_ref.shape[0]):
        dh2 = dh2 + parts_ref[i].astype(F32)
    unit2, inv2 = normalize(x1.value())
    small_ref[0:1] = jnp.sum(dh2 * unit2, 0, keepdims=True)
    small_ref[1:2] = jnp.sum(dh2, 0, keepdims=True)
    dx1 = dpooled_ref[...] + norm_back(dh2, unit2, inv2, vec_ref[3:4])
    dx1_ref[...] = dx1
    da = dx1.astype(BF)
    small_ref[2:3] = jnp.sum(da.astype(F32), 0, keepdims=True)
    ctx = ctx.value()
    pick = own_columns(rank * span, width, span)
    wout_ref[...] = tn(da, nn(ctx.astype(BF), pick).astype(BF)).astype(BF)
    dctx = nt(da, wo.value()).astype(BF)
    mask = head_mask(captions, span)
    wv_ref = wv.wait()
    for g in range(n_mp):
        tall = nn(spread_heads(dctx, g, mask), wv_ref[g * span : (g + 1) * span])
        a_ref[g * per_group : (g + 1) * per_group] = tall.astype(BF).reshape(
            per_group, captions, width
        )
    prod = dctx.astype(F32) * ctx
    lse = lse.value()
    scale = 1.0 / math.sqrt(HEAD_DIM)
    tall_shape = (heads * CAP_BLOCK, width)
    of_head = (iota2(tall_shape, 0) // CAP_BLOCK) == (iota2(tall_shape, 1) // HEAD_DIM)
    at_head = (iota2(tall_shape, 0) // CAP_BLOCK) * HEAD_DIM == iota2(tall_shape, 1)
    rows_ref, qk_ref = rows_all.wait(), qk_all.wait()
    same = same_caption(heads, seq_len)
    code = own_code(packed_ref[...], rank, vocab_part)
    tall = (heads * CAP_BLOCK, width)
    blocks = range(captions // CAP_BLOCK)
    cuts = [pl.ds(block * block_rows, block_rows) for block in blocks]
    caps = [pl.ds(block * CAP_BLOCK, CAP_BLOCK) for block in blocks]
    raw = [nt(qk_ref[:, caps[block], :].reshape(tall), rows_ref[cuts[block], :]) for block in blocks]
    pulled = [nt(a_ref[:, caps[block], :].reshape(tall), rows_ref[cuts[block], :]) for block in blocks]
    probs_all, ds_all = [], []
    for block in blocks:
        low = block * CAP_BLOCK
        here = code[:, block * block_rows : (block + 1) * block_rows]
        own = jnp.logical_and(same, here > 0)
        scores = jnp.where(here > 1, raw[block], MASK_FILL)
        spread = jnp.concatenate([lse[low : low + CAP_BLOCK]] * heads, axis=0)
        log_total = jnp.sum(jnp.where(at_head, spread, 0.0), -1, keepdims=True)
        spread = jnp.concatenate([prod[low : low + CAP_BLOCK]] * heads, axis=0)
        row_sum = jnp.sum(jnp.where(of_head, spread, 0.0), -1, keepdims=True)
        probs = jnp.where(own, jnp.exp(scores - log_total), 0.0)
        dscores = (probs * (pulled[block] - row_sum)).astype(BF)
        probs = probs.astype(BF)
        probs_ref[block] = probs
        ds_ref[block] = dscores
        probs_all.append(probs)
        ds_all.append(dscores)
    for block in blocks:
        rows = rows_ref[cuts[block], :]
        t_ref[:, caps[block], :] = (
            nn(probs_all[block], rows).astype(BF).reshape(heads, CAP_BLOCK, width)
        )
        s_ref[:, caps[block], :] = (
            (nn(ds_all[block], rows) * scale).astype(BF).reshape(heads, CAP_BLOCK, width)
        )
    q = q.value()
    wk_ref = wk.wait()
    for g in range(n_mp):
        some = slice(g * per_group, (g + 1) * per_group)
        tall = s_ref[some].reshape(per_group * captions, width)
        piece = nt(tall, wk_ref[g * span : (g + 1) * span])
        dq_ref[:, g * span : (g + 1) * span] = fold_heads(piece, captions, mask).astype(BF)
        wkv_ref[g, :, :span] = tn(tall, spread_heads(q, g, mask)).astype(BF)
        tall = t_ref[some].reshape(per_group * captions, width)
        wkv_ref[g, :, span:] = tn(tall, spread_heads(dctx, g, mask)).astype(BF)
    half = sent_one.shape[0]

    def put(low, piece):
        inside = min(max(half - low, 0), piece.shape[0])
        if inside > 0:
            sent_one[low : low + inside] = piece[:inside]
        if inside < piece.shape[0]:
            sent_two[low + inside - half : low + piece.shape[0] - half] = piece[inside:]

    for g in range(0, n_mp, 2):
        at = slice(g // 2 * width, (g // 2 + 1) * width)
        first, second = wkv_ref[g], wkv_ref[g + 1]
        kept_ref[at] = jnp.where(rank % 2 == 0, first, second)
        put(g // 2 * width, jnp.where(rank % 2 == 0, second, first))
    for k in range(n_mp // 2):
        at = slice(n_mp // 2 * width + k * captions, n_mp // 2 * width + (k + 1) * captions)
        piece = dq_ref[:, 2 * k * span : 2 * (k + 1) * span]
        kept_ref[at] = piece
        put(n_mp // 2 * width + k * captions, piece)


def between_body(meta_ref, kept_ref, got_one, got_two, kept_out, sent_out):
    block = kept_ref.shape[0] - kept_out.shape[0]
    half = got_one.shape[0]

    def total(low, high):
        parts = []
        if low < half:
            parts.append(got_one[low : min(high, half)])
        if high > half:
            parts.append(got_two[max(low, half) - half : high - half])
        got = parts[0] if len(parts) == 1 else jnp.concatenate(parts, axis=0)
        return kept_ref[low:high].astype(F32) + got.astype(F32)

    first, second = total(0, block), total(block, 2 * block)
    both = total(2 * block, kept_ref.shape[0]).astype(BF)
    upper = meta_ref[0] // 2 % 2
    kept_out[:block] = jnp.where(upper == 0, first, second).astype(BF)
    sent_out[:block] = jnp.where(upper == 0, second, first).astype(BF)
    kept_out[block:] = both
    sent_out[block:] = both


def slot_body(owner_rows, n_dp, meta_ref, packed_ref, out_ref):
    rows = packed_ref.shape[1]
    side = 128
    ids, _, _ = unpack(packed_ref[...])
    owner = ids // owner_rows
    order = iota2((1, rows), 1)

    def columns(row, k):
        piece = row[:, k * side : (k + 1) * side].astype(F32)
        return jnp.transpose(jnp.broadcast_to(piece, (side, side))).astype(I32)

    def tall(column):
        return jnp.concatenate([column] * (rows // side), axis=1)

    first_at = jnp.full((1, rows), rows, I32)
    for k in range(rows // side):
        there = k * side + iota2((side, rows), 0)
        hit = jnp.where(tall(columns(ids, k)) == ids, there, rows)
        first_at = jnp.minimum(first_at, jnp.min(hit, 0, keepdims=True))
    is_first = first_at == order
    first_owner = jnp.where(is_first, owner, -1)
    slot = jnp.zeros((1, rows), I32)
    for k in range(rows // side):
        there = k * side + iota2((side, rows), 0)
        ahead = jnp.logical_and(tall(columns(first_owner, k)) == owner, there < first_at)
        slot = slot + jnp.sum(jnp.where(ahead, 1, 0), 0, keepdims=True)
    here = owner - meta_ref[0] * n_dp
    dest = jnp.where(jnp.logical_and(here >= 0, here < n_dp), here, -1)
    most = jnp.max(slot.astype(F32), 1, keepdims=True).astype(I32) + 1
    out_ref[0:1] = slot
    out_ref[1:2] = dest
    out_ref[2:3] = jnp.where(is_first, ids % owner_rows + 1, 0)
    out_ref[3:4] = jnp.broadcast_to(most, (1, rows))
    out_ref[4:8] = jnp.zeros((4, rows), I32)


def slot_sums(turn, slot_cap, seq_len, slots_ref, packed_ref, dx_ref, n_dp):
    slots = n_dp * slot_cap
    rows = dx_ref.shape[0]
    step = min(512, rows)
    captions_per_step = step // seq_len
    total, digits, pooled = None, None, []
    for low in range(0, rows, step):
        cut = slice(low, low + step)
        place = slots_ref[0:1, cut] - turn * slot_cap
        dest, row = slots_ref[1:2, cut], slots_ref[2:3, cut]
        inside = jnp.logical_and(dest >= 0, jnp.logical_and(place >= 0, place < slot_cap))
        key = jnp.where(inside, dest * slot_cap + place, -1)
        hit = jnp.where(iota2((slots, step), 0) == key, 1.0, 0.0).astype(BF)
        piece = nn(hit, dx_ref[cut])
        total = piece if total is None else total + piece
        which = iota2((16, step), 0)
        value = jnp.where(which == 0, row // NOTE_BASE, jnp.where(which == 1, row % NOTE_BASE, 0))
        piece = nt(value.astype(F32).astype(BF), hit)
        digits = piece if digits is None else digits + piece
        _, _, is_end = unpack(packed_ref[:, cut])
        caption = iota2((captions_per_step, step), 1) // seq_len
        mark = jnp.logical_and(caption == iota2((captions_per_step, step), 0), is_end)
        pooled.append(nt(hit, jnp.where(mark, 1.0, 0.0).astype(BF)))
    return total, digits, jnp.concatenate(pooled, axis=1).astype(BF)


def rows_back_body(
    slot_cap, meta_ref, probs_ref, ds_ref, a_ref, vec_ref, slots_ref, packed_ref, qk_all, unit_all, inv_all,
    dx_out, posg_ref, small_ref, seg_ref, digits_ref, pooled_ref, dx_ref, sems,
):
    blocks = probs_ref.shape[0]
    heads = a_ref.shape[0]
    seq_len, width = posg_ref.shape
    block_rows = dx_ref.shape[0] // blocks
    gain = vec_ref[0:1]
    qk_ref, unit_ref, inv_ref = qk_all.ref, unit_all.ref, inv_all.ref
    pending = []
    gain_grad = jnp.zeros((1, width), F32)
    bias_grad = jnp.zeros((1, width), F32)
    pos_grad = jnp.zeros((seq_len, width), F32)
    for block in range(blocks):
        if block % HALF == 0:
            for k in range(block, min(block + HALF, blocks)):
                qk_all.wait(k)
                unit_all.wait(k)
                inv_all.wait(k)
        caps = pl.ds(block * CAP_BLOCK, CAP_BLOCK)
        here = pl.ds(block * block_rows, block_rows)
        a = a_ref[:, caps, :].reshape(heads * CAP_BLOCK, width)
        qk = qk_ref[:, caps, :].reshape(heads * CAP_BLOCK, width)
        unit = unit_ref[here, :].astype(F32)
        drows = tn(probs_ref[block], a) + tn(ds_ref[block], qk)
        gain_grad = gain_grad + jnp.sum(drows * unit, 0, keepdims=True)
        bias_grad = bias_grad + jnp.sum(drows, 0, keepdims=True)
        dx = norm_back(drows, unit, inv_ref[here, 0:1], gain).astype(BF)
        dx_ref[here, :] = dx
        pos_grad = pos_grad + jnp.sum(dx.astype(F32).reshape(CAP_BLOCK, seq_len, width), 0)
    for block in range(blocks):
        here = pl.ds(block * block_rows, block_rows)
        copy = pltpu.make_async_copy(dx_ref.at[here], dx_out.at[here], sems.at[block])
        copy.start()
        pending.append(copy)
    small_ref[0:1] = gain_grad
    small_ref[1:2] = bias_grad
    posg_ref[...] = pos_grad
    seg_ref[...], digits_ref[...], pooled_ref[...] = slot_sums(
        0, slot_cap, seq_len, slots_ref, packed_ref, dx_ref, seg_ref.shape[0] // slot_cap
    )
    for copy in pending:
        copy.wait()


def query_back_body(
    n_mp, meta_ref, kept_ref, got_ref, wout_ref, dx1_ref, vec_ref, pos_pick_ref, own_pick_ref, slots_ref,
    seg_ref, digits_ref, pooled_ref, pos_one_ref, small_one_ref, small_two_ref, small_three_ref, x0p, wq,
    dxp_ref, send_ref, kept_out, sent_out, rest_ref, smalls_ref, all_ref,
):
    captions, width = dx1_ref.shape
    n_dp = send_ref.shape[0]
    slots = seg_ref.shape[0]
    slot_cap = slots // n_dp
    lanes = send_ref.shape[2]
    span = width // n_mp
    rank = meta_ref[0]
    total = kept_ref[...].astype(F32) + got_ref[...].astype(F32)
    all_ref[:, : 2 * span] = total[:width]
    all_ref[:, 2 * span : 3 * span] = wout_ref[...].astype(F32)
    dq = jnp.concatenate(
        [total[width + k * captions : width + (k + 1) * captions] for k in range(n_mp // 2)], axis=1
    ).astype(BF)
    gain = vec_ref[0:1]
    unit, inverse = normalize(x0p.value())
    h1 = (unit * gain + vec_ref[1:2]).astype(BF)
    owned = jnp.sum(own_pick_ref[...].astype(F32), -1, keepdims=True)
    dh1 = nn(dq, wq.value()) * owned
    dxp = (dx1_ref[...] * owned + norm_back(dh1, unit, inverse, gain)).astype(BF)
    dxp_ref[...] = dxp
    seq_len = pos_one_ref.shape[0]
    smalls_ref[...] = jnp.zeros_like(smalls_ref)
    smalls_ref[:seq_len] = pos_one_ref[...] + tn(pos_pick_ref[...], dxp)
    at = seq_len
    smalls_ref[at : at + 1] = small_three_ref[0:1] + jnp.sum(dh1 * unit, 0, keepdims=True)
    smalls_ref[at + 1 : at + 2] = small_three_ref[1:2] + jnp.sum(dh1, 0, keepdims=True)
    smalls_ref[at + 2 : at + 5] = small_two_ref[...]
    smalls_ref[at + 5 : at + 7] = small_one_ref[...]
    smalls = smalls_ref[...]
    high = smalls.astype(BF)
    low = (smalls - high.astype(F32)).astype(BF)
    all_ref[:, 3 * span :] = tn(h1, nn(dq, own_columns(rank * span, width, span)).astype(BF))
    chunk = width // n_dp
    blocks = [
        functools.partial(lambda i: all_ref[pl.ds(i * chunk, chunk), :], i) for i in range(n_dp)
    ]
    split_blocks(blocks, DOWN_BIT, meta_ref[2] // DOWN_BIT % 2, kept_out, sent_out)
    shape = (SMALLS, 2 * SMALLS)
    place = iota2(shape, 1) - iota2(shape, 0)
    rest_ref[...] = tn(high, jnp.where(place == 0, 1.0, 0.0).astype(BF)) + tn(
        low, jnp.where(place == SMALLS, 1.0, 0.0).astype(BF)
    )
    seg = (seg_ref[...] + nn(pooled_ref[...], dxp)).astype(BF)
    most = slots_ref[3:4, :lanes]
    which = iota2((NOTES, lanes), 0)
    most = jnp.where(which == 2, most // NOTE_BASE, most % NOTE_BASE).astype(F32)
    chunk = width // n_dp
    base = (width // lanes) * slot_cap
    for i in range(n_dp):
        for j in range(width // lanes):
            send_ref[i, j * slot_cap : (j + 1) * slot_cap, :] = seg[
                i * slot_cap : (i + 1) * slot_cap, j * lanes : (j + 1) * lanes
            ]
        extra = send_ref.shape[1] - NOTES
        tall = extra - base
        if 4 * tall != chunk:
            send_ref[i, base:extra, :] = jnp.zeros((tall, lanes), BF)
        for k in range(4):
            count = min(tall, chunk - k * tall)
            if count > 0:
                send_ref[i, base : base + count, k * 2 * SMALLS : (k + 1) * 2 * SMALLS] = rest_ref[
                    pl.ds(i * chunk + k * tall, count), :
                ].astype(BF)
        digits = digits_ref[:NOTES, i * slot_cap : (i + 1) * slot_cap]
        note = jnp.concatenate([digits, jnp.zeros((NOTES, lanes - slot_cap), F32)], axis=1)
        send_ref[i, extra:, :] = jnp.where(which < 2, note, most).astype(BF)


def send_body(slot_cap, meta_ref, dx_ref, dxp_ref, slots_ref, packed_ref, send_ref, digits_ref):
    n_dp, _, lanes = send_ref.shape
    width = dx_ref.shape[1]
    seq_len = dx_ref.shape[0] // dxp_ref.shape[0]
    seg, digits_ref[...], pooled = slot_sums(
        meta_ref[0], slot_cap, seq_len, slots_ref, packed_ref, dx_ref, n_dp
    )
    seg = (seg + nn(pooled, dxp_ref[...])).astype(BF)
    for i in range(n_dp):
        for j in range(width // lanes):
            send_ref[i, j * slot_cap : (j + 1) * slot_cap, :] = seg[
                i * slot_cap : (i + 1) * slot_cap, j * lanes : (j + 1) * lanes
            ]


def place_rows(row, got_ref, table_ref, slot_cap, lanes):
    n_dp = got_ref.shape[0]
    shape = (table_ref.shape[0], n_dp * slot_cap)
    hit = jnp.where(iota2(shape, 0) == row, 1.0, 0.0).astype(BF)
    for j in range(table_ref.shape[1] // lanes):
        cut = slice(j * slot_cap, (j + 1) * slot_cap)
        rows = jnp.concatenate([got_ref[i, cut, :] for i in range(n_dp)], axis=0)
        table_ref[:, j * lanes : (j + 1) * lanes] = nn(hit, rows)


def place_body(slot_cap, chunk, meta_ref, got_ref, table_ref, rest_ref, most_ref, row_ref):
    lanes = got_ref.shape[2]
    extra = got_ref.shape[1] - NOTES
    most = jnp.zeros((1, 128), F32)
    for i in range(got_ref.shape[0]):
        note = got_ref[i, extra:, :].astype(F32)
        at = slice(i * slot_cap, (i + 1) * slot_cap)
        row_ref[:, at] = note[0:1, :slot_cap] * float(NOTE_BASE) + note[1:2, :slot_cap] - 1.0
        most = jnp.maximum(most, note[2:3, :128] * float(NOTE_BASE) + note[3:4, :128])
    most_ref[...] = most
    place_rows(row_ref[...].astype(I32), got_ref, table_ref, slot_cap, lanes)
    base = table_ref.shape[1] // lanes * slot_cap
    total = got_ref[0, base:extra, :].astype(F32)
    for i in range(1, got_ref.shape[0]):
        total = total + got_ref[i, base:extra, :].astype(F32)
    for k in range(4):
        count = min(extra - base, chunk - k * (extra - base))
        if count > 0:
            cut = slice(k * 2 * SMALLS, k * 2 * SMALLS + SMALLS)
            low = slice(k * 2 * SMALLS + SMALLS, (k + 1) * 2 * SMALLS)
            at = k * (extra - base)
            rest_ref[at : at + count, :] = total[:count, cut] + total[:count, low]


def place_more_body(meta_ref, row_ref, got_ref, old_ref, table_ref):
    lanes = got_ref.shape[2]
    slot_cap = got_ref.shape[1] // (table_ref.shape[1] // lanes)
    place_rows(row_ref[...], got_ref, table_ref, slot_cap, lanes)
    table_ref[...] += old_ref[...]


def on_device(
    token_ids, lengths, images, table, pos_table, ln1_gain, ln1_bias, w_qkv, w_out, b_out,
    ln2_gain, ln2_bias, w_up, b_up, w_down, b_down, w_head,
):
    n_mp, n_dp = lax.axis_size("mp"), lax.axis_size("dp")
    mp_rank, dp_rank = lax.axis_index("mp"), lax.axis_index("dp")
    captions, seq_len = token_ids.shape
    rows = captions * seq_len
    vocab_part, width = table.shape
    heads = width // HEAD_DIM
    own_width = width // n_mp
    ff = w_up.shape[1]
    owner_rows = vocab_part // n_dp
    slot_cap = -(-rows // (n_dp * n_mp * 16)) * 16
    slots = n_dp * slot_cap
    chunk = width // n_dp
    lanes = own_width + 2 * SMALLS
    n_all = captions * n_dp
    blocks = captions // CAP_BLOCK
    meta = jnp.stack([mp_rank, dp_rank * captions, dp_rank]).astype(I32)

    gather = functools.partial(lax.all_gather, axis_name="mp", axis=0)
    turned = jnp.swapaxes(w_qkv, 1, 2)
    shard = jnp.concatenate([turned, w_out[None]])
    image_f = images.astype(F32)
    image_unit = (
        image_f * lax.rsqrt(jnp.sum(image_f * image_f, -1, keepdims=True) + EPS)
    ).astype(BF)
    all_image = lax.all_gather(image_unit, ("dp", "mp"), axis=0, tiled=True)
    at_row = jnp.arange(8)[:, None]
    vecs = b_up.astype(F32)[None, :]
    for k, vec in enumerate((ln1_gain, ln1_bias, b_out, ln2_gain, ln2_bias, b_down)):
        vecs = jnp.where(at_row == k, vec.astype(F32)[None, :], vecs)

    valid = jnp.arange(seq_len)[None, :] < lengths[:, None]
    end_pick = jnp.arange(seq_len)[None, :] == (lengths - 1)[:, None]
    pos_pick = end_pick.astype(BF)
    local2 = token_ids - mp_rank * vocab_part
    owned2 = jnp.logical_and(local2 >= 0, local2 < vocab_part)
    own_pick = jnp.logical_and(end_pick, owned2).astype(BF)
    local = token_ids.reshape(rows) - mp_rank * vocab_part
    local = after(local, image_unit)
    emb = jnp.take(table, jnp.clip(local, 0, vocab_part - 1), axis=0, mode="clip")
    packed = token_ids + jnp.where(valid, VALID_BIT, 0) + jnp.where(end_pick, END_BIT, 0)
    packed = packed.astype(I32).reshape(1, rows)
    per_head = pltpu.VMEM((heads, captions, width), BF)
    per_head = pltpu.VMEM((heads, captions, width), BF)
    row_buffer = pltpu.VMEM((rows, width), BF)
    dma = pltpu.SemaphoreType.DMA
    ends, unit_rows, unit, inverse = vmem_call(
        functools.partial(rows_body, vocab_part),
        [
            ((captions, width), BF),
            ((rows, width), BF, False),
            ((rows, width), BF, False),
            ((rows, 128), F32, False),
        ],
        meta,
        [pos_table, vecs, packed],
        [fetch(emb, blocks)],
        [row_buffer, row_buffer, pltpu.VMEM((rows, 128), F32), dma((3 * blocks,))],
        flops=WORK,
        mib=28,
    )
    shards = everyone(shard, "mp", ends)
    wq, wk, wv, wo = (fetch_weight(shards, k) for k in range(4))
    pay, qk, x0p, q = vmem_call(
        functools.partial(attend_body, vocab_part),
        [
            ((captions, width + 128), BF),
            ((heads, captions, width), BF, False),
            ((captions, width), F32, True),
            ((captions, width), BF, True),
        ],
        meta,
        [gather(ends), pos_pick, pos_table, vecs, packed],
        [wq, wk, fetch(unit_rows, blocks), wv],
        [per_head, per_head, dma((n_mp,))],
        flops=WORK,
        mib=28,
    )
    ctx, lse, x1, u, part = vmem_call(
        hidden_body,
        [
            ((captions, width), F32, True),
            ((captions, width), F32, True),
            ((captions, width), F32, True),
            ((captions, ff), F32, True),
            ((captions, width), BF),
        ],
        meta,
        [gather(pay), vecs],
        [fetch(x0p), wo, fetch(w_up), fetch(w_down)],
        flops=WORK,
        mib=20,
    )
    pooled, proj, powers, sums = vmem_call(
        logits_body,
        [
            ((captions, width), BF, True),
            ((captions, width), F32, True),
            ((captions, n_all), F32, True),
            ((n_dp, 1, n_all + 128), F32),
        ],
        meta,
        [gather(part), vecs],
        [fetch(x1), fetch(w_head), fetch(all_image)],
        flops=WORK * 5,
    )
    all_sums = lax.all_to_all(sums, "dp", 0, 0, tiled=True)
    slot_table = vmem_call(
        functools.partial(slot_body, owner_rows, n_dp),
        [((8, rows), I32)],
        meta,
        [after(packed, sums)],
        flops=WORK * 7,
        mib=20,
    )[0]
    loss, dpooled, part, du, dproj = vmem_call(
        loss_body,
        [
            ((1, 128), F32),
            ((captions, width), F32),
            ((captions, width), BF),
            ((captions, ff), BF),
            ((captions, width), BF),
        ],
        meta,
        [after(all_sums, slot_table), vecs],
        [
            fetch(powers), fetch(all_image), fetch(proj), fetch(w_head), fetch(u), fetch(w_down),
            fetch(w_up),
        ],
        flops=WORK * 5,
    )
    kind = BF if chunk % 16 == 0 else F32
    *halves, small_one = vmem_call(
        weights_body,
        [
            *[((n_dp // 2, chunk, ff + own_width), BF)] * 2,
            *[((n_dp // 2, chunk, ff), BF)] * 2,
            ((2, width), F32),
        ],
        meta,
        [vecs, dpooled, du, dproj],
        [fetch(u), fetch(x1), fetch(pooled)],
        [pltpu.VMEM((width, ff + own_width), kind), pltpu.VMEM((width, ff), kind)],
        flops=WORK * 4,
        mib=24,
    )
    dp_bits = bits_of("dp")

    def next_half(total, bits):
        total = halve(total, "dp", bits, bits[0])
        bits.pop(0)
        return total

    one_step = len(dp_bits) == 1
    down = exchange_half(*halves[:2], "dp", DOWN_BIT, one_step)
    up = exchange_half(*halves[2:], "dp", UP_BIT, one_step)
    down_bits = [bit for bit in dp_bits if bit != DOWN_BIT]
    up_bits = [bit for bit in dp_bits if bit != UP_BIT]
    for bit in bits_of("mp"):
        part = part + lax.ppermute(part, "mp", [(i, i ^ bit) for i in range(n_mp)])
    parts = part[None]
    pair_rows = n_mp // 2 * (width + captions)
    dx1, wout, kept, *sent, a, probs, dscores, small_two = vmem_call(
        functools.partial(attend_back_body, vocab_part),
        [
            ((captions, width), F32),
            ((width, own_width), BF),
            ((pair_rows, 2 * own_width), BF),
            *[((pair_rows // 2, 2 * own_width), BF)] * 2,
            ((heads, captions, width), BF),
            ((blocks, heads * CAP_BLOCK, CAP_BLOCK * seq_len), BF),
            ((blocks, heads * CAP_BLOCK, CAP_BLOCK * seq_len), BF),
            ((3, width), F32),
        ],
        meta,
        [parts, packed, vecs, dpooled],
        [
            fetch(x1), fetch(ctx), wo, wv, fetch(lse), fetch(qk, blocks, 1),
            fetch(unit_rows, blocks), wk, fetch(q),
        ],
        [
            per_head, per_head, pltpu.VMEM((n_mp, width, 2 * own_width), BF),
            pltpu.VMEM((captions, width), BF),
        ],
        flops=WORK * 13,
    )
    got = [lax.ppermute(x, "mp", [(i, i ^ 1) for i in range(n_mp)]) for x in sent]
    last_rows = pair_rows - width
    kept, sent = vmem_call(
        between_body, [((last_rows, 2 * own_width), BF)] * 2, meta, [kept, *got], flops=WORK * 2, mib=12
    )
    got = lax.ppermute(sent, "mp", [(i, i ^ 2) for i in range(n_mp)])
    dx, pos_one, small_three, seg, digits, pooled_slots = vmem_call(
        functools.partial(rows_back_body, slot_cap),
        [
            ((rows, width), BF, False),
            ((seq_len, width), F32),
            ((2, width), F32),
            ((slots, width), F32),
            ((16, slots), F32),
            ((slots, captions), BF),
        ],
        meta,
        [after(probs, sent), dscores, a, vecs, slot_table, packed],
        [fetch(qk, blocks, 1), fetch(unit, blocks), fetch(inverse, blocks)],
        [row_buffer, dma((blocks,))],
        flops=WORK * 12,
        mib=32,
    )
    down, up = next_half(down, down_bits), next_half(up, up_bits)
    rest_rows = -(-chunk // 32) * 8
    send_rows = width // lanes * slot_cap
    dxp, send, kept, sent = vmem_call(
        functools.partial(query_back_body, n_mp),
        [
            ((captions, width), BF),
            ((n_dp, send_rows + rest_rows + NOTES, lanes), BF),
            *[((n_dp // 2, chunk, 4 * own_width), BF)] * 2,
        ],
        meta,
        [
            kept, got, wout, dx1, vecs, pos_pick, own_pick, slot_table, seg, digits, pooled_slots, pos_one,
            small_one, small_two, small_three,
        ],
        [fetch(x0p), wq],
        [
            pltpu.VMEM((width, 2 * SMALLS), F32), pltpu.VMEM((SMALLS, width), F32),
            pltpu.VMEM((width, 4 * own_width), F32),
        ],
        flops=WORK * 4,
        mib=24,
    )
    got = lax.all_to_all(send, "dp", 0, 0, tiled=True)
    wkvo = exchange_half(kept, sent, "dp", DOWN_BIT, one_step)
    bits = [bit for bit in dp_bits if bit != DOWN_BIT]
    while len(bits) > 1:
        wkvo = next_half(wkvo, bits)
    while down_bits:
        down = next_half(down, down_bits)
    while up_bits:
        up = next_half(up, up_bits)
    down, up = lax.optimization_barrier((down[0], up[0]))
    table_grad, rest, most_all = vmem_call(
        functools.partial(place_body, slot_cap, chunk),
        [((owner_rows, width), F32), ((chunk, SMALLS), F32), ((1, 128), F32)],
        meta,
        [got],
        (),
        [pltpu.VMEM((1, slots), F32)],
        flops=WORK * 3,
        mib=20,
    )
    most_all = most_all[0, 0].astype(I32)
    small = rest
    last = gather(jnp.concatenate([down[:, ff:], small, jnp.zeros_like(small)], 1))
    wkvo = lax.optimization_barrier(next_half(wkvo, bits)[0])

    def another(carry):
        turn, total = carry
        sent, digits = vmem_call(
            functools.partial(send_body, slot_cap),
            [((n_dp, send_rows, lanes), BF), ((16, slots), F32)],
            turn.reshape(1),
            [dx, dxp, slot_table, packed],
        )
        row = (digits[0] * NOTE_BASE + digits[1] - 1.0).astype(I32)
        row = lax.all_to_all(row.reshape(n_dp, slot_cap), "dp", 0, 0, tiled=True)
        sent = lax.all_to_all(sent, "dp", 0, 0, tiled=True)
        total = vmem_call(
            place_more_body,
            [((owner_rows, width), F32)],
            meta,
            [row.reshape(1, slots), sent, total],
        )[0]
        return turn + 1, total

    _, table_grad = lax.while_loop(
        lambda carry: carry[0] * slot_cap < most_all, another, (jnp.int32(1), table_grad)
    )
    w_head_grad = jnp.swapaxes(last[:, :, :own_width], 0, 1).reshape(chunk, width)
    shared = jnp.sum(last[:, :, own_width : own_width + SMALLS], 0)
    qkv_grad = jnp.stack(
        [wkvo[:, k * own_width : (k + 1) * own_width] for k in (3, 0, 1)]
    )
    return (
        loss[0, 0],
        table_grad,
        shared[:, :seq_len].T,
        shared[:, seq_len],
        shared[:, seq_len + 1],
        qkv_grad,
        wkvo[:, 2 * own_width : 3 * own_width].T,
        small[:, seq_len + 4],
        small[:, seq_len + 2],
        small[:, seq_len + 3],
        up,
        small[:, seq_len + 6],
        down[:, :ff].T,
        small[:, seq_len + 5],
        w_head_grad,
    )


def solution(mesh):
    placed = (
        P("dp", None),
        P("dp"),
        P(("dp", "mp"), None),
        P("mp", None),
        P(),
        P(),
        P(),
        P(None, None, "mp"),
        P("mp", None),
        P(),
        P(),
        P(),
        P(None, "mp"),
        P("mp"),
        P("mp", None),
        P(),
        P(),
    )
    return jax.shard_map(
        on_device,
        mesh=mesh,
        in_specs=placed,
        out_specs=(
            P(),
            P(("mp", "dp"), None),
            P(None, "dp"),
            P("dp"),
            P("dp"),
            P(None, "dp", "mp"),
            P("mp", "dp"),
            P("dp"),
            P("dp"),
            P("dp"),
            P("dp", "mp"),
            P(("mp", "dp")),
            P("mp", "dp"),
            P("dp"),
            P("dp", None),
        ),
        check_vma=False,
    )
```

```python
import functools
import math

import jax
import jax.numpy as jnp
from jax import lax
from jax.experimental import pallas as pl
from jax.experimental.pallas import tpu as pltpu
from jax.sharding import PartitionSpec as P

HEAD_DIM = 64
LOGIT_SCALE = 50.0
EPS = 1e-06
MASK_FILL = -1000000000.0
NO_KEY = -1e30
BF = jnp.bfloat16
F32 = jnp.float32
I32 = jnp.int32
GELU_C = math.sqrt(2.0 / math.pi)
CAP_BLOCK = 16
SMALLS = 32
NOTES = 8
HALF = 4
VALID_BIT = 1 << 20
END_BIT = 1 << 21
NOTE_BASE = 32
WORK = 920000000
DOWN_BIT = 1
UP_BIT = 2


def nn(a, b):
    return lax.dot_general(a, b, (((1,), (0,)), ((), ())), preferred_element_type=F32)


def nt(a, b):
    return lax.dot_general(a, b, (((1,), (1,)), ((), ())), preferred_element_type=F32)


def tn(a, b):
    return lax.dot_general(a, b, (((0,), (0,)), ((), ())), preferred_element_type=F32)


def normalize(rows):
    centred = rows - jnp.mean(rows, -1, keepdims=True)
    inverse = lax.rsqrt(jnp.mean(centred * centred, -1, keepdims=True) + EPS)
    return centred * inverse, inverse


def norm_back(upstream, unit, inverse, gain):
    scaled = upstream * gain
    mean_scaled = jnp.mean(scaled, -1, keepdims=True)
    mean_unit = jnp.mean(scaled * unit, -1, keepdims=True)
    return inverse * (scaled - mean_scaled - unit * mean_unit)


def iota2(shape, dim):
    return lax.broadcasted_iota(I32, shape, dim)


class Late:
    def __init__(self, ref, pairs, sems):
        self.ref = ref
        self.copies = [
            pltpu.make_async_copy(src, dst, sem) for (src, dst), sem in zip(pairs, sems)
        ]
        self.waiting = set(range(len(self.copies)))

    def start(self):
        for copy in self.copies:
            copy.start()

    def wait(self, part=None):
        for k in sorted(self.waiting) if part is None else [part]:
            if k in self.waiting:
                self.copies[k].wait()
                self.waiting.discard(k)
        return self.ref

    def value(self):
        return self.wait()[...]


def fetch(array, parts=1, axis=0):
    return ("blocks", [array], parts, axis)


def fetch_weight(shards, which):
    return ("weight", list(shards), which, 0)


def vmem_call(body, outs, meta, args, late=(), scratch=(), flops=1, mib=40):
    vmem = pl.BlockSpec(memory_space=pltpu.VMEM)
    hbm = pl.BlockSpec(memory_space=pltpu.HBM)
    sources, buffers, counts = [], [], []
    for kind, arrays, parts, axis in late:
        sources += arrays
        if kind == "weight":
            _, rows, width = arrays[0].shape
            buffers.append(pltpu.VMEM((rows * len(arrays), width), arrays[0].dtype))
            counts.append(len(arrays))
        else:
            buffers.append(pltpu.VMEM(arrays[0].shape, arrays[0].dtype))
            counts.append(parts)

    staged = [k for k, o in enumerate(outs) if len(o) > 2 and o[2]]

    def kernel(meta_ref, *refs):
        arg_refs, refs = refs[: len(args)], refs[len(args) :]
        source_refs, refs = refs[: len(sources)], refs[len(sources) :]
        out_refs, refs = refs[: len(outs)], refs[len(outs) :]
        buffer_refs, refs = refs[: len(buffers)], refs[len(buffers) :]
        sems, stage_sems, refs = refs[0], refs[1], refs[2:]
        stages, refs = refs[: len(staged)], refs[len(staged) :]
        targets = list(out_refs)
        for k, stage in zip(staged, stages):
            targets[k] = stage
        handles, at, place = [], 0, 0
        for (kind, arrays, parts, axis), buffer in zip(late, buffer_refs):
            if kind == "weight":
                rows = arrays[0].shape[1]
                pairs = []
                for k in range(len(arrays)):
                    low = pl.multiple_of((meta_ref[0] ^ k) * rows, rows)
                    pairs.append((source_refs[place + k].at[parts], buffer.at[pl.ds(low, rows)]))
                place += len(arrays)
            else:
                size = arrays[0].shape[axis] // parts
                pairs = []
                for k in range(parts):
                    cut = (slice(None),) * axis + (pl.ds(k * size, size),)
                    pairs.append((source_refs[place].at[cut], buffer.at[cut]))
                place += 1
            handles.append(Late(buffer, pairs, [sems.at[at + k] for k in range(len(pairs))]))
            at += len(pairs)
        for handle in handles:
            handle.start()
        body(meta_ref, *arg_refs, *handles, *targets, *refs)
        copies = [
            pltpu.make_async_copy(stage, out_refs[k], stage_sems.at[i])
            for i, (k, stage) in enumerate(zip(staged, stages))
        ]
        for copy in copies:
            copy.start()
        for handle in handles:
            handle.wait()
        for copy in copies:
            copy.wait()

    return pl.pallas_call(
        kernel,
        out_shape=[
            pltpu.HBM(*o[:2]) if len(o) > 2 else jax.ShapeDtypeStruct(*o) for o in outs
        ],
        in_specs=[pl.BlockSpec(memory_space=pltpu.SMEM)]
        + [vmem] * len(args)
        + [hbm] * len(sources),
        out_specs=[hbm if len(o) > 2 else vmem for o in outs],
        scratch_shapes=[
            *buffers,
            pltpu.SemaphoreType.DMA((max(1, sum(counts)),)),
            pltpu.SemaphoreType.DMA((max(1, len(staged)),)),
            *(pltpu.VMEM(*outs[k][:2]) for k in staged),
            *scratch,
        ],
        compiler_params=pltpu.CompilerParams(vmem_limit_bytes=mib << 20),
        cost_estimate=pl.CostEstimate(flops=flops, bytes_accessed=1, transcendentals=0),
    )(meta, *args, *(pltpu.with_memory_space_constraint(x, pltpu.HBM) for x in sources))


def exchange_half(kept, sent, axis, bit, last):
    count = lax.axis_size(axis)
    got = lax.ppermute(sent, axis, [(i, i ^ bit) for i in range(count)])
    total = kept.astype(F32) + got.astype(F32)
    return total if last else total.astype(BF)


def halve(total, axis, bits, bit, hold=None):
    low = 1 << bits.index(bit)
    pairs = total.reshape((total.shape[0] // (2 * low), 2, low) + total.shape[1:])
    shape = (total.shape[0] // 2,) + total.shape[1:]
    mine = (lax.axis_index(axis) // bit) % 2
    sent = lax.dynamic_index_in_dim(pairs, 1 - mine, 1, keepdims=False).reshape(shape)
    kept = lax.dynamic_index_in_dim(pairs, mine, 1, keepdims=False).reshape(shape)
    if hold is not None:
        kept = after(kept, hold)
    return exchange_half(kept, sent, axis, bit, len(bits) == 1)


def split_blocks(blocks, bit, mine, kept_ref, sent_ref):
    place = 0
    for i in range(len(blocks)):
        if i & bit == 0:
            first, second = blocks[i](), blocks[i | bit]()
            kept_ref[place] = jnp.where(mine == 0, first, second).astype(BF)
            sent_ref[place] = jnp.where(mine == 0, second, first).astype(BF)
            place += 1


def bits_of(axis):
    count = lax.axis_size(axis)
    return [1 << k for k in range(count.bit_length() - 1)]


def after(x, *others):
    return lax.optimization_barrier((x, others))[0]


def everyone(x, axis, before):
    count = lax.axis_size(axis)
    have = {0: x}
    bit = count // 2
    while bit:
        pairs = [(i, i ^ bit) for i in range(count)]
        for k, v in list(have.items()):
            have[k | bit] = lax.ppermute(after(v, before) if k else v, axis, pairs)
        bit //= 2
    return [have[k] for k in range(count)]


def own_columns(start, width, own_width):
    shape = (width, own_width)
    hit = iota2(shape, 0) == start + iota2(shape, 1)
    return jnp.where(hit, 1.0, 0.0).astype(BF)


def unpack(packed):
    return packed % VALID_BIT, packed // VALID_BIT % 2 > 0, packed // END_BIT > 0


def own_code(packed, rank, vocab_part):
    ids, valid, _ = unpack(packed)
    return jnp.where(ids // vocab_part == rank, jnp.where(valid, 2, 1), 0)


def head_mask(captions, span):
    shape = (span // HEAD_DIM * captions, span)
    return (iota2(shape, 0) // captions) == (iota2(shape, 1) // HEAD_DIM)


def spread_heads(rows, group, mask):
    span = mask.shape[1]
    part = rows[:, group * span : (group + 1) * span].astype(F32)
    tall = jnp.concatenate([part] * (span // HEAD_DIM), axis=0)
    return jnp.where(mask, tall, 0.0).astype(BF)


def fold_heads(tall, captions, mask):
    kept = jnp.where(mask, tall, 0.0)
    total = kept[:captions]
    for h in range(1, tall.shape[0] // captions):
        total = total + kept[h * captions : (h + 1) * captions]
    return total


def same_caption(heads, seq_len):
    shape = (heads * CAP_BLOCK, CAP_BLOCK * seq_len)
    return (iota2(shape, 0) % CAP_BLOCK) == (iota2(shape, 1) // seq_len)


def rows_body(
    vocab_part, meta_ref, pos_ref, vec_ref, packed_ref, emb,
    end_ref, rows_out, unit_out, inv_out, rows_ref, unit_ref, inv_ref, sems,
):
    captions = end_ref.shape[0]
    seq_len = pos_ref.shape[0]
    block_rows = CAP_BLOCK * seq_len
    gain, bias = vec_ref[0:1], vec_ref[1:2]
    pos = jnp.concatenate([pos_ref[...].astype(F32)] * CAP_BLOCK, axis=0)
    pending = []

    def write_back(src, dst):
        copy = pltpu.make_async_copy(src, dst, sems.at[len(pending)])
        copy.start()
        pending.append(copy)

    blocks = captions // CAP_BLOCK
    for block in range(blocks):
        here = pl.ds(block * block_rows, block_rows)
        if block % HALF == 0:
            for k in range(block, min(block + HALF, blocks)):
                emb.wait(k)
        packed = packed_ref[:, block * block_rows : (block + 1) * block_rows]
        low = emb.ref[here, :]
        ids, _, is_end = unpack(packed)
        shape = (CAP_BLOCK, block_rows)
        mark = jnp.logical_and(is_end, ids // vocab_part == meta_ref[0])
        mark = jnp.logical_and(iota2(shape, 0) == iota2(shape, 1) // seq_len, mark)
        ends = nn(jnp.where(mark, 1.0, 0.0).astype(BF), low)
        end_ref[block * CAP_BLOCK : (block + 1) * CAP_BLOCK] = ends.astype(BF)
        unit, inverse = normalize(low.astype(F32) + pos)
        unit_ref[here, :] = unit.astype(BF)
        inv_ref[here, :] = jnp.broadcast_to(inverse, (block_rows, 128))
        rows_ref[here, :] = (unit * gain + bias).astype(BF)
        if block % HALF == HALF - 1 or block == blocks - 1:
            low_row = block // HALF * HALF * block_rows
            done = pl.ds(low_row, (block + 1) * block_rows - low_row)
            write_back(unit_ref.at[done], unit_out.at[done])
            write_back(inv_ref.at[done], inv_out.at[done])
            write_back(rows_ref.at[done], rows_out.at[done])
    for copy in pending:
        copy.wait()


def attend_body(
    vocab_part, meta_ref, ends_ref, pos_pick_ref, pos_ref, vec_ref, packed_ref, wq, wk, rows_all, wv,
    pay_ref, qk_out, x0p_ref, q_ref, qk_ref, t_ref, sems,
):
    n_mp = ends_ref.shape[0]
    captions, width = x0p_ref.shape
    heads = width // HEAD_DIM
    span = width // n_mp
    per_group = span // HEAD_DIM
    seq_len = pos_ref.shape[0]
    block_rows = CAP_BLOCK * seq_len
    gain, bias = vec_ref[0:1], vec_ref[1:2]
    pooled_in = nn(pos_pick_ref[...], pos_ref[...])
    for i in range(n_mp):
        pooled_in = pooled_in + ends_ref[i].astype(F32)
    pending = []
    x0p_ref[...] = pooled_in
    unit, _ = normalize(pooled_in)
    q = nt((unit * gain + bias).astype(BF), wq.value()).astype(BF)
    q_ref[...] = q
    mask = head_mask(captions, span)
    scale = 1.0 / math.sqrt(HEAD_DIM)
    wk_ref = wk.wait()
    for g in range(n_mp):
        some = slice(g * per_group, (g + 1) * per_group)
        tall = nn(spread_heads(q, g, mask), wk_ref[g * span : (g + 1) * span]) * scale
        qk_ref[some] = tall.astype(BF).reshape(per_group, captions, width)
        copy = pltpu.make_async_copy(qk_ref.at[some], qk_out.at[some], sems.at[g])
        copy.start()
        pending.append(copy)
    lane = iota2((heads, CAP_BLOCK, 128), 2)
    head_of = iota2((heads, CAP_BLOCK, 128), 0)
    rows_ref = rows_all.wait()
    blocks = range(captions // CAP_BLOCK)
    cuts = [pl.ds(block * block_rows, block_rows) for block in blocks]
    caps = [pl.ds(block * CAP_BLOCK, CAP_BLOCK) for block in blocks]
    raw = [
        nt(qk_ref[:, caps[block], :].reshape(heads * CAP_BLOCK, width), rows_ref[cuts[block], :])
        for block in blocks
    ]
    same = same_caption(heads, seq_len)
    code = own_code(packed_ref[...], meta_ref[0], vocab_part)
    log_totals, weights = [], []
    for block in blocks:
        here = code[:, block * block_rows : (block + 1) * block_rows]
        own = jnp.logical_and(same, here > 0)
        scores = jnp.where(own, jnp.where(here > 1, raw[block], MASK_FILL), NO_KEY)
        top = jnp.max(scores, -1, keepdims=True)
        power = jnp.where(own, jnp.exp(scores - top), 0.0)
        total = jnp.sum(power, -1, keepdims=True)
        some = total > 0.0
        total = jnp.where(some, total, 1.0)
        log_totals.append(jnp.where(some, top + jnp.log(total), NO_KEY))
        weights.append((power * (1.0 / total)).astype(BF))
    for block in blocks:
        mixed = nn(weights[block], rows_ref[cuts[block], :])
        t_ref[:, caps[block], :] = mixed.astype(BF).reshape(heads, CAP_BLOCK, width)
    for block in blocks:
        log_total = log_totals[block]
        first = log_total.astype(BF).astype(F32)
        second = (log_total - first).astype(BF).astype(F32)
        third = log_total - first - second
        stat = jnp.zeros((heads, CAP_BLOCK, 128), F32)
        for k, piece in enumerate((first, second, third)):
            stat = stat + jnp.where(
                lane == head_of + 16 * k, piece.reshape(heads, CAP_BLOCK, 1), 0.0
            )
        pay_ref[caps[block], width:] = jnp.sum(stat, 0).astype(BF)
    wv_ref = wv.wait()
    for g in range(n_mp):
        tall = t_ref[g * per_group : (g + 1) * per_group].reshape(per_group * captions, width)
        piece = nt(tall, wv_ref[g * span : (g + 1) * span])
        pay_ref[:, g * span : (g + 1) * span] = fold_heads(piece, captions, mask).astype(BF)
    for copy in pending:
        copy.wait()


def hidden_body(
    meta_ref, pay_ref, vec_ref, x0p, wo, wup, wdown,
    ctx_ref, lse_ref, x1_ref, u_ref, part_ref,
):
    n_mp = pay_ref.shape[0]
    captions, width = ctx_ref.shape
    shape = (128, width)
    stat_row, head = iota2(shape, 0), iota2(shape, 1) // HEAD_DIM
    picks = jnp.logical_and(stat_row % 16 == head, stat_row < 48)
    expand = jnp.where(picks, 1.0, 0.0).astype(BF)
    logs = [nn(pay_ref[i, :, width:], expand) for i in range(n_mp)]
    top = functools.reduce(jnp.maximum, logs)
    total = jnp.zeros_like(top)
    ctx = jnp.zeros_like(top)
    for i in range(n_mp):
        weight = jnp.exp(logs[i] - top)
        total = total + weight
        ctx = ctx + weight * pay_ref[i, :, :width].astype(F32)
    ctx = ctx / total
    ctx_ref[...] = ctx
    lse_ref[...] = top + jnp.log(total)
    x1 = x0p.value() + nn(ctx.astype(BF), wo.value()) + vec_ref[2:3]
    x1_ref[...] = x1
    unit, _ = normalize(x1)
    h2 = (unit * vec_ref[3:4] + vec_ref[4:5]).astype(BF)
    u = nn(h2, wup.value()) + vec_ref[6:7]
    u_ref[...] = u
    hidden = (0.5 * u * (1.0 + jnp.tanh(GELU_C * (u + 0.044715 * u * u * u)))).astype(BF)
    part_ref[...] = nn(hidden, wdown.value()).astype(BF)


def logits_body(
    meta_ref, parts_ref, vec_ref, x1, wh, images,
    pooled_ref, proj_ref, e_ref, sums_ref,
):
    x2 = x1.value() + vec_ref[5:6]
    for i in range(parts_ref.shape[0]):
        x2 = x2 + parts_ref[i].astype(F32)
    pooled = x2.astype(BF)
    pooled_ref[...] = pooled
    proj = nn(pooled, wh.value())
    proj_ref[...] = proj
    text = (proj * lax.rsqrt(jnp.sum(proj * proj, -1, keepdims=True) + EPS)).astype(BF)
    logits = LOGIT_SCALE * nt(text, images.value())
    powers = jnp.exp(logits)
    e_ref[...] = powers
    n_all = powers.shape[1]
    is_diag = iota2(logits.shape, 1) == meta_ref[1] + iota2(logits.shape, 0)
    rows = jnp.log(jnp.sum(powers, -1, keepdims=True))
    rows = rows - 2.0 * jnp.sum(jnp.where(is_diag, logits, 0.0), -1, keepdims=True)
    cols = jnp.sum(powers, 0, keepdims=True)
    rows = jnp.broadcast_to(jnp.sum(rows, 0, keepdims=True), (1, 128))
    for i in range(sums_ref.shape[0]):
        sums_ref[i, :, :n_all] = cols
        sums_ref[i, :, n_all:] = rows


def loss_body(
    meta_ref, sums_ref, vec_ref, e, images, proj, wh, u, wdown, wup,
    loss_ref, dpooled_ref, part_ref, du_ref, dproj_ref,
):
    sums = jnp.sum(sums_ref[...], 0)
    n_all = sums.shape[1] - 128
    cols = sums[:, :n_all]
    loss = jnp.sum(jnp.log(cols), -1, keepdims=True) + sums[:, n_all : n_all + 1]
    loss_ref[...] = jnp.broadcast_to(loss * (0.5 / n_all), (1, 128))
    powers = e.value()
    row_inv = 1.0 / jnp.sum(powers, -1, keepdims=True)
    is_diag = iota2(powers.shape, 1) == meta_ref[1] + iota2(powers.shape, 0)
    grad = powers * row_inv + powers * (1.0 / cols) - jnp.where(is_diag, 2.0, 0.0)
    grad = (grad * (0.5 / n_all)).astype(BF)
    dtext = LOGIT_SCALE * nn(grad, images.value())
    proj = proj.value()
    inv = lax.rsqrt(jnp.sum(proj * proj, -1, keepdims=True) + EPS)
    along = jnp.sum(proj * dtext, -1, keepdims=True)
    dproj = (inv * dtext - inv * inv * inv * proj * along).astype(BF)
    dproj_ref[...] = dproj
    dpooled = nt(dproj, wh.value())
    dpooled_ref[...] = dpooled
    u = u.value()
    th = jnp.tanh(GELU_C * (u + 0.044715 * u * u * u))
    slope = 0.5 * (1.0 + th) + 0.5 * u * (1.0 - th * th) * (
        GELU_C * (1.0 + 3.0 * 0.044715 * u * u)
    )
    du = (nt(dpooled.astype(BF), wdown.value()) * slope).astype(BF)
    du_ref[...] = du
    part_ref[...] = nt(du, wup.value()).astype(BF)


def weights_body(
    meta_ref, vec_ref, dpooled_ref, du_ref, dproj_ref, u, x1, pooled,
    down_kept, down_sent, up_kept, up_sent, small_ref, down_ref, up_ref,
):
    width = dpooled_ref.shape[1]
    dy, du, dproj = dpooled_ref[...].astype(BF), du_ref[...], dproj_ref[...]
    u = u.value()
    th = jnp.tanh(GELU_C * (u + 0.044715 * u * u * u))
    hidden = (0.5 * u * (1.0 + th)).astype(BF)
    unit, _ = normalize(x1.value())
    h2 = (unit * vec_ref[3:4] + vec_ref[4:5]).astype(BF)
    ff = u.shape[1]
    own_width = down_ref.shape[1] - ff
    pick = own_columns(meta_ref[0] * own_width, width, own_width)
    kind = down_ref.dtype
    down_ref[:, :ff] = tn(dy, hidden).astype(kind)
    up_ref[...] = tn(h2, du).astype(kind)
    down_ref[:, ff:] = tn(pooled.value(), nn(dproj, pick).astype(BF)).astype(kind)
    chunk = down_kept.shape[1]
    n_dp = 2 * down_kept.shape[0]
    for ref, bit, kept, sent in (
        (down_ref, DOWN_BIT, down_kept, down_sent),
        (up_ref, UP_BIT, up_kept, up_sent),
    ):
        blocks = [
            functools.partial(lambda ref, i: ref[pl.ds(i * chunk, chunk), :], ref, i)
            for i in range(n_dp)
        ]
        split_blocks(blocks, bit, meta_ref[2] // bit % 2, kept, sent)
    small_ref[0:1] = jnp.sum(dy.astype(F32), 0, keepdims=True)
    small_ref[1:2] = jnp.sum(du.astype(F32), 0, keepdims=True)


def attend_back_body(
    vocab_part, meta_ref, parts_ref, packed_ref, vec_ref, dpooled_ref, x1, ctx, wo, wv, lse, qk_all, rows_all, wk, q,
    dx1_ref, wout_ref, kept_ref, sent_one, sent_two, a_ref, probs_ref, ds_ref, small_ref,
    t_ref, s_ref, wkv_ref, dq_ref,
):
    n_mp = wkv_ref.shape[0]
    captions, width = dpooled_ref.shape
    heads = width // HEAD_DIM
    span = width // n_mp
    per_group = span // HEAD_DIM
    block_rows = rows_all.ref.shape[0] // (captions // CAP_BLOCK)
    seq_len = block_rows // CAP_BLOCK
    rank = meta_ref[0]
    dh2 = parts_ref[0].astype(F32)
    for i in range(1, parts_ref.shape[0]):
        dh2 = dh2 + parts_ref[i].astype(F32)
    unit2, inv2 = normalize(x1.value())
    small_ref[0:1] = jnp.sum(dh2 * unit2, 0, keepdims=True)
    small_ref[1:2] = jnp.sum(dh2, 0, keepdims=True)
    dx1 = dpooled_ref[...] + norm_back(dh2, unit2, inv2, vec_ref[3:4])
    dx1_ref[...] = dx1
    da = dx1.astype(BF)
    small_ref[2:3] = jnp.sum(da.astype(F32), 0, keepdims=True)
    ctx = ctx.value()
    pick = own_columns(rank * span, width, span)
    wout_ref[...] = tn(da, nn(ctx.astype(BF), pick).astype(BF)).astype(BF)
    dctx = nt(da, wo.value()).astype(BF)
    mask = head_mask(captions, span)
    wv_ref = wv.wait()
    for g in range(n_mp):
        tall = nn(spread_heads(dctx, g, mask), wv_ref[g * span : (g + 1) * span])
        a_ref[g * per_group : (g + 1) * per_group] = tall.astype(BF).reshape(
            per_group, captions, width
        )
    prod = dctx.astype(F32) * ctx
    lse = lse.value()
    scale = 1.0 / math.sqrt(HEAD_DIM)
    tall_shape = (heads * CAP_BLOCK, width)
    of_head = (iota2(tall_shape, 0) // CAP_BLOCK) == (iota2(tall_shape, 1) // HEAD_DIM)
    at_head = (iota2(tall_shape, 0) // CAP_BLOCK) * HEAD_DIM == iota2(tall_shape, 1)
    rows_ref, qk_ref = rows_all.wait(), qk_all.wait()
    same = same_caption(heads, seq_len)
    code = own_code(packed_ref[...], rank, vocab_part)
    tall = (heads * CAP_BLOCK, width)
    blocks = range(captions // CAP_BLOCK)
    cuts = [pl.ds(block * block_rows, block_rows) for block in blocks]
    caps = [pl.ds(block * CAP_BLOCK, CAP_BLOCK) for block in blocks]
    raw = [nt(qk_ref[:, caps[block], :].reshape(tall), rows_ref[cuts[block], :]) for block in blocks]
    pulled = [nt(a_ref[:, caps[block], :].reshape(tall), rows_ref[cuts[block], :]) for block in blocks]
    probs_all, ds_all = [], []
    for block in blocks:
        low = block * CAP_BLOCK
        here = code[:, block * block_rows : (block + 1) * block_rows]
        own = jnp.logical_and(same, here > 0)
        scores = jnp.where(here > 1, raw[block], MASK_FILL)
        spread = jnp.concatenate([lse[low : low + CAP_BLOCK]] * heads, axis=0)
        log_total = jnp.sum(jnp.where(at_head, spread, 0.0), -1, keepdims=True)
        spread = jnp.concatenate([prod[low : low + CAP_BLOCK]] * heads, axis=0)
        row_sum = jnp.sum(jnp.where(of_head, spread, 0.0), -1, keepdims=True)
        probs = jnp.where(own, jnp.exp(scores - log_total), 0.0)
        dscores = (probs * (pulled[block] - row_sum)).astype(BF)
        probs = probs.astype(BF)
        probs_ref[block] = probs
        ds_ref[block] = dscores
        probs_all.append(probs)
        ds_all.append(dscores)
    for block in blocks:
        rows = rows_ref[cuts[block], :]
        t_ref[:, caps[block], :] = (
            nn(probs_all[block], rows).astype(BF).reshape(heads, CAP_BLOCK, width)
        )
        s_ref[:, caps[block], :] = (
            (nn(ds_all[block], rows) * scale).astype(BF).reshape(heads, CAP_BLOCK, width)
        )
    q = q.value()
    wk_ref = wk.wait()
    for g in range(n_mp):
        some = slice(g * per_group, (g + 1) * per_group)
        tall = s_ref[some].reshape(per_group * captions, width)
        piece = nt(tall, wk_ref[g * span : (g + 1) * span])
        dq_ref[:, g * span : (g + 1) * span] = fold_heads(piece, captions, mask).astype(BF)
        wkv_ref[g, :, :span] = tn(tall, spread_heads(q, g, mask)).astype(BF)
        tall = t_ref[some].reshape(per_group * captions, width)
        wkv_ref[g, :, span:] = tn(tall, spread_heads(dctx, g, mask)).astype(BF)
    half = sent_one.shape[0]

    def put(low, piece):
        inside = min(max(half - low, 0), piece.shape[0])
        if inside > 0:
            sent_one[low : low + inside] = piece[:inside]
        if inside < piece.shape[0]:
            sent_two[low + inside - half : low + piece.shape[0] - half] = piece[inside:]

    for g in range(0, n_mp, 2):
        at = slice(g // 2 * width, (g // 2 + 1) * width)
        first, second = wkv_ref[g], wkv_ref[g + 1]
        kept_ref[at] = jnp.where(rank % 2 == 0, first, second)
        put(g // 2 * width, jnp.where(rank % 2 == 0, second, first))
    for k in range(n_mp // 2):
        at = slice(n_mp // 2 * width + k * captions, n_mp // 2 * width + (k + 1) * captions)
        piece = dq_ref[:, 2 * k * span : 2 * (k + 1) * span]
        kept_ref[at] = piece
        put(n_mp // 2 * width + k * captions, piece)


def between_body(meta_ref, kept_ref, got_one, got_two, kept_out, sent_out):
    block = kept_ref.shape[0] - kept_out.shape[0]
    half = got_one.shape[0]

    def total(low, high):
        parts = []
        if low < half:
            parts.append(got_one[low : min(high, half)])
        if high > half:
            parts.append(got_two[max(low, half) - half : high - half])
        got = parts[0] if len(parts) == 1 else jnp.concatenate(parts, axis=0)
        return kept_ref[low:high].astype(F32) + got.astype(F32)

    first, second = total(0, block), total(block, 2 * block)
    both = total(2 * block, kept_ref.shape[0]).astype(BF)
    upper = meta_ref[0] // 2 % 2
    kept_out[:block] = jnp.where(upper == 0, first, second).astype(BF)
    sent_out[:block] = jnp.where(upper == 0, second, first).astype(BF)
    kept_out[block:] = both
    sent_out[block:] = both


def slot_body(owner_rows, n_dp, meta_ref, packed_ref, out_ref):
    rows = packed_ref.shape[1]
    side = 128
    ids, _, _ = unpack(packed_ref[...])
    owner = ids // owner_rows
    order = iota2((1, rows), 1)

    def columns(row, k):
        piece = row[:, k * side : (k + 1) * side].astype(F32)
        return jnp.transpose(jnp.broadcast_to(piece, (side, side))).astype(I32)

    def tall(column):
        return jnp.concatenate([column] * (rows // side), axis=1)

    first_at = jnp.full((1, rows), rows, I32)
    for k in range(rows // side):
        there = k * side + iota2((side, rows), 0)
        hit = jnp.where(tall(columns(ids, k)) == ids, there, rows)
        first_at = jnp.minimum(first_at, jnp.min(hit, 0, keepdims=True))
    is_first = first_at == order
    first_owner = jnp.where(is_first, owner, -1)
    slot = jnp.zeros((1, rows), I32)
    for k in range(rows // side):
        there = k * side + iota2((side, rows), 0)
        ahead = jnp.logical_and(tall(columns(first_owner, k)) == owner, there < first_at)
        slot = slot + jnp.sum(jnp.where(ahead, 1, 0), 0, keepdims=True)
    here = owner - meta_ref[0] * n_dp
    dest = jnp.where(jnp.logical_and(here >= 0, here < n_dp), here, -1)
    most = jnp.max(slot.astype(F32), 1, keepdims=True).astype(I32) + 1
    out_ref[0:1] = slot
    out_ref[1:2] = dest
    out_ref[2:3] = jnp.where(is_first, ids % owner_rows + 1, 0)
    out_ref[3:4] = jnp.broadcast_to(most, (1, rows))
    out_ref[4:8] = jnp.zeros((4, rows), I32)


def slot_sums(turn, slot_cap, seq_len, slots_ref, packed_ref, dx_ref, n_dp):
    slots = n_dp * slot_cap
    rows = dx_ref.shape[0]
    step = min(512, rows)
    captions_per_step = step // seq_len
    total, digits, pooled = None, None, []
    for low in range(0, rows, step):
        cut = slice(low, low + step)
        place = slots_ref[0:1, cut] - turn * slot_cap
        dest, row = slots_ref[1:2, cut], slots_ref[2:3, cut]
        inside = jnp.logical_and(dest >= 0, jnp.logical_and(place >= 0, place < slot_cap))
        key = jnp.where(inside, dest * slot_cap + place, -1)
        hit = jnp.where(iota2((slots, step), 0) == key, 1.0, 0.0).astype(BF)
        piece = nn(hit, dx_ref[cut])
        total = piece if total is None else total + piece
        which = iota2((16, step), 0)
        value = jnp.where(which == 0, row // NOTE_BASE, jnp.where(which == 1, row % NOTE_BASE, 0))
        piece = nt(value.astype(F32).astype(BF), hit)
        digits = piece if digits is None else digits + piece
        _, _, is_end = unpack(packed_ref[:, cut])
        caption = iota2((captions_per_step, step), 1) // seq_len
        mark = jnp.logical_and(caption == iota2((captions_per_step, step), 0), is_end)
        pooled.append(nt(hit, jnp.where(mark, 1.0, 0.0).astype(BF)))
    return total, digits, jnp.concatenate(pooled, axis=1).astype(BF)


def rows_back_body(
    slot_cap, meta_ref, probs_ref, ds_ref, a_ref, vec_ref, slots_ref, packed_ref, qk_all, unit_all, inv_all,
    dx_out, posg_ref, small_ref, seg_ref, digits_ref, pooled_ref, dx_ref, sems,
):
    blocks = probs_ref.shape[0]
    heads = a_ref.shape[0]
    seq_len, width = posg_ref.shape
    block_rows = dx_ref.shape[0] // blocks
    gain = vec_ref[0:1]
    qk_ref, unit_ref, inv_ref = qk_all.ref, unit_all.ref, inv_all.ref
    pending = []
    gain_grad = jnp.zeros((1, width), F32)
    bias_grad = jnp.zeros((1, width), F32)
    pos_grad = jnp.zeros((seq_len, width), F32)
    for block in range(blocks):
        if block % HALF == 0:
            for k in range(block, min(block + HALF, blocks)):
                qk_all.wait(k)
                unit_all.wait(k)
                inv_all.wait(k)
        caps = pl.ds(block * CAP_BLOCK, CAP_BLOCK)
        here = pl.ds(block * block_rows, block_rows)
        a = a_ref[:, caps, :].reshape(heads * CAP_BLOCK, width)
        qk = qk_ref[:, caps, :].reshape(heads * CAP_BLOCK, width)
        unit = unit_ref[here, :].astype(F32)
        drows = tn(probs_ref[block], a) + tn(ds_ref[block], qk)
        gain_grad = gain_grad + jnp.sum(drows * unit, 0, keepdims=True)
        bias_grad = bias_grad + jnp.sum(drows, 0, keepdims=True)
        dx = norm_back(drows, unit, inv_ref[here, 0:1], gain).astype(BF)
        dx_ref[here, :] = dx
        pos_grad = pos_grad + jnp.sum(dx.astype(F32).reshape(CAP_BLOCK, seq_len, width), 0)
    for block in range(blocks):
        here = pl.ds(block * block_rows, block_rows)
        copy = pltpu.make_async_copy(dx_ref.at[here], dx_out.at[here], sems.at[block])
        copy.start()
        pending.append(copy)
    small_ref[0:1] = gain_grad
    small_ref[1:2] = bias_grad
    posg_ref[...] = pos_grad
    seg_ref[...], digits_ref[...], pooled_ref[...] = slot_sums(
        0, slot_cap, seq_len, slots_ref, packed_ref, dx_ref, seg_ref.shape[0] // slot_cap
    )
    for copy in pending:
        copy.wait()


def query_back_body(
    n_mp, meta_ref, kept_ref, got_ref, wout_ref, dx1_ref, vec_ref, pos_pick_ref, own_pick_ref, slots_ref,
    seg_ref, digits_ref, pooled_ref, pos_one_ref, small_one_ref, small_two_ref, small_three_ref, x0p, wq,
    dxp_ref, send_ref, kept_out, sent_out, rest_ref, smalls_ref, all_ref,
):
    captions, width = dx1_ref.shape
    n_dp = send_ref.shape[0]
    slots = seg_ref.shape[0]
    slot_cap = slots // n_dp
    lanes = send_ref.shape[2]
    span = width // n_mp
    rank = meta_ref[0]
    total = kept_ref[...].astype(F32) + got_ref[...].astype(F32)
    all_ref[:, : 2 * span] = total[:width]
    all_ref[:, 2 * span : 3 * span] = wout_ref[...].astype(F32)
    dq = jnp.concatenate(
        [total[width + k * captions : width + (k + 1) * captions] for k in range(n_mp // 2)], axis=1
    ).astype(BF)
    gain = vec_ref[0:1]
    unit, inverse = normalize(x0p.value())
    h1 = (unit * gain + vec_ref[1:2]).astype(BF)
    owned = jnp.sum(own_pick_ref[...].astype(F32), -1, keepdims=True)
    dh1 = nn(dq, wq.value()) * owned
    dxp = (dx1_ref[...] * owned + norm_back(dh1, unit, inverse, gain)).astype(BF)
    dxp_ref[...] = dxp
    seq_len = pos_one_ref.shape[0]
    smalls_ref[...] = jnp.zeros_like(smalls_ref)
    smalls_ref[:seq_len] = pos_one_ref[...] + tn(pos_pick_ref[...], dxp)
    at = seq_len
    smalls_ref[at : at + 1] = small_three_ref[0:1] + jnp.sum(dh1 * unit, 0, keepdims=True)
    smalls_ref[at + 1 : at + 2] = small_three_ref[1:2] + jnp.sum(dh1, 0, keepdims=True)
    smalls_ref[at + 2 : at + 5] = small_two_ref[...]
    smalls_ref[at + 5 : at + 7] = small_one_ref[...]
    smalls = smalls_ref[...]
    high = smalls.astype(BF)
    low = (smalls - high.astype(F32)).astype(BF)
    all_ref[:, 3 * span :] = tn(h1, nn(dq, own_columns(rank * span, width, span)).astype(BF))
    chunk = width // n_dp
    blocks = [
        functools.partial(lambda i: all_ref[pl.ds(i * chunk, chunk), :], i) for i in range(n_dp)
    ]
    split_blocks(blocks, DOWN_BIT, meta_ref[2] // DOWN_BIT % 2, kept_out, sent_out)
    shape = (SMALLS, 2 * SMALLS)
    place = iota2(shape, 1) - iota2(shape, 0)
    rest_ref[...] = tn(high, jnp.where(place == 0, 1.0, 0.0).astype(BF)) + tn(
        low, jnp.where(place == SMALLS, 1.0, 0.0).astype(BF)
    )
    seg = (seg_ref[...] + nn(pooled_ref[...], dxp)).astype(BF)
    most = slots_ref[3:4, :lanes]
    which = iota2((NOTES, lanes), 0)
    most = jnp.where(which == 2, most // NOTE_BASE, most % NOTE_BASE).astype(F32)
    chunk = width // n_dp
    base = (width // lanes) * slot_cap
    for i in range(n_dp):
        for j in range(width // lanes):
            send_ref[i, j * slot_cap : (j + 1) * slot_cap, :] = seg[
                i * slot_cap : (i + 1) * slot_cap, j * lanes : (j + 1) * lanes
            ]
        extra = send_ref.shape[1] - NOTES
        tall = extra - base
        if 4 * tall != chunk:
            send_ref[i, base:extra, :] = jnp.zeros((tall, lanes), BF)
        for k in range(4):
            count = min(tall, chunk - k * tall)
            if count > 0:
                send_ref[i, base : base + count, k * 2 * SMALLS : (k + 1) * 2 * SMALLS] = rest_ref[
                    pl.ds(i * chunk + k * tall, count), :
                ].astype(BF)
        digits = digits_ref[:NOTES, i * slot_cap : (i + 1) * slot_cap]
        note = jnp.concatenate([digits, jnp.zeros((NOTES, lanes - slot_cap), F32)], axis=1)
        send_ref[i, extra:, :] = jnp.where(which < 2, note, most).astype(BF)


def send_body(slot_cap, meta_ref, dx_ref, dxp_ref, slots_ref, packed_ref, send_ref, digits_ref):
    n_dp, _, lanes = send_ref.shape
    width = dx_ref.shape[1]
    seq_len = dx_ref.shape[0] // dxp_ref.shape[0]
    seg, digits_ref[...], pooled = slot_sums(
        meta_ref[0], slot_cap, seq_len, slots_ref, packed_ref, dx_ref, n_dp
    )
    seg = (seg + nn(pooled, dxp_ref[...])).astype(BF)
    for i in range(n_dp):
        for j in range(width // lanes):
            send_ref[i, j * slot_cap : (j + 1) * slot_cap, :] = seg[
                i * slot_cap : (i + 1) * slot_cap, j * lanes : (j + 1) * lanes
            ]


def place_rows(row, got_ref, table_ref, slot_cap, lanes):
    n_dp = got_ref.shape[0]
    shape = (table_ref.shape[0], n_dp * slot_cap)
    hit = jnp.where(iota2(shape, 0) == row, 1.0, 0.0).astype(BF)
    for j in range(table_ref.shape[1] // lanes):
        cut = slice(j * slot_cap, (j + 1) * slot_cap)
        rows = jnp.concatenate([got_ref[i, cut, :] for i in range(n_dp)], axis=0)
        table_ref[:, j * lanes : (j + 1) * lanes] = nn(hit, rows)


def place_body(slot_cap, chunk, meta_ref, got_ref, table_ref, rest_ref, most_ref, row_ref):
    lanes = got_ref.shape[2]
    extra = got_ref.shape[1] - NOTES
    most = jnp.zeros((1, 128), F32)
    for i in range(got_ref.shape[0]):
        note = got_ref[i, extra:, :].astype(F32)
        at = slice(i * slot_cap, (i + 1) * slot_cap)
        row_ref[:, at] = note[0:1, :slot_cap] * float(NOTE_BASE) + note[1:2, :slot_cap] - 1.0
        most = jnp.maximum(most, note[2:3, :128] * float(NOTE_BASE) + note[3:4, :128])
    most_ref[...] = most
    place_rows(row_ref[...].astype(I32), got_ref, table_ref, slot_cap, lanes)
    base = table_ref.shape[1] // lanes * slot_cap
    total = got_ref[0, base:extra, :].astype(F32)
    for i in range(1, got_ref.shape[0]):
        total = total + got_ref[i, base:extra, :].astype(F32)
    for k in range(4):
        count = min(extra - base, chunk - k * (extra - base))
        if count > 0:
            cut = slice(k * 2 * SMALLS, k * 2 * SMALLS + SMALLS)
            low = slice(k * 2 * SMALLS + SMALLS, (k + 1) * 2 * SMALLS)
            at = k * (extra - base)
            rest_ref[at : at + count, :] = total[:count, cut] + total[:count, low]


def place_more_body(meta_ref, row_ref, got_ref, old_ref, table_ref):
    lanes = got_ref.shape[2]
    slot_cap = got_ref.shape[1] // (table_ref.shape[1] // lanes)
    place_rows(row_ref[...], got_ref, table_ref, slot_cap, lanes)
    table_ref[...] += old_ref[...]


def on_device(
    token_ids, lengths, images, table, pos_table, ln1_gain, ln1_bias, w_qkv, w_out, b_out,
    ln2_gain, ln2_bias, w_up, b_up, w_down, b_down, w_head,
):
    n_mp, n_dp = lax.axis_size("mp"), lax.axis_size("dp")
    mp_rank, dp_rank = lax.axis_index("mp"), lax.axis_index("dp")
    captions, seq_len = token_ids.shape
    rows = captions * seq_len
    vocab_part, width = table.shape
    heads = width // HEAD_DIM
    own_width = width // n_mp
    ff = w_up.shape[1]
    owner_rows = vocab_part // n_dp
    slot_cap = -(-rows // (n_dp * n_mp * 16)) * 16
    slots = n_dp * slot_cap
    chunk = width // n_dp
    lanes = own_width + 2 * SMALLS
    n_all = captions * n_dp
    blocks = captions // CAP_BLOCK
    meta = jnp.stack([mp_rank, dp_rank * captions, dp_rank]).astype(I32)

    gather = functools.partial(lax.all_gather, axis_name="mp", axis=0)
    turned = jnp.swapaxes(w_qkv, 1, 2)
    shard = jnp.concatenate([turned, w_out[None]])
    image_f = images.astype(F32)
    image_unit = (
        image_f * lax.rsqrt(jnp.sum(image_f * image_f, -1, keepdims=True) + EPS)
    ).astype(BF)
    all_image = lax.all_gather(image_unit, ("dp", "mp"), axis=0, tiled=True)
    at_row = jnp.arange(8)[:, None]
    vecs = b_up.astype(F32)[None, :]
    for k, vec in enumerate((ln1_gain, ln1_bias, b_out, ln2_gain, ln2_bias, b_down)):
        vecs = jnp.where(at_row == k, vec.astype(F32)[None, :], vecs)

    valid = jnp.arange(seq_len)[None, :] < lengths[:, None]
    end_pick = jnp.arange(seq_len)[None, :] == (lengths - 1)[:, None]
    pos_pick = end_pick.astype(BF)
    local2 = token_ids - mp_rank * vocab_part
    owned2 = jnp.logical_and(local2 >= 0, local2 < vocab_part)
    own_pick = jnp.logical_and(end_pick, owned2).astype(BF)
    local = token_ids.reshape(rows) - mp_rank * vocab_part
    local = after(local, image_unit)
    emb = jnp.take(table, jnp.clip(local, 0, vocab_part - 1), axis=0, mode="clip")
    packed = token_ids + jnp.where(valid, VALID_BIT, 0) + jnp.where(end_pick, END_BIT, 0)
    packed = packed.astype(I32).reshape(1, rows)
    per_head = pltpu.VMEM((heads, captions, width), BF)
    per_head = pltpu.VMEM((heads, captions, width), BF)
    row_buffer = pltpu.VMEM((rows, width), BF)
    dma = pltpu.SemaphoreType.DMA
    ends, unit_rows, unit, inverse = vmem_call(
        functools.partial(rows_body, vocab_part),
        [
            ((captions, width), BF),
            ((rows, width), BF, False),
            ((rows, width), BF, False),
            ((rows, 128), F32, False),
        ],
        meta,
        [pos_table, vecs, packed],
        [fetch(emb, blocks)],
        [row_buffer, row_buffer, pltpu.VMEM((rows, 128), F32), dma((3 * blocks,))],
        flops=WORK,
        mib=28,
    )
    shards = everyone(shard, "mp", ends)
    wq, wk, wv, wo = (fetch_weight(shards, k) for k in range(4))
    pay, qk, x0p, q = vmem_call(
        functools.partial(attend_body, vocab_part),
        [
            ((captions, width + 128), BF),
            ((heads, captions, width), BF, False),
            ((captions, width), F32, True),
            ((captions, width), BF, True),
        ],
        meta,
        [gather(ends), pos_pick, pos_table, vecs, packed],
        [wq, wk, fetch(unit_rows, blocks), wv],
        [per_head, per_head, dma((n_mp,))],
        flops=WORK,
        mib=28,
    )
    ctx, lse, x1, u, part = vmem_call(
        hidden_body,
        [
            ((captions, width), F32, True),
            ((captions, width), F32, True),
            ((captions, width), F32, True),
            ((captions, ff), F32, True),
            ((captions, width), BF),
        ],
        meta,
        [gather(pay), vecs],
        [fetch(x0p), wo, fetch(w_up), fetch(w_down)],
        flops=WORK,
        mib=20,
    )
    pooled, proj, powers, sums = vmem_call(
        logits_body,
        [
            ((captions, width), BF, True),
            ((captions, width), F32, True),
            ((captions, n_all), F32, True),
            ((n_dp, 1, n_all + 128), F32),
        ],
        meta,
        [gather(part), vecs],
        [fetch(x1), fetch(w_head), fetch(all_image)],
        flops=WORK * 5,
    )
    all_sums = lax.all_to_all(sums, "dp", 0, 0, tiled=True)
    slot_table = vmem_call(
        functools.partial(slot_body, owner_rows, n_dp),
        [((8, rows), I32)],
        meta,
        [after(packed, sums)],
        flops=WORK * 7,
        mib=20,
    )[0]
    loss, dpooled, part, du, dproj = vmem_call(
        loss_body,
        [
            ((1, 128), F32),
            ((captions, width), F32),
            ((captions, width), BF),
            ((captions, ff), BF),
            ((captions, width), BF),
        ],
        meta,
        [after(all_sums, slot_table), vecs],
        [
            fetch(powers), fetch(all_image), fetch(proj), fetch(w_head), fetch(u), fetch(w_down),
            fetch(w_up),
        ],
        flops=WORK * 5,
    )
    kind = BF if chunk % 16 == 0 else F32
    *halves, small_one = vmem_call(
        weights_body,
        [
            *[((n_dp // 2, chunk, ff + own_width), BF)] * 2,
            *[((n_dp // 2, chunk, ff), BF)] * 2,
            ((2, width), F32),
        ],
        meta,
        [vecs, dpooled, du, dproj],
        [fetch(u), fetch(x1), fetch(pooled)],
        [pltpu.VMEM((width, ff + own_width), kind), pltpu.VMEM((width, ff), kind)],
        flops=WORK * 4,
        mib=24,
    )
    dp_bits = bits_of("dp")

    def next_half(total, bits, hold=None):
        total = halve(total, "dp", bits, bits[0], hold)
        bits.pop(0)
        return total

    one_step = len(dp_bits) == 1
    down = exchange_half(*halves[:2], "dp", DOWN_BIT, one_step)
    up = exchange_half(*halves[2:], "dp", UP_BIT, one_step)
    down_bits = [bit for bit in dp_bits if bit != DOWN_BIT]
    up_bits = [bit for bit in dp_bits if bit != UP_BIT]
    for bit in bits_of("mp"):
        part = part + lax.ppermute(part, "mp", [(i, i ^ bit) for i in range(n_mp)])
    parts = part[None]
    pair_rows = n_mp // 2 * (width + captions)
    dx1, wout, kept, *sent, a, probs, dscores, small_two = vmem_call(
        functools.partial(attend_back_body, vocab_part),
        [
            ((captions, width), F32),
            ((width, own_width), BF),
            ((pair_rows, 2 * own_width), BF),
            *[((pair_rows // 2, 2 * own_width), BF)] * 2,
            ((heads, captions, width), BF),
            ((blocks, heads * CAP_BLOCK, CAP_BLOCK * seq_len), BF),
            ((blocks, heads * CAP_BLOCK, CAP_BLOCK * seq_len), BF),
            ((3, width), F32),
        ],
        meta,
        [parts, packed, vecs, dpooled],
        [
            fetch(x1), fetch(ctx), wo, wv, fetch(lse), fetch(qk, blocks, 1),
            fetch(unit_rows, blocks), wk, fetch(q),
        ],
        [
            per_head, per_head, pltpu.VMEM((n_mp, width, 2 * own_width), BF),
            pltpu.VMEM((captions, width), BF),
        ],
        flops=WORK * 13,
    )
    got = [lax.ppermute(x, "mp", [(i, i ^ 1) for i in range(n_mp)]) for x in sent]
    last_rows = pair_rows - width
    kept, sent = vmem_call(
        between_body, [((last_rows, 2 * own_width), BF)] * 2, meta, [kept, *got], flops=WORK * 2, mib=12
    )
    got = lax.ppermute(sent, "mp", [(i, i ^ 2) for i in range(n_mp)])
    dx, pos_one, small_three, seg, digits, pooled_slots = vmem_call(
        functools.partial(rows_back_body, slot_cap),
        [
            ((rows, width), BF, False),
            ((seq_len, width), F32),
            ((2, width), F32),
            ((slots, width), F32),
            ((16, slots), F32),
            ((slots, captions), BF),
        ],
        meta,
        [after(probs, sent), dscores, a, vecs, slot_table, packed],
        [fetch(qk, blocks, 1), fetch(unit, blocks), fetch(inverse, blocks)],
        [row_buffer, dma((blocks,))],
        flops=WORK * 12,
        mib=32,
    )
    down, up = next_half(down, down_bits), next_half(up, up_bits, seg)
    rest_rows = -(-chunk // 32) * 8
    send_rows = width // lanes * slot_cap
    dxp, send, kept, sent = vmem_call(
        functools.partial(query_back_body, n_mp),
        [
            ((captions, width), BF),
            ((n_dp, send_rows + rest_rows + NOTES, lanes), BF),
            *[((n_dp // 2, chunk, 4 * own_width), BF)] * 2,
        ],
        meta,
        [
            kept, got, wout, dx1, vecs, pos_pick, own_pick, slot_table, seg, digits, pooled_slots, pos_one,
            small_one, small_two, small_three,
        ],
        [fetch(x0p), wq],
        [
            pltpu.VMEM((width, 2 * SMALLS), F32), pltpu.VMEM((SMALLS, width), F32),
            pltpu.VMEM((width, 4 * own_width), F32),
        ],
        flops=WORK * 4,
        mib=24,
    )
    got = lax.all_to_all(send, "dp", 0, 0, tiled=True)
    wkvo = exchange_half(kept, sent, "dp", DOWN_BIT, one_step)
    bits = [bit for bit in dp_bits if bit != DOWN_BIT]
    while len(bits) > 1:
        wkvo = next_half(wkvo, bits)
    while down_bits:
        down = next_half(down, down_bits)
    while up_bits:
        up = next_half(up, up_bits)
    down, up = lax.optimization_barrier((down[0], up[0]))
    table_grad, rest, most_all = vmem_call(
        functools.partial(place_body, slot_cap, chunk),
        [((owner_rows, width), F32), ((chunk, SMALLS), F32), ((1, 128), F32)],
        meta,
        [got],
        (),
        [pltpu.VMEM((1, slots), F32)],
        flops=WORK * 3,
        mib=20,
    )
    most_all = most_all[0, 0].astype(I32)
    small = rest
    last = gather(jnp.concatenate([down[:, ff:], small, jnp.zeros_like(small)], 1))
    wkvo = lax.optimization_barrier(next_half(wkvo, bits, last)[0])

    def another(carry):
        turn, total = carry
        sent, digits = vmem_call(
            functools.partial(send_body, slot_cap),
            [((n_dp, send_rows, lanes), BF), ((16, slots), F32)],
            turn.reshape(1),
            [dx, dxp, slot_table, packed],
        )
        row = (digits[0] * NOTE_BASE + digits[1] - 1.0).astype(I32)
        row = lax.all_to_all(row.reshape(n_dp, slot_cap), "dp", 0, 0, tiled=True)
        sent = lax.all_to_all(sent, "dp", 0, 0, tiled=True)
        total = vmem_call(
            place_more_body,
            [((owner_rows, width), F32)],
            meta,
            [row.reshape(1, slots), sent, total],
        )[0]
        return turn + 1, total

    _, table_grad = lax.while_loop(
        lambda carry: carry[0] * slot_cap < most_all, another, (jnp.int32(1), table_grad)
    )
    w_head_grad = jnp.swapaxes(last[:, :, :own_width], 0, 1).reshape(chunk, width)
    shared = jnp.sum(last[:, :, own_width : own_width + SMALLS], 0)
    qkv_grad = jnp.stack(
        [wkvo[:, k * own_width : (k + 1) * own_width] for k in (3, 0, 1)]
    )
    return (
        loss[0, 0],
        table_grad,
        shared[:, :seq_len].T,
        shared[:, seq_len],
        shared[:, seq_len + 1],
        qkv_grad,
        wkvo[:, 2 * own_width : 3 * own_width].T,
        small[:, seq_len + 4],
        small[:, seq_len + 2],
        small[:, seq_len + 3],
        up,
        small[:, seq_len + 6],
        down[:, :ff].T,
        small[:, seq_len + 5],
        w_head_grad,
    )


def solution(mesh):
    placed = (
        P("dp", None),
        P("dp"),
        P(("dp", "mp"), None),
        P("mp", None),
        P(),
        P(),
        P(),
        P(None, None, "mp"),
        P("mp", None),
        P(),
        P(),
        P(),
        P(None, "mp"),
        P("mp"),
        P("mp", None),
        P(),
        P(),
    )
    return jax.shard_map(
        on_device,
        mesh=mesh,
        in_specs=placed,
        out_specs=(
            P(),
            P(("mp", "dp"), None),
            P(None, "dp"),
            P("dp"),
            P("dp"),
            P(None, "dp", "mp"),
            P("mp", "dp"),
            P("dp"),
            P("dp"),
            P("dp"),
            P("dp", "mp"),
            P(("mp", "dp")),
            P("mp", "dp"),
            P("dp"),
            P("dp", None),
        ),
        check_vma=False,
    )
```

```python
import functools
import math

import jax
import jax.numpy as jnp
from jax import lax
from jax.experimental import pallas as pl
from jax.experimental.pallas import tpu as pltpu
from jax.sharding import PartitionSpec as P

HEAD_DIM = 64
LOGIT_SCALE = 50.0
EPS = 1e-06
MASK_FILL = -1000000000.0
NO_KEY = -1e30
BF = jnp.bfloat16
F32 = jnp.float32
I32 = jnp.int32
GELU_C = math.sqrt(2.0 / math.pi)
CAP_BLOCK = 16
SMALLS = 32
NOTES = 8
HALF = 4
VALID_BIT = 1 << 20
END_BIT = 1 << 21
NOTE_BASE = 32
WORK = 920000000
DOWN_BIT = 1
UP_BIT = 2


def nn(a, b):
    return lax.dot_general(a, b, (((1,), (0,)), ((), ())), preferred_element_type=F32)


def nt(a, b):
    return lax.dot_general(a, b, (((1,), (1,)), ((), ())), preferred_element_type=F32)


def tn(a, b):
    return lax.dot_general(a, b, (((0,), (0,)), ((), ())), preferred_element_type=F32)


def normalize(rows):
    centred = rows - jnp.mean(rows, -1, keepdims=True)
    inverse = lax.rsqrt(jnp.mean(centred * centred, -1, keepdims=True) + EPS)
    return centred * inverse, inverse


def norm_back(upstream, unit, inverse, gain):
    scaled = upstream * gain
    mean_scaled = jnp.mean(scaled, -1, keepdims=True)
    mean_unit = jnp.mean(scaled * unit, -1, keepdims=True)
    return inverse * (scaled - mean_scaled - unit * mean_unit)


def iota2(shape, dim):
    return lax.broadcasted_iota(I32, shape, dim)


class Late:
    def __init__(self, ref, pairs, sems):
        self.ref = ref
        self.copies = [
            pltpu.make_async_copy(src, dst, sem) for (src, dst), sem in zip(pairs, sems)
        ]
        self.waiting = set(range(len(self.copies)))

    def start(self):
        for copy in self.copies:
            copy.start()

    def wait(self, part=None):
        for k in sorted(self.waiting) if part is None else [part]:
            if k in self.waiting:
                self.copies[k].wait()
                self.waiting.discard(k)
        return self.ref

    def value(self):
        return self.wait()[...]


def fetch(array, parts=1, axis=0):
    return ("blocks", [array], parts, axis)


def fetch_weight(shards, which):
    return ("weight", list(shards), which, 0)


def vmem_call(body, outs, meta, args, late=(), scratch=(), flops=1, mib=40):
    vmem = pl.BlockSpec(memory_space=pltpu.VMEM)
    hbm = pl.BlockSpec(memory_space=pltpu.HBM)
    sources, buffers, counts = [], [], []
    for kind, arrays, parts, axis in late:
        sources += arrays
        if kind == "weight":
            _, rows, width = arrays[0].shape
            buffers.append(pltpu.VMEM((rows * len(arrays), width), arrays[0].dtype))
            counts.append(len(arrays))
        else:
            buffers.append(pltpu.VMEM(arrays[0].shape, arrays[0].dtype))
            counts.append(parts)

    staged = [k for k, o in enumerate(outs) if len(o) > 2 and o[2]]

    def kernel(meta_ref, *refs):
        arg_refs, refs = refs[: len(args)], refs[len(args) :]
        source_refs, refs = refs[: len(sources)], refs[len(sources) :]
        out_refs, refs = refs[: len(outs)], refs[len(outs) :]
        buffer_refs, refs = refs[: len(buffers)], refs[len(buffers) :]
        sems, stage_sems, refs = refs[0], refs[1], refs[2:]
        stages, refs = refs[: len(staged)], refs[len(staged) :]
        targets = list(out_refs)
        for k, stage in zip(staged, stages):
            targets[k] = stage
        handles, at, place = [], 0, 0
        for (kind, arrays, parts, axis), buffer in zip(late, buffer_refs):
            if kind == "weight":
                rows = arrays[0].shape[1]
                pairs = []
                for k in range(len(arrays)):
                    low = pl.multiple_of((meta_ref[0] ^ k) * rows, rows)
                    pairs.append((source_refs[place + k].at[parts], buffer.at[pl.ds(low, rows)]))
                place += len(arrays)
            else:
                size = arrays[0].shape[axis] // parts
                pairs = []
                for k in range(parts):
                    cut = (slice(None),) * axis + (pl.ds(k * size, size),)
                    pairs.append((source_refs[place].at[cut], buffer.at[cut]))
                place += 1
            handles.append(Late(buffer, pairs, [sems.at[at + k] for k in range(len(pairs))]))
            at += len(pairs)
        for handle in handles:
            handle.start()
        body(meta_ref, *arg_refs, *handles, *targets, *refs)
        copies = [
            pltpu.make_async_copy(stage, out_refs[k], stage_sems.at[i])
            for i, (k, stage) in enumerate(zip(staged, stages))
        ]
        for copy in copies:
            copy.start()
        for handle in handles:
            handle.wait()
        for copy in copies:
            copy.wait()

    return pl.pallas_call(
        kernel,
        out_shape=[
            pltpu.HBM(*o[:2]) if len(o) > 2 else jax.ShapeDtypeStruct(*o) for o in outs
        ],
        in_specs=[pl.BlockSpec(memory_space=pltpu.SMEM)]
        + [vmem] * len(args)
        + [hbm] * len(sources),
        out_specs=[hbm if len(o) > 2 else vmem for o in outs],
        scratch_shapes=[
            *buffers,
            pltpu.SemaphoreType.DMA((max(1, sum(counts)),)),
            pltpu.SemaphoreType.DMA((max(1, len(staged)),)),
            *(pltpu.VMEM(*outs[k][:2]) for k in staged),
            *scratch,
        ],
        compiler_params=pltpu.CompilerParams(vmem_limit_bytes=mib << 20),
        cost_estimate=pl.CostEstimate(flops=flops, bytes_accessed=1, transcendentals=0),
    )(meta, *args, *(pltpu.with_memory_space_constraint(x, pltpu.HBM) for x in sources))


def exchange_half(kept, sent, axis, bit, last):
    count = lax.axis_size(axis)
    got = lax.ppermute(sent, axis, [(i, i ^ bit) for i in range(count)])
    total = kept.astype(F32) + got.astype(F32)
    return total if last else total.astype(BF)


def halve(total, axis, bits, bit, hold=None):
    low = 1 << bits.index(bit)
    pairs = total.reshape((total.shape[0] // (2 * low), 2, low) + total.shape[1:])
    shape = (total.shape[0] // 2,) + total.shape[1:]
    mine = (lax.axis_index(axis) // bit) % 2
    sent = lax.dynamic_index_in_dim(pairs, 1 - mine, 1, keepdims=False).reshape(shape)
    kept = lax.dynamic_index_in_dim(pairs, mine, 1, keepdims=False).reshape(shape)
    if hold is not None:
        kept = after(kept, hold)
    return exchange_half(kept, sent, axis, bit, len(bits) == 1)


def split_blocks(blocks, bit, mine, kept_ref, sent_ref):
    place = 0
    for i in range(len(blocks)):
        if i & bit == 0:
            first, second = blocks[i](), blocks[i | bit]()
            kept_ref[place] = jnp.where(mine == 0, first, second).astype(BF)
            sent_ref[place] = jnp.where(mine == 0, second, first).astype(BF)
            place += 1


def bits_of(axis):
    count = lax.axis_size(axis)
    return [1 << k for k in range(count.bit_length() - 1)]


def after(x, *others):
    return lax.optimization_barrier((x, others))[0]


def everyone(x, axis, before):
    count = lax.axis_size(axis)
    have = {0: x}
    bit = count // 2
    while bit:
        pairs = [(i, i ^ bit) for i in range(count)]
        for k, v in list(have.items()):
            have[k | bit] = lax.ppermute(after(v, before) if k else v, axis, pairs)
        bit //= 2
    return [have[k] for k in range(count)]


def own_columns(start, width, own_width):
    shape = (width, own_width)
    hit = iota2(shape, 0) == start + iota2(shape, 1)
    return jnp.where(hit, 1.0, 0.0).astype(BF)


def unpack(packed):
    return packed % VALID_BIT, packed // VALID_BIT % 2 > 0, packed // END_BIT > 0


def own_code(packed, rank, vocab_part):
    ids, valid, _ = unpack(packed)
    return jnp.where(ids // vocab_part == rank, jnp.where(valid, 2, 1), 0)


def head_mask(captions, span):
    shape = (span // HEAD_DIM * captions, span)
    return (iota2(shape, 0) // captions) == (iota2(shape, 1) // HEAD_DIM)


def spread_heads(rows, group, mask):
    span = mask.shape[1]
    part = rows[:, group * span : (group + 1) * span].astype(F32)
    tall = jnp.concatenate([part] * (span // HEAD_DIM), axis=0)
    return jnp.where(mask, tall, 0.0).astype(BF)


def fold_heads(tall, captions, mask):
    kept = jnp.where(mask, tall, 0.0)
    total = kept[:captions]
    for h in range(1, tall.shape[0] // captions):
        total = total + kept[h * captions : (h + 1) * captions]
    return total


def same_caption(heads, seq_len):
    shape = (heads * CAP_BLOCK, CAP_BLOCK * seq_len)
    return (iota2(shape, 0) % CAP_BLOCK) == (iota2(shape, 1) // seq_len)


def rows_body(
    vocab_part, meta_ref, pos_ref, vec_ref, packed_ref, emb,
    end_ref, rows_out, unit_out, inv_out, rows_ref, unit_ref, inv_ref, sems,
):
    captions = end_ref.shape[0]
    seq_len = pos_ref.shape[0]
    block_rows = CAP_BLOCK * seq_len
    gain, bias = vec_ref[0:1], vec_ref[1:2]
    pos = jnp.concatenate([pos_ref[...].astype(F32)] * CAP_BLOCK, axis=0)
    pending = []

    def write_back(src, dst):
        copy = pltpu.make_async_copy(src, dst, sems.at[len(pending)])
        copy.start()
        pending.append(copy)

    blocks = captions // CAP_BLOCK
    for block in range(blocks):
        here = pl.ds(block * block_rows, block_rows)
        if block % HALF == 0:
            for k in range(block, min(block + HALF, blocks)):
                emb.wait(k)
        packed = packed_ref[:, block * block_rows : (block + 1) * block_rows]
        low = emb.ref[here, :]
        ids, _, is_end = unpack(packed)
        shape = (CAP_BLOCK, block_rows)
        mark = jnp.logical_and(is_end, ids // vocab_part == meta_ref[0])
        mark = jnp.logical_and(iota2(shape, 0) == iota2(shape, 1) // seq_len, mark)
        ends = nn(jnp.where(mark, 1.0, 0.0).astype(BF), low)
        end_ref[block * CAP_BLOCK : (block + 1) * CAP_BLOCK] = ends.astype(BF)
        unit, inverse = normalize(low.astype(F32) + pos)
        unit_ref[here, :] = unit.astype(BF)
        inv_ref[here, :] = jnp.broadcast_to(inverse, (block_rows, 128))
        rows_ref[here, :] = (unit * gain + bias).astype(BF)
        if block % HALF == HALF - 1 or block == blocks - 1:
            low_row = block // HALF * HALF * block_rows
            done = pl.ds(low_row, (block + 1) * block_rows - low_row)
            write_back(unit_ref.at[done], unit_out.at[done])
            write_back(inv_ref.at[done], inv_out.at[done])
            write_back(rows_ref.at[done], rows_out.at[done])
    for copy in pending:
        copy.wait()


def attend_body(
    vocab_part, meta_ref, ends_ref, pos_pick_ref, pos_ref, vec_ref, packed_ref, wq, wk, rows_all, wv,
    pay_ref, qk_out, x0p_ref, q_ref, qk_ref, t_ref, sems,
):
    n_mp = ends_ref.shape[0]
    captions, width = x0p_ref.shape
    heads = width // HEAD_DIM
    span = width // n_mp
    per_group = span // HEAD_DIM
    seq_len = pos_ref.shape[0]
    block_rows = CAP_BLOCK * seq_len
    gain, bias = vec_ref[0:1], vec_ref[1:2]
    pooled_in = nn(pos_pick_ref[...], pos_ref[...])
    for i in range(n_mp):
        pooled_in = pooled_in + ends_ref[i].astype(F32)
    pending = []
    x0p_ref[...] = pooled_in
    unit, _ = normalize(pooled_in)
    q = nt((unit * gain + bias).astype(BF), wq.value()).astype(BF)
    q_ref[...] = q
    mask = head_mask(captions, span)
    scale = 1.0 / math.sqrt(HEAD_DIM)
    wk_ref = wk.wait()
    for g in range(n_mp):
        some = slice(g * per_group, (g + 1) * per_group)
        tall = nn(spread_heads(q, g, mask), wk_ref[g * span : (g + 1) * span]) * scale
        qk_ref[some] = tall.astype(BF).reshape(per_group, captions, width)
        copy = pltpu.make_async_copy(qk_ref.at[some], qk_out.at[some], sems.at[g])
        copy.start()
        pending.append(copy)
    lane = iota2((heads, CAP_BLOCK, 128), 2)
    head_of = iota2((heads, CAP_BLOCK, 128), 0)
    rows_ref = rows_all.wait()
    blocks = range(captions // CAP_BLOCK)
    cuts = [pl.ds(block * block_rows, block_rows) for block in blocks]
    caps = [pl.ds(block * CAP_BLOCK, CAP_BLOCK) for block in blocks]
    raw = [
        nt(qk_ref[:, caps[block], :].reshape(heads * CAP_BLOCK, width), rows_ref[cuts[block], :])
        for block in blocks
    ]
    same = same_caption(heads, seq_len)
    code = own_code(packed_ref[...], meta_ref[0], vocab_part)
    log_totals, weights = [], []
    for block in blocks:
        here = code[:, block * block_rows : (block + 1) * block_rows]
        own = jnp.logical_and(same, here > 0)
        scores = jnp.where(own, jnp.where(here > 1, raw[block], MASK_FILL), NO_KEY)
        top = jnp.max(scores, -1, keepdims=True)
        power = jnp.where(own, jnp.exp(scores - top), 0.0)
        total = jnp.sum(power, -1, keepdims=True)
        some = total > 0.0
        total = jnp.where(some, total, 1.0)
        log_totals.append(jnp.where(some, top + jnp.log(total), NO_KEY))
        weights.append((power * (1.0 / total)).astype(BF))
    for block in blocks:
        mixed = nn(weights[block], rows_ref[cuts[block], :])
        t_ref[:, caps[block], :] = mixed.astype(BF).reshape(heads, CAP_BLOCK, width)
    for block in blocks:
        log_total = log_totals[block]
        first = log_total.astype(BF).astype(F32)
        second = (log_total - first).astype(BF).astype(F32)
        third = log_total - first - second
        stat = jnp.zeros((heads, CAP_BLOCK, 128), F32)
        for k, piece in enumerate((first, second, third)):
            stat = stat + jnp.where(
                lane == head_of + 16 * k, piece.reshape(heads, CAP_BLOCK, 1), 0.0
            )
        pay_ref[caps[block], width:] = jnp.sum(stat, 0).astype(BF)
    wv_ref = wv.wait()
    for g in range(n_mp):
        tall = t_ref[g * per_group : (g + 1) * per_group].reshape(per_group * captions, width)
        piece = nt(tall, wv_ref[g * span : (g + 1) * span])
        pay_ref[:, g * span : (g + 1) * span] = fold_heads(piece, captions, mask).astype(BF)
    for copy in pending:
        copy.wait()


def hidden_body(
    meta_ref, pay_ref, vec_ref, x0p, wo, wup, wdown,
    ctx_ref, lse_ref, x1_ref, u_ref, part_ref,
):
    n_mp = pay_ref.shape[0]
    captions, width = ctx_ref.shape
    shape = (128, width)
    stat_row, head = iota2(shape, 0), iota2(shape, 1) // HEAD_DIM
    picks = jnp.logical_and(stat_row % 16 == head, stat_row < 48)
    expand = jnp.where(picks, 1.0, 0.0).astype(BF)
    logs = [nn(pay_ref[i, :, width:], expand) for i in range(n_mp)]
    top = functools.reduce(jnp.maximum, logs)
    total = jnp.zeros_like(top)
    ctx = jnp.zeros_like(top)
    for i in range(n_mp):
        weight = jnp.exp(logs[i] - top)
        total = total + weight
        ctx = ctx + weight * pay_ref[i, :, :width].astype(F32)
    ctx = ctx / total
    ctx_ref[...] = ctx
    lse_ref[...] = top + jnp.log(total)
    x1 = x0p.value() + nn(ctx.astype(BF), wo.value()) + vec_ref[2:3]
    x1_ref[...] = x1
    unit, _ = normalize(x1)
    h2 = (unit * vec_ref[3:4] + vec_ref[4:5]).astype(BF)
    u = nn(h2, wup.value()) + vec_ref[6:7]
    u_ref[...] = u
    hidden = (0.5 * u * (1.0 + jnp.tanh(GELU_C * (u + 0.044715 * u * u * u)))).astype(BF)
    part_ref[...] = nn(hidden, wdown.value()).astype(BF)


def logits_body(
    meta_ref, parts_ref, vec_ref, x1, wh, images,
    pooled_ref, proj_ref, e_ref, sums_ref,
):
    x2 = x1.value() + vec_ref[5:6]
    for i in range(parts_ref.shape[0]):
        x2 = x2 + parts_ref[i].astype(F32)
    pooled = x2.astype(BF)
    pooled_ref[...] = pooled
    proj = nn(pooled, wh.value())
    proj_ref[...] = proj
    text = (proj * lax.rsqrt(jnp.sum(proj * proj, -1, keepdims=True) + EPS)).astype(BF)
    logits = LOGIT_SCALE * nt(text, images.value())
    powers = jnp.exp(logits)
    e_ref[...] = powers
    n_all = powers.shape[1]
    is_diag = iota2(logits.shape, 1) == meta_ref[1] + iota2(logits.shape, 0)
    rows = jnp.log(jnp.sum(powers, -1, keepdims=True))
    rows = rows - 2.0 * jnp.sum(jnp.where(is_diag, logits, 0.0), -1, keepdims=True)
    cols = jnp.sum(powers, 0, keepdims=True)
    rows = jnp.broadcast_to(jnp.sum(rows, 0, keepdims=True), (1, 128))
    for i in range(sums_ref.shape[0]):
        sums_ref[i, :, :n_all] = cols
        sums_ref[i, :, n_all:] = rows


def loss_body(
    meta_ref, sums_ref, vec_ref, e, images, proj, wh, u, wdown, wup,
    loss_ref, dpooled_ref, part_ref, du_ref, dproj_ref,
):
    sums = jnp.sum(sums_ref[...], 0)
    n_all = sums.shape[1] - 128
    cols = sums[:, :n_all]
    loss = jnp.sum(jnp.log(cols), -1, keepdims=True) + sums[:, n_all : n_all + 1]
    loss_ref[...] = jnp.broadcast_to(loss * (0.5 / n_all), (1, 128))
    powers = e.value()
    row_inv = 1.0 / jnp.sum(powers, -1, keepdims=True)
    is_diag = iota2(powers.shape, 1) == meta_ref[1] + iota2(powers.shape, 0)
    grad = powers * row_inv + powers * (1.0 / cols) - jnp.where(is_diag, 2.0, 0.0)
    grad = (grad * (0.5 / n_all)).astype(BF)
    dtext = LOGIT_SCALE * nn(grad, images.value())
    proj = proj.value()
    inv = lax.rsqrt(jnp.sum(proj * proj, -1, keepdims=True) + EPS)
    along = jnp.sum(proj * dtext, -1, keepdims=True)
    dproj = (inv * dtext - inv * inv * inv * proj * along).astype(BF)
    dproj_ref[...] = dproj
    dpooled = nt(dproj, wh.value())
    dpooled_ref[...] = dpooled
    u = u.value()
    th = jnp.tanh(GELU_C * (u + 0.044715 * u * u * u))
    slope = 0.5 * (1.0 + th) + 0.5 * u * (1.0 - th * th) * (
        GELU_C * (1.0 + 3.0 * 0.044715 * u * u)
    )
    du = (nt(dpooled.astype(BF), wdown.value()) * slope).astype(BF)
    du_ref[...] = du
    part_ref[...] = nt(du, wup.value()).astype(BF)


def weights_body(
    meta_ref, vec_ref, dpooled_ref, du_ref, dproj_ref, u, x1, pooled,
    down_kept, down_sent, up_kept, up_sent, small_ref, down_ref, up_ref,
):
    width = dpooled_ref.shape[1]
    dy, du, dproj = dpooled_ref[...].astype(BF), du_ref[...], dproj_ref[...]
    u = u.value()
    th = jnp.tanh(GELU_C * (u + 0.044715 * u * u * u))
    hidden = (0.5 * u * (1.0 + th)).astype(BF)
    unit, _ = normalize(x1.value())
    h2 = (unit * vec_ref[3:4] + vec_ref[4:5]).astype(BF)
    ff = u.shape[1]
    own_width = down_ref.shape[1] - ff
    pick = own_columns(meta_ref[0] * own_width, width, own_width)
    kind = down_ref.dtype
    down_ref[:, :ff] = tn(dy, hidden).astype(kind)
    up_ref[...] = tn(h2, du).astype(kind)
    down_ref[:, ff:] = tn(pooled.value(), nn(dproj, pick).astype(BF)).astype(kind)
    chunk = down_kept.shape[1]
    n_dp = 2 * down_kept.shape[0]
    for ref, bit, kept, sent in (
        (down_ref, DOWN_BIT, down_kept, down_sent),
        (up_ref, UP_BIT, up_kept, up_sent),
    ):
        blocks = [
            functools.partial(lambda ref, i: ref[pl.ds(i * chunk, chunk), :], ref, i)
            for i in range(n_dp)
        ]
        split_blocks(blocks, bit, meta_ref[2] // bit % 2, kept, sent)
    small_ref[0:1] = jnp.sum(dy.astype(F32), 0, keepdims=True)
    small_ref[1:2] = jnp.sum(du.astype(F32), 0, keepdims=True)


def attend_back_body(
    vocab_part, meta_ref, parts_ref, packed_ref, vec_ref, dpooled_ref, x1, ctx, wo, wv, lse, qk_all, rows_all, wk, q,
    dx1_ref, wout_ref, kept_ref, sent_one, sent_two, a_ref, probs_ref, ds_ref, small_ref,
    t_ref, s_ref, wkv_ref, dq_ref,
):
    n_mp = wkv_ref.shape[0]
    captions, width = dpooled_ref.shape
    heads = width // HEAD_DIM
    span = width // n_mp
    per_group = span // HEAD_DIM
    block_rows = rows_all.ref.shape[0] // (captions // CAP_BLOCK)
    seq_len = block_rows // CAP_BLOCK
    rank = meta_ref[0]
    dh2 = parts_ref[0].astype(F32)
    for i in range(1, parts_ref.shape[0]):
        dh2 = dh2 + parts_ref[i].astype(F32)
    unit2, inv2 = normalize(x1.value())
    small_ref[0:1] = jnp.sum(dh2 * unit2, 0, keepdims=True)
    small_ref[1:2] = jnp.sum(dh2, 0, keepdims=True)
    dx1 = dpooled_ref[...] + norm_back(dh2, unit2, inv2, vec_ref[3:4])
    dx1_ref[...] = dx1
    da = dx1.astype(BF)
    small_ref[2:3] = jnp.sum(da.astype(F32), 0, keepdims=True)
    ctx = ctx.value()
    pick = own_columns(rank * span, width, span)
    wout_ref[...] = tn(da, nn(ctx.astype(BF), pick).astype(BF)).astype(BF)
    dctx = nt(da, wo.value()).astype(BF)
    mask = head_mask(captions, span)
    wv_ref = wv.wait()
    for g in range(n_mp):
        tall = nn(spread_heads(dctx, g, mask), wv_ref[g * span : (g + 1) * span])
        a_ref[g * per_group : (g + 1) * per_group] = tall.astype(BF).reshape(
            per_group, captions, width
        )
    prod = dctx.astype(F32) * ctx
    lse = lse.value()
    scale = 1.0 / math.sqrt(HEAD_DIM)
    tall_shape = (heads * CAP_BLOCK, width)
    of_head = (iota2(tall_shape, 0) // CAP_BLOCK) == (iota2(tall_shape, 1) // HEAD_DIM)
    at_head = (iota2(tall_shape, 0) // CAP_BLOCK) * HEAD_DIM == iota2(tall_shape, 1)
    rows_ref, qk_ref = rows_all.wait(), qk_all.wait()
    same = same_caption(heads, seq_len)
    code = own_code(packed_ref[...], rank, vocab_part)
    tall = (heads * CAP_BLOCK, width)
    blocks = range(captions // CAP_BLOCK)
    cuts = [pl.ds(block * block_rows, block_rows) for block in blocks]
    caps = [pl.ds(block * CAP_BLOCK, CAP_BLOCK) for block in blocks]
    raw = [nt(qk_ref[:, caps[block], :].reshape(tall), rows_ref[cuts[block], :]) for block in blocks]
    pulled = [nt(a_ref[:, caps[block], :].reshape(tall), rows_ref[cuts[block], :]) for block in blocks]
    probs_all, ds_all = [], []
    for block in blocks:
        low = block * CAP_BLOCK
        here = code[:, block * block_rows : (block + 1) * block_rows]
        own = jnp.logical_and(same, here > 0)
        scores = jnp.where(here > 1, raw[block], MASK_FILL)
        spread = jnp.concatenate([lse[low : low + CAP_BLOCK]] * heads, axis=0)
        log_total = jnp.sum(jnp.where(at_head, spread, 0.0), -1, keepdims=True)
        spread = jnp.concatenate([prod[low : low + CAP_BLOCK]] * heads, axis=0)
        row_sum = jnp.sum(jnp.where(of_head, spread, 0.0), -1, keepdims=True)
        probs = jnp.where(own, jnp.exp(scores - log_total), 0.0)
        dscores = (probs * (pulled[block] - row_sum)).astype(BF)
        probs = probs.astype(BF)
        probs_ref[block] = probs
        ds_ref[block] = dscores
        probs_all.append(probs)
        ds_all.append(dscores)
    for block in blocks:
        rows = rows_ref[cuts[block], :]
        t_ref[:, caps[block], :] = (
            nn(probs_all[block], rows).astype(BF).reshape(heads, CAP_BLOCK, width)
        )
        s_ref[:, caps[block], :] = (
            (nn(ds_all[block], rows) * scale).astype(BF).reshape(heads, CAP_BLOCK, width)
        )
    q = q.value()
    wk_ref = wk.wait()
    for g in range(n_mp):
        some = slice(g * per_group, (g + 1) * per_group)
        tall = s_ref[some].reshape(per_group * captions, width)
        piece = nt(tall, wk_ref[g * span : (g + 1) * span])
        dq_ref[:, g * span : (g + 1) * span] = fold_heads(piece, captions, mask).astype(BF)
        wkv_ref[g, :, :span] = tn(tall, spread_heads(q, g, mask)).astype(BF)
        tall = t_ref[some].reshape(per_group * captions, width)
        wkv_ref[g, :, span:] = tn(tall, spread_heads(dctx, g, mask)).astype(BF)
    half = sent_one.shape[0]

    def put(low, piece):
        inside = min(max(half - low, 0), piece.shape[0])
        if inside > 0:
            sent_one[low : low + inside] = piece[:inside]
        if inside < piece.shape[0]:
            sent_two[low + inside - half : low + piece.shape[0] - half] = piece[inside:]

    for g in range(0, n_mp, 2):
        at = slice(g // 2 * width, (g // 2 + 1) * width)
        first, second = wkv_ref[g], wkv_ref[g + 1]
        kept_ref[at] = jnp.where(rank % 2 == 0, first, second)
        put(g // 2 * width, jnp.where(rank % 2 == 0, second, first))
    for k in range(n_mp // 2):
        at = slice(n_mp // 2 * width + k * captions, n_mp // 2 * width + (k + 1) * captions)
        piece = dq_ref[:, 2 * k * span : 2 * (k + 1) * span]
        kept_ref[at] = piece
        put(n_mp // 2 * width + k * captions, piece)


def between_body(meta_ref, kept_ref, got_one, got_two, kept_out, sent_out):
    block = kept_ref.shape[0] - kept_out.shape[0]
    half = got_one.shape[0]

    def total(low, high):
        parts = []
        if low < half:
            parts.append(got_one[low : min(high, half)])
        if high > half:
            parts.append(got_two[max(low, half) - half : high - half])
        got = parts[0] if len(parts) == 1 else jnp.concatenate(parts, axis=0)
        return kept_ref[low:high].astype(F32) + got.astype(F32)

    first, second = total(0, block), total(block, 2 * block)
    both = total(2 * block, kept_ref.shape[0]).astype(BF)
    upper = meta_ref[0] // 2 % 2
    kept_out[:block] = jnp.where(upper == 0, first, second).astype(BF)
    sent_out[:block] = jnp.where(upper == 0, second, first).astype(BF)
    kept_out[block:] = both
    sent_out[block:] = both


def slot_body(owner_rows, n_dp, meta_ref, packed_ref, out_ref):
    rows = packed_ref.shape[1]
    side = 128
    ids, _, _ = unpack(packed_ref[...])
    owner = ids // owner_rows
    order = iota2((1, rows), 1)

    def columns(row, k):
        piece = row[:, k * side : (k + 1) * side].astype(F32)
        return jnp.transpose(jnp.broadcast_to(piece, (side, side))).astype(I32)

    def tall(column):
        return jnp.concatenate([column] * (rows // side), axis=1)

    first_at = jnp.full((1, rows), rows, I32)
    for k in range(rows // side):
        there = k * side + iota2((side, rows), 0)
        hit = jnp.where(tall(columns(ids, k)) == ids, there, rows)
        first_at = jnp.minimum(first_at, jnp.min(hit, 0, keepdims=True))
    is_first = first_at == order
    first_owner = jnp.where(is_first, owner, -1)
    slot = jnp.zeros((1, rows), I32)
    for k in range(rows // side):
        there = k * side + iota2((side, rows), 0)
        ahead = jnp.logical_and(tall(columns(first_owner, k)) == owner, there < first_at)
        slot = slot + jnp.sum(jnp.where(ahead, 1, 0), 0, keepdims=True)
    here = owner - meta_ref[0] * n_dp
    dest = jnp.where(jnp.logical_and(here >= 0, here < n_dp), here, -1)
    most = jnp.max(slot.astype(F32), 1, keepdims=True).astype(I32) + 1
    out_ref[0:1] = slot
    out_ref[1:2] = dest
    out_ref[2:3] = jnp.where(is_first, ids % owner_rows + 1, 0)
    out_ref[3:4] = jnp.broadcast_to(most, (1, rows))
    out_ref[4:8] = jnp.zeros((4, rows), I32)


def slot_sums(turn, slot_cap, seq_len, slots_ref, packed_ref, dx_ref, n_dp):
    slots = n_dp * slot_cap
    rows = dx_ref.shape[0]
    step = min(512, rows)
    captions_per_step = step // seq_len
    total, digits, pooled = None, None, []
    for low in range(0, rows, step):
        cut = slice(low, low + step)
        place = slots_ref[0:1, cut] - turn * slot_cap
        dest, row = slots_ref[1:2, cut], slots_ref[2:3, cut]
        inside = jnp.logical_and(dest >= 0, jnp.logical_and(place >= 0, place < slot_cap))
        key = jnp.where(inside, dest * slot_cap + place, -1)
        hit = jnp.where(iota2((slots, step), 0) == key, 1.0, 0.0).astype(BF)
        piece = nn(hit, dx_ref[cut])
        total = piece if total is None else total + piece
        which = iota2((16, step), 0)
        value = jnp.where(which == 0, row // NOTE_BASE, jnp.where(which == 1, row % NOTE_BASE, 0))
        piece = nt(value.astype(F32).astype(BF), hit)
        digits = piece if digits is None else digits + piece
        _, _, is_end = unpack(packed_ref[:, cut])
        caption = iota2((captions_per_step, step), 1) // seq_len
        mark = jnp.logical_and(caption == iota2((captions_per_step, step), 0), is_end)
        pooled.append(nt(hit, jnp.where(mark, 1.0, 0.0).astype(BF)))
    return total, digits, jnp.concatenate(pooled, axis=1).astype(BF)


def rows_back_body(
    slot_cap, meta_ref, probs_ref, ds_ref, a_ref, vec_ref, slots_ref, packed_ref, qk_all, unit_all, inv_all,
    dx_out, posg_ref, small_ref, seg_ref, digits_ref, pooled_ref, dx_ref, sems,
):
    blocks = probs_ref.shape[0]
    heads = a_ref.shape[0]
    seq_len, width = posg_ref.shape
    block_rows = dx_ref.shape[0] // blocks
    gain = vec_ref[0:1]
    qk_ref, unit_ref, inv_ref = qk_all.ref, unit_all.ref, inv_all.ref
    pending = []
    gain_grad = jnp.zeros((1, width), F32)
    bias_grad = jnp.zeros((1, width), F32)
    pos_grad = jnp.zeros((seq_len, width), F32)
    for block in range(blocks):
        if block % HALF == 0:
            for k in range(block, min(block + HALF, blocks)):
                qk_all.wait(k)
                unit_all.wait(k)
                inv_all.wait(k)
        caps = pl.ds(block * CAP_BLOCK, CAP_BLOCK)
        here = pl.ds(block * block_rows, block_rows)
        a = a_ref[:, caps, :].reshape(heads * CAP_BLOCK, width)
        qk = qk_ref[:, caps, :].reshape(heads * CAP_BLOCK, width)
        unit = unit_ref[here, :].astype(F32)
        drows = tn(probs_ref[block], a) + tn(ds_ref[block], qk)
        gain_grad = gain_grad + jnp.sum(drows * unit, 0, keepdims=True)
        bias_grad = bias_grad + jnp.sum(drows, 0, keepdims=True)
        dx = norm_back(drows, unit, inv_ref[here, 0:1], gain).astype(BF)
        dx_ref[here, :] = dx
        pos_grad = pos_grad + jnp.sum(dx.astype(F32).reshape(CAP_BLOCK, seq_len, width), 0)
    for block in range(blocks):
        here = pl.ds(block * block_rows, block_rows)
        copy = pltpu.make_async_copy(dx_ref.at[here], dx_out.at[here], sems.at[block])
        copy.start()
        pending.append(copy)
    small_ref[0:1] = gain_grad
    small_ref[1:2] = bias_grad
    posg_ref[...] = pos_grad
    seg_ref[...], digits_ref[...], pooled_ref[...] = slot_sums(
        0, slot_cap, seq_len, slots_ref, packed_ref, dx_ref, seg_ref.shape[0] // slot_cap
    )
    for copy in pending:
        copy.wait()


def query_back_body(
    n_mp, meta_ref, kept_ref, got_ref, wout_ref, dx1_ref, vec_ref, pos_pick_ref, own_pick_ref, slots_ref,
    seg_ref, digits_ref, pooled_ref, pos_one_ref, small_one_ref, small_two_ref, small_three_ref, x0p, wq,
    dxp_ref, send_ref, kept_out, sent_out, rest_ref, smalls_ref, all_ref,
):
    captions, width = dx1_ref.shape
    n_dp = send_ref.shape[0]
    slots = seg_ref.shape[0]
    slot_cap = slots // n_dp
    lanes = send_ref.shape[2]
    span = width // n_mp
    rank = meta_ref[0]
    total = kept_ref[...].astype(F32) + got_ref[...].astype(F32)
    all_ref[:, : 2 * span] = total[:width]
    all_ref[:, 2 * span : 3 * span] = wout_ref[...].astype(F32)
    dq = jnp.concatenate(
        [total[width + k * captions : width + (k + 1) * captions] for k in range(n_mp // 2)], axis=1
    ).astype(BF)
    gain = vec_ref[0:1]
    unit, inverse = normalize(x0p.value())
    h1 = (unit * gain + vec_ref[1:2]).astype(BF)
    owned = jnp.sum(own_pick_ref[...].astype(F32), -1, keepdims=True)
    dh1 = nn(dq, wq.value()) * owned
    dxp = (dx1_ref[...] * owned + norm_back(dh1, unit, inverse, gain)).astype(BF)
    dxp_ref[...] = dxp
    seq_len = pos_one_ref.shape[0]
    smalls_ref[...] = jnp.zeros_like(smalls_ref)
    smalls_ref[:seq_len] = pos_one_ref[...] + tn(pos_pick_ref[...], dxp)
    at = seq_len
    smalls_ref[at : at + 1] = small_three_ref[0:1] + jnp.sum(dh1 * unit, 0, keepdims=True)
    smalls_ref[at + 1 : at + 2] = small_three_ref[1:2] + jnp.sum(dh1, 0, keepdims=True)
    smalls_ref[at + 2 : at + 5] = small_two_ref[...]
    smalls_ref[at + 5 : at + 7] = small_one_ref[...]
    smalls = smalls_ref[...]
    high = smalls.astype(BF)
    low = (smalls - high.astype(F32)).astype(BF)
    all_ref[:, 3 * span :] = tn(h1, nn(dq, own_columns(rank * span, width, span)).astype(BF))
    chunk = width // n_dp
    blocks = [
        functools.partial(lambda i: all_ref[pl.ds(i * chunk, chunk), :], i) for i in range(n_dp)
    ]
    split_blocks(blocks, DOWN_BIT, meta_ref[2] // DOWN_BIT % 2, kept_out, sent_out)
    shape = (SMALLS, 2 * SMALLS)
    place = iota2(shape, 1) - iota2(shape, 0)
    rest_ref[...] = tn(high, jnp.where(place == 0, 1.0, 0.0).astype(BF)) + tn(
        low, jnp.where(place == SMALLS, 1.0, 0.0).astype(BF)
    )
    seg = (seg_ref[...] + nn(pooled_ref[...], dxp)).astype(BF)
    most = slots_ref[3:4, :lanes]
    which = iota2((NOTES, lanes), 0)
    most = jnp.where(which == 2, most // NOTE_BASE, most % NOTE_BASE).astype(F32)
    chunk = width // n_dp
    base = (width // lanes) * slot_cap
    for i in range(n_dp):
        for j in range(width // lanes):
            send_ref[i, j * slot_cap : (j + 1) * slot_cap, :] = seg[
                i * slot_cap : (i + 1) * slot_cap, j * lanes : (j + 1) * lanes
            ]
        extra = send_ref.shape[1] - NOTES
        tall = extra - base
        if 4 * tall != chunk:
            send_ref[i, base:extra, :] = jnp.zeros((tall, lanes), BF)
        for k in range(4):
            count = min(tall, chunk - k * tall)
            if count > 0:
                send_ref[i, base : base + count, k * 2 * SMALLS : (k + 1) * 2 * SMALLS] = rest_ref[
                    pl.ds(i * chunk + k * tall, count), :
                ].astype(BF)
        digits = digits_ref[:NOTES, i * slot_cap : (i + 1) * slot_cap]
        note = jnp.concatenate([digits, jnp.zeros((NOTES, lanes - slot_cap), F32)], axis=1)
        send_ref[i, extra:, :] = jnp.where(which < 2, note, most).astype(BF)


def send_body(slot_cap, meta_ref, dx_ref, dxp_ref, slots_ref, packed_ref, send_ref, digits_ref):
    n_dp, _, lanes = send_ref.shape
    width = dx_ref.shape[1]
    seq_len = dx_ref.shape[0] // dxp_ref.shape[0]
    seg, digits_ref[...], pooled = slot_sums(
        meta_ref[0], slot_cap, seq_len, slots_ref, packed_ref, dx_ref, n_dp
    )
    seg = (seg + nn(pooled, dxp_ref[...])).astype(BF)
    for i in range(n_dp):
        for j in range(width // lanes):
            send_ref[i, j * slot_cap : (j + 1) * slot_cap, :] = seg[
                i * slot_cap : (i + 1) * slot_cap, j * lanes : (j + 1) * lanes
            ]


def place_rows(row, got_ref, table_ref, slot_cap, lanes):
    n_dp = got_ref.shape[0]
    shape = (table_ref.shape[0], n_dp * slot_cap)
    hit = jnp.where(iota2(shape, 0) == row, 1.0, 0.0).astype(BF)
    for j in range(table_ref.shape[1] // lanes):
        cut = slice(j * slot_cap, (j + 1) * slot_cap)
        rows = jnp.concatenate([got_ref[i, cut, :] for i in range(n_dp)], axis=0)
        table_ref[:, j * lanes : (j + 1) * lanes] = nn(hit, rows)


def place_body(slot_cap, chunk, meta_ref, got_ref, table_ref, rest_ref, most_ref, row_ref):
    lanes = got_ref.shape[2]
    extra = got_ref.shape[1] - NOTES
    most = jnp.zeros((1, 128), F32)
    for i in range(got_ref.shape[0]):
        note = got_ref[i, extra:, :].astype(F32)
        at = slice(i * slot_cap, (i + 1) * slot_cap)
        row_ref[:, at] = note[0:1, :slot_cap] * float(NOTE_BASE) + note[1:2, :slot_cap] - 1.0
        most = jnp.maximum(most, note[2:3, :128] * float(NOTE_BASE) + note[3:4, :128])
    most_ref[...] = most
    place_rows(row_ref[...].astype(I32), got_ref, table_ref, slot_cap, lanes)
    base = table_ref.shape[1] // lanes * slot_cap
    total = got_ref[0, base:extra, :].astype(F32)
    for i in range(1, got_ref.shape[0]):
        total = total + got_ref[i, base:extra, :].astype(F32)
    for k in range(4):
        count = min(extra - base, chunk - k * (extra - base))
        if count > 0:
            cut = slice(k * 2 * SMALLS, k * 2 * SMALLS + SMALLS)
            low = slice(k * 2 * SMALLS + SMALLS, (k + 1) * 2 * SMALLS)
            at = k * (extra - base)
            rest_ref[at : at + count, :] = total[:count, cut] + total[:count, low]


def place_more_body(meta_ref, row_ref, got_ref, old_ref, table_ref):
    lanes = got_ref.shape[2]
    slot_cap = got_ref.shape[1] // (table_ref.shape[1] // lanes)
    place_rows(row_ref[...], got_ref, table_ref, slot_cap, lanes)
    table_ref[...] += old_ref[...]


def on_device(
    token_ids, lengths, images, table, pos_table, ln1_gain, ln1_bias, w_qkv, w_out, b_out,
    ln2_gain, ln2_bias, w_up, b_up, w_down, b_down, w_head,
):
    n_mp, n_dp = lax.axis_size("mp"), lax.axis_size("dp")
    mp_rank, dp_rank = lax.axis_index("mp"), lax.axis_index("dp")
    captions, seq_len = token_ids.shape
    rows = captions * seq_len
    vocab_part, width = table.shape
    heads = width // HEAD_DIM
    own_width = width // n_mp
    ff = w_up.shape[1]
    owner_rows = vocab_part // n_dp
    slot_cap = -(-7 * rows // (n_dp * n_mp * 64)) * 8
    slots = n_dp * slot_cap
    chunk = width // n_dp
    lanes = own_width + 2 * SMALLS
    n_all = captions * n_dp
    blocks = captions // CAP_BLOCK
    meta = jnp.stack([mp_rank, dp_rank * captions, dp_rank]).astype(I32)

    gather = functools.partial(lax.all_gather, axis_name="mp", axis=0)
    turned = jnp.swapaxes(w_qkv, 1, 2)
    shard = jnp.concatenate([turned, w_out[None]])
    image_f = images.astype(F32)
    image_unit = (
        image_f * lax.rsqrt(jnp.sum(image_f * image_f, -1, keepdims=True) + EPS)
    ).astype(BF)
    all_image = lax.all_gather(image_unit, ("dp", "mp"), axis=0, tiled=True)
    at_row = jnp.arange(8)[:, None]
    vecs = b_up.astype(F32)[None, :]
    for k, vec in enumerate((ln1_gain, ln1_bias, b_out, ln2_gain, ln2_bias, b_down)):
        vecs = jnp.where(at_row == k, vec.astype(F32)[None, :], vecs)

    valid = jnp.arange(seq_len)[None, :] < lengths[:, None]
    end_pick = jnp.arange(seq_len)[None, :] == (lengths - 1)[:, None]
    pos_pick = end_pick.astype(BF)
    local2 = token_ids - mp_rank * vocab_part
    owned2 = jnp.logical_and(local2 >= 0, local2 < vocab_part)
    own_pick = jnp.logical_and(end_pick, owned2).astype(BF)
    local = token_ids.reshape(rows) - mp_rank * vocab_part
    local = after(local, image_unit)
    emb = jnp.take(table, jnp.clip(local, 0, vocab_part - 1), axis=0, mode="clip")
    packed = token_ids + jnp.where(valid, VALID_BIT, 0) + jnp.where(end_pick, END_BIT, 0)
    packed = packed.astype(I32).reshape(1, rows)
    per_head = pltpu.VMEM((heads, captions, width), BF)
    per_head = pltpu.VMEM((heads, captions, width), BF)
    row_buffer = pltpu.VMEM((rows, width), BF)
    dma = pltpu.SemaphoreType.DMA
    ends, unit_rows, unit, inverse = vmem_call(
        functools.partial(rows_body, vocab_part),
        [
            ((captions, width), BF),
            ((rows, width), BF, False),
            ((rows, width), BF, False),
            ((rows, 128), F32, False),
        ],
        meta,
        [pos_table, vecs, packed],
        [fetch(emb, blocks)],
        [row_buffer, row_buffer, pltpu.VMEM((rows, 128), F32), dma((3 * blocks,))],
        flops=WORK,
        mib=28,
    )
    shards = everyone(shard, "mp", ends)
    wq, wk, wv, wo = (fetch_weight(shards, k) for k in range(4))
    pay, qk, x0p, q = vmem_call(
        functools.partial(attend_body, vocab_part),
        [
            ((captions, width + 128), BF),
            ((heads, captions, width), BF, False),
            ((captions, width), F32, True),
            ((captions, width), BF, True),
        ],
        meta,
        [gather(ends), pos_pick, pos_table, vecs, packed],
        [wq, wk, fetch(unit_rows, blocks), wv],
        [per_head, per_head, dma((n_mp,))],
        flops=WORK,
        mib=28,
    )
    ctx, lse, x1, u, part = vmem_call(
        hidden_body,
        [
            ((captions, width), F32, True),
            ((captions, width), F32, True),
            ((captions, width), F32, True),
            ((captions, ff), F32, True),
            ((captions, width), BF),
        ],
        meta,
        [gather(pay), vecs],
        [fetch(x0p), wo, fetch(w_up), fetch(w_down)],
        flops=WORK,
        mib=20,
    )
    pooled, proj, powers, sums = vmem_call(
        logits_body,
        [
            ((captions, width), BF, True),
            ((captions, width), F32, True),
            ((captions, n_all), F32, True),
            ((n_dp, 1, n_all + 128), F32),
        ],
        meta,
        [gather(part), vecs],
        [fetch(x1), fetch(w_head), fetch(all_image)],
        flops=WORK * 5,
    )
    all_sums = lax.all_to_all(sums, "dp", 0, 0, tiled=True)
    slot_table = vmem_call(
        functools.partial(slot_body, owner_rows, n_dp),
        [((8, rows), I32)],
        meta,
        [after(packed, sums)],
        flops=WORK * 7,
        mib=20,
    )[0]
    loss, dpooled, part, du, dproj = vmem_call(
        loss_body,
        [
            ((1, 128), F32),
            ((captions, width), F32),
            ((captions, width), BF),
            ((captions, ff), BF),
            ((captions, width), BF),
        ],
        meta,
        [after(all_sums, slot_table), vecs],
        [
            fetch(powers), fetch(all_image), fetch(proj), fetch(w_head), fetch(u), fetch(w_down),
            fetch(w_up),
        ],
        flops=WORK * 5,
    )
    kind = BF if chunk % 16 == 0 else F32
    *halves, small_one = vmem_call(
        weights_body,
        [
            *[((n_dp // 2, chunk, ff + own_width), BF)] * 2,
            *[((n_dp // 2, chunk, ff), BF)] * 2,
            ((2, width), F32),
        ],
        meta,
        [vecs, dpooled, du, dproj],
        [fetch(u), fetch(x1), fetch(pooled)],
        [pltpu.VMEM((width, ff + own_width), kind), pltpu.VMEM((width, ff), kind)],
        flops=WORK * 4,
        mib=24,
    )
    dp_bits = bits_of("dp")

    def next_half(total, bits, hold=None):
        total = halve(total, "dp", bits, bits[0], hold)
        bits.pop(0)
        return total

    one_step = len(dp_bits) == 1
    down = exchange_half(*halves[:2], "dp", DOWN_BIT, one_step)
    up = exchange_half(*halves[2:], "dp", UP_BIT, one_step)
    down_bits = [bit for bit in dp_bits if bit != DOWN_BIT]
    up_bits = [bit for bit in dp_bits if bit != UP_BIT]
    for bit in bits_of("mp"):
        part = part + lax.ppermute(part, "mp", [(i, i ^ bit) for i in range(n_mp)])
    parts = part[None]
    pair_rows = n_mp // 2 * (width + captions)
    dx1, wout, kept, *sent, a, probs, dscores, small_two = vmem_call(
        functools.partial(attend_back_body, vocab_part),
        [
            ((captions, width), F32),
            ((width, own_width), BF),
            ((pair_rows, 2 * own_width), BF),
            *[((pair_rows // 2, 2 * own_width), BF)] * 2,
            ((heads, captions, width), BF),
            ((blocks, heads * CAP_BLOCK, CAP_BLOCK * seq_len), BF),
            ((blocks, heads * CAP_BLOCK, CAP_BLOCK * seq_len), BF),
            ((3, width), F32),
        ],
        meta,
        [parts, packed, vecs, dpooled],
        [
            fetch(x1), fetch(ctx), wo, wv, fetch(lse), fetch(qk, blocks, 1),
            fetch(unit_rows, blocks), wk, fetch(q),
        ],
        [
            per_head, per_head, pltpu.VMEM((n_mp, width, 2 * own_width), BF),
            pltpu.VMEM((captions, width), BF),
        ],
        flops=WORK * 13,
    )
    got = [lax.ppermute(x, "mp", [(i, i ^ 1) for i in range(n_mp)]) for x in sent]
    last_rows = pair_rows - width
    kept, sent = vmem_call(
        between_body, [((last_rows, 2 * own_width), BF)] * 2, meta, [kept, *got], flops=WORK * 2, mib=12
    )
    got = lax.ppermute(sent, "mp", [(i, i ^ 2) for i in range(n_mp)])
    dx, pos_one, small_three, seg, digits, pooled_slots = vmem_call(
        functools.partial(rows_back_body, slot_cap),
        [
            ((rows, width), BF, False),
            ((seq_len, width), F32),
            ((2, width), F32),
            ((slots, width), F32),
            ((16, slots), F32),
            ((slots, captions), BF),
        ],
        meta,
        [after(probs, sent), dscores, a, vecs, slot_table, packed],
        [fetch(qk, blocks, 1), fetch(unit, blocks), fetch(inverse, blocks)],
        [row_buffer, dma((blocks,))],
        flops=WORK * 12,
        mib=32,
    )
    down, up = next_half(down, down_bits), next_half(up, up_bits, seg)
    rest_rows = -(-chunk // 32) * 8
    send_rows = width // lanes * slot_cap
    dxp, send, kept, sent = vmem_call(
        functools.partial(query_back_body, n_mp),
        [
            ((captions, width), BF),
            ((n_dp, send_rows + rest_rows + NOTES, lanes), BF),
            *[((n_dp // 2, chunk, 4 * own_width), BF)] * 2,
        ],
        meta,
        [
            kept, got, wout, dx1, vecs, pos_pick, own_pick, slot_table, seg, digits, pooled_slots, pos_one,
            small_one, small_two, small_three,
        ],
        [fetch(x0p), wq],
        [
            pltpu.VMEM((width, 2 * SMALLS), F32), pltpu.VMEM((SMALLS, width), F32),
            pltpu.VMEM((width, 4 * own_width), F32),
        ],
        flops=WORK * 4,
        mib=24,
    )
    got = lax.all_to_all(send, "dp", 0, 0, tiled=True)
    wkvo = exchange_half(kept, sent, "dp", DOWN_BIT, one_step)
    bits = [bit for bit in dp_bits if bit != DOWN_BIT]
    while len(bits) > 1:
        wkvo = next_half(wkvo, bits)
    while down_bits:
        down = next_half(down, down_bits)
    while up_bits:
        up = next_half(up, up_bits)
    down, up = lax.optimization_barrier((down[0], up[0]))
    table_grad, rest, most_all = vmem_call(
        functools.partial(place_body, slot_cap, chunk),
        [((owner_rows, width), F32), ((chunk, SMALLS), F32), ((1, 128), F32)],
        meta,
        [got],
        (),
        [pltpu.VMEM((1, slots), F32)],
        flops=WORK * 3,
        mib=20,
    )
    most_all = most_all[0, 0].astype(I32)
    small = rest
    last = gather(jnp.concatenate([down[:, ff:], small, jnp.zeros_like(small)], 1))
    wkvo = lax.optimization_barrier(next_half(wkvo, bits, last)[0])

    def another(carry):
        turn, total = carry
        sent, digits = vmem_call(
            functools.partial(send_body, slot_cap),
            [((n_dp, send_rows, lanes), BF), ((16, slots), F32)],
            turn.reshape(1),
            [dx, dxp, slot_table, packed],
        )
        row = (digits[0] * NOTE_BASE + digits[1] - 1.0).astype(I32)
        row = lax.all_to_all(row.reshape(n_dp, slot_cap), "dp", 0, 0, tiled=True)
        sent = lax.all_to_all(sent, "dp", 0, 0, tiled=True)
        total = vmem_call(
            place_more_body,
            [((owner_rows, width), F32)],
            meta,
            [row.reshape(1, slots), sent, total],
        )[0]
        return turn + 1, total

    _, table_grad = lax.while_loop(
        lambda carry: carry[0] * slot_cap < most_all, another, (jnp.int32(1), table_grad)
    )
    w_head_grad = jnp.swapaxes(last[:, :, :own_width], 0, 1).reshape(chunk, width)
    shared = jnp.sum(last[:, :, own_width : own_width + SMALLS], 0)
    qkv_grad = jnp.stack(
        [wkvo[:, k * own_width : (k + 1) * own_width] for k in (3, 0, 1)]
    )
    return (
        loss[0, 0],
        table_grad,
        shared[:, :seq_len].T,
        shared[:, seq_len],
        shared[:, seq_len + 1],
        qkv_grad,
        wkvo[:, 2 * own_width : 3 * own_width].T,
        small[:, seq_len + 4],
        small[:, seq_len + 2],
        small[:, seq_len + 3],
        up,
        small[:, seq_len + 6],
        down[:, :ff].T,
        small[:, seq_len + 5],
        w_head_grad,
    )


def solution(mesh):
    placed = (
        P("dp", None),
        P("dp"),
        P(("dp", "mp"), None),
        P("mp", None),
        P(),
        P(),
        P(),
        P(None, None, "mp"),
        P("mp", None),
        P(),
        P(),
        P(),
        P(None, "mp"),
        P("mp"),
        P("mp", None),
        P(),
        P(),
    )
    return jax.shard_map(
        on_device,
        mesh=mesh,
        in_specs=placed,
        out_specs=(
            P(),
            P(("mp", "dp"), None),
            P(None, "dp"),
            P("dp"),
            P("dp"),
            P(None, "dp", "mp"),
            P("mp", "dp"),
            P("dp"),
            P("dp"),
            P("dp"),
            P("dp", "mp"),
            P(("mp", "dp")),
            P("mp", "dp"),
            P("dp"),
            P("dp", None),
        ),
        check_vma=False,
    )
```
